128 devices in a mesh: lat: 8 (over y_lo, x), lon: 16 (over y_hi, z, core).
Axes of the slice: x: 4, y: 4 (y_hi: 2, y_lo: 2; y = y_hi * 2 + y_lo), z: 4, core: 2. Of those that a mesh axis runs over, the one named last changes fastest.
Arguments:
- latents: bfloat16 [16384, 256], P(('lat', 'lon')), may hold values from -6 to 6
- in_proj: bfloat16 [256, 128], replicated, may hold values from -0.375 to 0.375
- kernel_one: bfloat16 [3, 3, 128, 128], replicated, may hold values from -0.1875 to 0.1875
- kernel_two: bfloat16 [3, 3, 128, 128], replicated, may hold values from -0.1875 to 0.1875
- kernel_three: bfloat16 [3, 3, 128, 128], replicated, may hold values from -0.1875 to 0.1875
- out_proj: bfloat16 [128, 71], replicated, may hold values from -0.5 to 0.5
- bank: bfloat16 [32, 256, 128], replicated, may hold values from -0.375 to 0.375
- obs_values: float32 [4096, 71, 128], P(('lat', 'lon')), may hold values from -6 to 6
- obs_scale: float32 [71], replicated, may hold values from 0.5 to 2
- owner_col: int32 [4096, 1], P(('lat', 'lon')), may hold values from 0 to 15; in each aligned block of 32 rows (0 to 31, 32 to 63, ...) at most 4 rows name the same one
- patch_id: int32 [4096], P(('lat', 'lon')), may hold values from 0 to 7
- bank_id: int32 [4096], P(('lat', 'lon')), may hold values from 0 to 31
Outputs:
- latent_gradient: float32 [16384, 256], P(('lat', 'lon'))
The draws below stay inside these ranges and needn't reach their ends.
Inputs may be any that keep to these rules, and one draw needn't show every extreme that they name: Block k is held by device k // 32 of lat+lon; its owner tile is in that device's tile row. Among the 32 blocks of one device at most 4 have the same owner_col.
All inputs are finite; a program needn't handle non-finite values.
Results may differ from the reference program's by a relative error of at most 0.011.
Values may be sent and summed in bfloat16 or wider, within the bound.
A program may use at most 64 MiB of HBM per device.

```python
import math
import jax
import jax.numpy as jnp
import numpy as np

CHANNELS = 256
WIDTH = 128
VARS = 71
PATCH = 256
OB = 128
NBANK = 32
CAP = 4
LW = 8
OBS_DEV = 32
LH = 16
LAT_ROWS = 128
LAT_COLS = 128
TOKENS = 16384
GRID_ROWS = 512
GRID_COLS = 512
NPATCH = 8
OBS_BLOCKS = 4096
N_LAT = 8
N_LON = 16


def touch_ends(array, own_key, least, top_value):
    longest = array.shape.index(max(array.shape))
    spots = []
    for shift in (0, 1):
        where = [jax.random.randint(jax.random.fold_in(own_key, axis), (), 0, length) for axis, length in enumerate(array.shape)]
        where[longest] = (where[longest] + shift) % array.shape[longest]
        spots.append(tuple(where))
    return array.at[spots[0]].set(least).at[spots[1]].set(top_value)


def steps_of(stream_key, shape, shards, low, top_value):
    gain = 1.0
    for axis_at, shards_of in shards:
        steps = jax.random.uniform(jax.random.fold_in(jax.random.fold_in(stream_key, 6), axis_at), (shards_of,), jnp.float32, low / len(shards), top_value / len(shards))
        gain = gain * jnp.repeat(jnp.exp(steps), shape[axis_at] // shards_of).reshape((-1,) + (1,) * (len(shape) - 1 - axis_at))
    return gain


def shared_out(own_key, own, number, rows, count, top, most, lean):
    sequence = jax.random.permutation(own_key, count)
    packed, usual = portions_of(count, rows * top, most, lean, True), portions_of(count, rows * top, most, lean, False)
    places = jnp.arange(count)

    def named(tallies, turn):
        used = int((tallies > 0).sum())
        fixed = max(1, used // 4)
        moved = fixed + (places - fixed + turn * (used - fixed)) % max(1, count - fixed)
        return jnp.zeros((count,), jnp.int32).at[sequence[jnp.where(places < fixed, places, moved)]].set(jnp.asarray(tallies, jnp.int32))

    tallies = jnp.where(number % 4 == 0, named(packed, number // 4), named(usual, number - number // 4 - 1))
    mixed = jax.random.permutation(jax.random.fold_in(own, 3), count)
    giver, receiver = mixed[0:count // 2 * 2:2], mixed[1:count // 2 * 2:2]
    room = jnp.minimum(tallies[giver] - 1, most - tallies[receiver]) // 2
    room = jnp.where((giver == sequence[0]) | (receiver == sequence[0]) | (tallies[receiver] == 0), 0, jnp.maximum(room, 0))
    moved = jax.random.randint(jax.random.fold_in(own, 4), (count // 2,), 0, 1 << 20) % (room + 1)
    tallies = tallies.at[giver].add(-moved).at[receiver].add(moved)
    labels = jnp.searchsorted(jnp.cumsum(tallies), jnp.arange(rows * top), side="right").astype(jnp.int32)
    listing = labels.reshape(top, rows).T
    listing = listing[jax.random.permutation(jax.random.fold_in(own, 1), rows)]
    turn = jax.random.randint(jax.random.fold_in(own, 2), (rows, 1), 0, top)
    return jnp.take_along_axis(listing, (jnp.arange(top)[None, :] + turn) % top, axis=1)


def portions_of(number_of, total, bound, skew, full):
    portions = [(1 << 20) // math.isqrt(rank ** skew) + 1 for rank in range(1, number_of + 1)]
    largest = bound if full else min(bound, max(-(-total // number_of), total * portions[0] // sum(portions)))
    least = 1 if total - largest >= number_of - 1 else 0
    holding, surplus = [largest] + [least] * (number_of - 1), total - largest - least * (number_of - 1)
    while surplus > 0:
        movable = [i for i in range(1, number_of) if holding[i] < largest] or [i for i in range(1, number_of) if holding[i] < bound]
        whole, budget = sum([portions[i] for i in movable]), surplus
        for i in movable:
            extra = min(bound - holding[i], max(1, budget * portions[i] // whole), surplus)
            holding[i] = holding[i] + extra
            surplus = surplus - extra
    return np.array(holding)


def noise(stream_key, dims, spread, limit, shards=(), kind=jnp.bfloat16):
    factor_of = steps_of(stream_key, dims, shards, -0.22, 0.18) if shards else 1.0
    drawn = jax.random.normal(stream_key, dims, jnp.float32) * spread * factor_of
    return jnp.minimum(jnp.maximum(drawn, -limit), limit).astype(kind)


def setup_inputs(seed: int = 0) -> dict:
    splits = jax.random.split(jax.random.key(seed), 13)
    latents = noise(splits[0], (TOKENS, CHANNELS), 1.0, 6.0, ((0, 128),))
    in_proj = noise(splits[1], (CHANNELS, WIDTH), CHANNELS ** -0.5, 0.375)
    kernel_one = noise(splits[2], (3, 3, WIDTH, WIDTH), (9 * WIDTH) ** -0.5, 0.1875)
    kernel_two = noise(splits[3], (3, 3, WIDTH, WIDTH), (9 * WIDTH) ** -0.5, 0.1875)
    kernel_three = noise(splits[4], (3, 3, WIDTH, WIDTH), (9 * WIDTH) ** -0.5, 0.1875)
    out_proj = noise(splits[5], (WIDTH, VARS), WIDTH ** -0.5, 0.5)
    bank = noise(splits[6], (NBANK, PATCH, OB), PATCH ** -0.5, 0.375)
    obs_values = noise(splits[7], (OBS_BLOCKS, VARS, OB), 1.0, 6.0, ((0, 128),), jnp.float32)
    obs_scale = jnp.clip(jnp.exp(jax.random.uniform(splits[8], (VARS,), jnp.float32, math.log(0.5), math.log(2.0))), 0.5, 2.0)
    owner_col_keys = jax.random.split(jax.random.fold_in(splits[9], 1), OBS_BLOCKS // OBS_DEV)
    owner_col_turns = jax.random.permutation(jax.random.fold_in(splits[9], 3), OBS_BLOCKS // OBS_DEV)
    owner_col = jax.vmap(lambda own, number: shared_out(jax.random.fold_in(splits[9], 2), own, number, OBS_DEV, N_LON, 1, CAP, 2))(owner_col_keys, owner_col_turns).reshape((OBS_BLOCKS, 1))
    patch_id = touch_ends(jax.random.randint(splits[10], (OBS_BLOCKS,), 0, NPATCH), jax.random.fold_in(splits[10], 1), 0, NPATCH - 1).astype(jnp.int32)
    bank_id = touch_ends(jax.random.randint(splits[11], (OBS_BLOCKS,), 0, NBANK), jax.random.fold_in(splits[11], 1), 0, NBANK - 1).astype(jnp.int32)
    return {"latents": latents, "in_proj": in_proj, "kernel_one": kernel_one, "kernel_two": kernel_two, "kernel_three": kernel_three, "out_proj": out_proj, "bank": bank, "obs_values": obs_values, "obs_scale": obs_scale, "owner_col": owner_col, "patch_id": patch_id, "bank_id": bank_id}


def pad_rim(field_in):
    wide = jnp.concatenate([field_in[:, -1:], field_in, field_in[:, :1]], axis=1)
    zeros_row = jnp.zeros((1,) + wide.shape[1:], wide.dtype)
    return jnp.concatenate([zeros_row, wide, zeros_row], axis=0)


def conv_rim(padded, kernel):
    span_rows = padded.shape[0] - 2
    span_cols = padded.shape[1] - 2
    channel = padded.shape[2]
    summed = jnp.zeros((span_rows * span_cols, kernel.shape[3]), jnp.float32)
    for i in range(3):
        for j in range(3):
            shifted = padded[i:i + span_rows, j:j + span_cols].reshape(span_rows * span_cols, channel)
            summed = summed + jnp.dot(shifted, kernel[i, j], preferred_element_type=jnp.float32)
    return summed.reshape(span_rows, span_cols, kernel.shape[3])


def flipped(kernel):
    return jnp.transpose(kernel[::-1, ::-1], (0, 1, 3, 2))


def upsample(field_in):
    return jnp.repeat(jnp.repeat(field_in, 2, axis=0), 2, axis=1)


def downsum(field_in):
    span_rows, span_cols, channel = field_in.shape
    return field_in.reshape(span_rows // 2, 2, span_cols // 2, 2, channel).sum(axis=(1, 3))


def silu_slope(preact):
    logistic = jax.nn.sigmoid(preact)
    return logistic * (1.0 + preact * (1.0 - logistic))


def reference(latents, in_proj, kernel_one, kernel_two, kernel_three, out_proj, bank, obs_values, obs_scale, owner_col, patch_id, bank_id):
    start_feat = jnp.dot(latents, in_proj, preferred_element_type=jnp.float32).astype(jnp.bfloat16)
    start_feat = start_feat.reshape(LAT_ROWS, LAT_COLS, WIDTH)
    lift_one = upsample(start_feat)
    pre_one = conv_rim(pad_rim(lift_one), kernel_one)
    feat_one = (jax.nn.silu(pre_one) + lift_one.astype(jnp.float32)).astype(jnp.bfloat16)
    lift_two = upsample(feat_one)
    pre_two = conv_rim(pad_rim(lift_two), kernel_two)
    feat_two = (jax.nn.silu(pre_two) + lift_two.astype(jnp.float32)).astype(jnp.bfloat16)
    pre_three = conv_rim(pad_rim(feat_two), kernel_three)
    act_three = jax.nn.silu(pre_three).astype(jnp.bfloat16)
    fields = jnp.dot(act_three.reshape(-1, WIDTH), out_proj, preferred_element_type=jnp.float32).astype(jnp.bfloat16)
    tiles = fields.reshape(N_LAT, 4 * LH, N_LON, 4 * LW, VARS).transpose(0, 2, 4, 1, 3)
    tiles = tiles.reshape(N_LAT, N_LON, VARS, NPATCH, PATCH).transpose(0, 1, 3, 2, 4)
    holder = jnp.arange(OBS_BLOCKS, dtype=jnp.int32) // OBS_DEV
    owner_row = holder // N_LON
    owner_cols = owner_col[:, 0]
    chosen = tiles[owner_row, owner_cols, patch_id]
    bank_rows = bank[bank_id]
    predicted = jnp.einsum('bvp,bpo->bvo', chosen.astype(jnp.float32), bank_rows.astype(jnp.float32))
    weights = (obs_scale * obs_scale)[None, :, None]
    adjoint = (weights * (predicted - obs_values)).astype(jnp.bfloat16)
    block_grad = jnp.einsum('bvo,bpo->bvp', adjoint.astype(jnp.float32), bank_rows.astype(jnp.float32))
    grad_tiles = jnp.zeros((N_LAT, N_LON, NPATCH, VARS, PATCH), jnp.float32)
    grad_tiles = grad_tiles.at[owner_row, owner_cols, patch_id].add(block_grad).astype(jnp.bfloat16)
    grad_tiles = grad_tiles.transpose(0, 1, 3, 2, 4).reshape(N_LAT, N_LON, VARS, 4 * LH, 4 * LW)
    field_grad = grad_tiles.transpose(0, 3, 1, 4, 2).reshape(-1, VARS)
    grad_act = jnp.dot(field_grad, out_proj.T, preferred_element_type=jnp.float32)
    grad_act = grad_act.reshape(GRID_ROWS, GRID_COLS, WIDTH)
    adj_three = (grad_act * silu_slope(pre_three)).astype(jnp.bfloat16)
    back_two = conv_rim(pad_rim(adj_three), flipped(kernel_three))
    adj_two = (back_two * silu_slope(pre_two)).astype(jnp.bfloat16)
    sum_two = back_two + conv_rim(pad_rim(adj_two), flipped(kernel_two))
    back_one = downsum(sum_two)
    adj_one = (back_one * silu_slope(pre_one)).astype(jnp.bfloat16)
    sum_one = back_one + conv_rim(pad_rim(adj_one), flipped(kernel_one))
    back_zero = downsum(sum_one).astype(jnp.bfloat16)
    return jnp.dot(back_zero.reshape(-1, WIDTH), in_proj.T, preferred_element_type=jnp.float32)
```

```python
import functools

import jax
import jax.numpy as jnp
from jax import lax
from jax.experimental import pallas as pl
from jax.experimental.pallas import tpu as pltpu
from jax.sharding import PartitionSpec as P

F32 = jnp.float32
BF16 = jnp.bfloat16
I32 = jnp.int32
MESH = pl.DeviceIdType.MESH
CAP = 4
LW = 8
W = 128
VP = 72
MP = 24
LP = 16
GUARD = 3
HALO = [(-1, -1), (-1, 0), (-1, 1), (0, -1), (0, 1), (1, -1), (1, 0), (1, 1)]


def dot(x, y):
    return jnp.dot(x, y, preferred_element_type=F32)


def dot_nt(x, y):
    return lax.dot_general(x, y, (((1,), (1,)), ((), ())), preferred_element_type=F32)


def shifted(x, by):
    return x if by == 0 else pltpu.roll(x, (-by) % x.shape[0], 0)


def logistic(x):
    return 0.5 * jnp.tanh(0.5 * x) + 0.5


def rounded(x):
    return x.astype(BF16).astype(F32)


TAPS = [(1, -1), (0, 0), (1, 0), (0, 1)]


def window(src, first, count, pitch):
    planes = []
    for p, dr in TAPS:
        line = []
        for q, dc in TAPS:
            at = pl.multiple_of((first + dr) * pitch, 8)
            line.append(shifted(src[2 * q + p, pl.ds(at, count * pitch), :], dc).astype(BF16))
        planes.append(line)
    return planes


def up_weights(k_ref, out_ref):
    rows = {(0, 0): [0], (0, 1): [1, 2], (0, 2): [], (1, 0): [], (1, 1): [0, 1], (1, 2): [2]}
    cols = {(0, 0): [0], (0, 1): [1, 2], (1, 0): [0, 1], (1, 1): [2]}
    for q in range(2):
        for rr in range(3):
            for cc in range(2):
                for p in range(2):
                    block = jnp.zeros((W, W), F32)
                    for i in rows[p, rr]:
                        for j in cols[q, cc]:
                            block = block + k_ref[i, j].astype(F32)
                    at = (rr * 2 + cc) * W
                    out_ref[q, at : at + W, p * W : (p + 1) * W] = block.astype(BF16)


def pair_weights(k_ref, out_ref, flip):
    for m in range(4):
        for j in range(3):
            at = (m * 3 + j) * W
            for p in range(2):
                i = m - p
                if 0 <= i <= 2:
                    block = k_ref[2 - i, 2 - j].astype(F32).T if flip else k_ref[i, j].astype(F32)
                else:
                    block = jnp.zeros((W, W), F32)
                out_ref[at : at + W, p * W : (p + 1) * W] = block.astype(BF16)


def down_weights(k_ref, out_ref):
    for m in range(4):
        for n in range(4):
            block = jnp.zeros((W, W), F32)
            for i in (m - 1, m):
                for j in (n - 1, n):
                    if 0 <= i <= 2 and 0 <= j <= 2:
                        block = block + k_ref[2 - i, 2 - j].astype(F32)
            at = (m * 4 + n) * W
            out_ref[at : at + W, :] = block.T.astype(BF16)


def kernel(
    n_lat,
    n_lon,
    lat_ref,
    inp_ref,
    k1_ref,
    k2_ref,
    k3_ref,
    outp_ref,
    bank_hbm,
    obs_hbm,
    scale_ref,
    owner_ref,
    patch_ref,
    bankid_ref,
    out_ref,
    bank,
    obs,
    row_x,
    sbuf,
    srecv,
    meta_v,
    idx_s,
    meta_s,
    tmp,
    sv,
    rv,
    wu1,
    wu2,
    w3,
    b3,
    wd1,
    wd2,
    opt,
    opad,
    w2,
    f1s,
    d1s,
    f1,
    sl1,
    f2,
    sl2,
    act2,
    sl3,
    actp,
    ft,
    hist,
    ga,
    a3,
    a2,
    ds2,
    b1,
    m1,
    a1,
    zbuf,
    zs,
    zr,
    ctmp,
    ns_s,
    ns_r,
    ew_s,
    ew_r,
    co_s,
    co_r,
    dma_sem,
    st_send,
    st_recv,
    me_send,
    me_recv,
    ob_send,
    ob_recv,
    ha_send,
    ha_recv,
    z_send,
    z_recv,
):
    a, b = lax.axis_index("lat"), lax.axis_index("lon")
    LR = n_lon
    MR = 2 * LR
    npatch = (4 * LR * 4 * LW) // bank.shape[1]
    plen = bank.shape[1]
    nblk = obs.shape[0]
    nvar = obs.shape[1]
    up, down = a > 0, a < n_lat - 1
    upi, downi = jnp.where(up, 1, 0), jnp.where(down, 1, 0)
    first_two, last_two = b < 2, b >= n_lon - 2

    bank_copy = pltpu.make_async_copy(bank_hbm, bank, dma_sem.at[0])
    obs_copy = pltpu.make_async_copy(obs_hbm, obs, dma_sem.at[1])
    obs_copy.start()
    bank_copy.start()
    for row in (0, 1, LR + 2, LR + 3):
        srecv[row] = jnp.zeros((LP, W), BF16)

    barrier = pltpu.get_barrier_semaphore()

    def greet(i, j):
        pl.semaphore_signal(barrier, inc=1, device_id=(i, j), device_id_type=MESH)

    def greet_row(t, c):
        greet(a, lax.rem(b + t, n_lon))
        return c

    lax.fori_loop(1, n_lon, greet_row, 0)

    @pl.when(up)
    def _():
        greet(a - 1, n_lon - 2)
        greet(a - 1, n_lon - 1)
        for d in range(3):
            greet(a - 1, lax.rem(b + n_lon - 1 + d, n_lon))

    @pl.when(down)
    def _():
        greet(a + 1, 0)
        greet(a + 1, 1)
        for d in range(3):
            greet(a + 1, lax.rem(b + n_lon - 1 + d, n_lon))

    feat = rounded(dot(lat_ref[...], inp_ref[...]))
    n_col = n_lon * LW
    row_x[0:8] = feat[n_col - 8 :]
    row_x[8 : 8 + n_col] = feat
    row_x[8 + n_col : 16 + n_col] = feat[0:8]
    for t in range(n_lon):
        sbuf[t] = row_x[8 * t + 4 : 8 * t + 20].astype(BF16)

    lane = lax.broadcasted_iota(I32, (nblk, W), 1)
    sub = lax.broadcasted_iota(I32, (nblk, W), 0)
    eye = lane == sub
    own_c = jnp.broadcast_to(owner_ref[...], (nblk, W))
    own_r = jnp.sum(jnp.where(eye, own_c, 0), axis=0, keepdims=True)
    earlier = jnp.where((own_c == own_r) & (lane < sub), 1, 0)
    rank = jnp.sum(earlier, axis=1, keepdims=True)
    slot = own_c * CAP + rank
    pick = lane == slot

    def column(row_ref):
        row = jnp.broadcast_to(row_ref[...], (nblk, nblk))
        return jnp.sum(jnp.where(eye[:, :nblk], row, 0), axis=1, keepdims=True)

    def per_slot(value):
        return jnp.sum(jnp.where(pick, value, 0), axis=0, keepdims=True)

    rows8 = lax.broadcasted_iota(I32, (8, W), 0)
    meta = jnp.where(rows8 == 0, per_slot(sub), 0)
    meta = jnp.where(rows8 == 1, per_slot(jnp.broadcast_to(column(patch_ref), (nblk, W))), meta)
    meta = jnp.where(rows8 == 2, per_slot(jnp.broadcast_to(column(bankid_ref), (nblk, W))), meta)
    meta = jnp.where(rows8 == 3, per_slot(jnp.ones_like(sub)), meta)
    meta_v[b] = meta
    idx_copy = pltpu.make_async_copy(meta_v.at[b], idx_s, dma_sem.at[2])
    idx_copy.start()

    expected = (
        n_lon - 1
        + jnp.where(first_two & up, n_lon, 0)
        + jnp.where(last_two & down, n_lon, 0)
        + 3 * upi
        + 3 * downi
    )
    pl.semaphore_wait(barrier, expected)

    def row_copy(i, t, at, sem):
        return pltpu.make_async_remote_copy(
            src_ref=sbuf.at[t],
            dst_ref=srecv.at[at],
            send_sem=st_send.at[sem],
            recv_sem=st_recv.at[at],
            device_id=(i, t),
            device_id_type=MESH,
        )

    def send_row(s, c):
        t = lax.rem(b + s, n_lon)
        row_copy(a, t, b + 2, t).start()
        return c

    @pl.when(first_two & up)
    def _():
        def go(t, c):
            row_copy(a - 1, t, LR + 2 + b, n_lon + t).start()
            return c

        lax.fori_loop(0, n_lon, go, 0)

    @pl.when(last_two & down)
    def _():
        def go(t, c):
            row_copy(a + 1, t, b - (n_lon - 2), n_lon + t).start()
            return c

        lax.fori_loop(0, n_lon, go, 0)

    lax.fori_loop(1, n_lon, send_row, 0)
    srecv[b + 2] = sbuf[b]

    def meta_copy(t, slot_at):
        return pltpu.make_async_remote_copy(
            src_ref=meta_v.at[b],
            dst_ref=meta_v.at[slot_at],
            send_sem=me_send.at[t],
            recv_sem=me_recv.at[slot_at],
            device_id=(a, t),
            device_id_type=MESH,
        )

    def send_meta(s, c):
        meta_copy(lax.rem(b + s, n_lon), b).start()
        return c

    lax.fori_loop(1, n_lon, send_meta, 0)

    def obs_copy_to(t, slot_at):
        return pltpu.make_async_remote_copy(
            src_ref=sv.at[t],
            dst_ref=rv.at[slot_at],
            send_sem=ob_send.at[t],
            recv_sem=ob_recv.at[slot_at],
            device_id=(a, t),
            device_id_type=MESH,
        )

    tmp[...] = jnp.zeros_like(tmp)
    obs_copy.wait()
    idx_copy.wait()

    def gathered(t):
        for k in range(CAP):
            tmp[pl.ds(k * VP, nvar), :] = obs[idx_s[0, t * CAP + k]]
        return tmp[...].astype(BF16)

    def send_obs(s, c):
        t = lax.rem(b + s, n_lon)
        sv[t] = gathered(t)
        obs_copy_to(t, b).start()
        return c

    lax.fori_loop(1, n_lon, send_obs, 0)
    rv[b] = gathered(b)

    up_weights(k1_ref, wu1)
    up_weights(k2_ref, wu2)
    pair_weights(k3_ref, w3, False)
    pair_weights(k3_ref, b3, True)
    down_weights(k2_ref, wd2)
    down_weights(k1_ref, wd1)
    opad[...] = jnp.zeros_like(opad)
    opad[:, 0:nvar] = outp_ref[...].astype(F32)
    opt[...] = opad[...].T[0:VP].astype(BF16)
    vlane = lax.broadcasted_iota(I32, (VP, nvar), 1)
    vsub = lax.broadcasted_iota(I32, (VP, nvar), 0)
    scale = jnp.broadcast_to(scale_ref[...], (VP, nvar))
    scale = jnp.sum(jnp.where(vlane == vsub, scale, 0.0), axis=1, keepdims=True)
    w2[...] = jnp.broadcast_to(scale * scale, (VP, W))
    for ref in (f1, sl1, m1, b1):
        ref[...] = jnp.zeros_like(ref)
    for ref in (a3, a2):
        ref[...] = jnp.zeros_like(ref)

    def wait_row(s, c):
        at = lax.rem(b + s, n_lon) + 2
        row_copy(a, b, at, 0).wait_recv()
        return c

    lax.fori_loop(1, n_lon, wait_row, 0)

    @pl.when(up)
    def _():
        row_copy(a, b, 0, 0).wait_recv()
        row_copy(a, b, 1, 0).wait_recv()

    @pl.when(down)
    def _():
        row_copy(a, b, LR + 2, 0).wait_recv()
        row_copy(a, b, LR + 3, 0).wait_recv()

    def inside(first, count, pitch, size):
        row = lax.broadcasted_iota(I32, (count, pitch, W), 0) + first
        low = jnp.where(up, -8, 0)
        high = jnp.where(down, size + 8, size)
        return jnp.where((row >= low) & (row < high), 1.0, 0.0).reshape(count * pitch, W)

    def lifted(line, weights):
        left = [shifted(x, -1).astype(BF16) for x in line]
        here = [x.astype(BF16) for x in line]
        right = [shifted(x, 1).astype(BF16) for x in line]
        phases = []
        for q, (u, v) in enumerate(((left, here), (here, right))):
            x = jnp.concatenate([u[0], v[0], u[1], v[1], u[2], v[2]], axis=1)
            y = dot(x, weights[q])
            phases += [y[:, :W], y[:, W:]]
        return phases

    n1 = LR + 2
    line = [srecv[pl.ds(i, n1)].astype(F32).reshape(n1 * LP, W) for i in range(3)]
    mask = inside(-1, n1, LP, LR)
    for ph, pre in enumerate(lifted(line, wu1)):
        s = logistic(pre)
        f1s[ph] = mask * rounded(pre * s + line[1])
        d1s[ph] = mask * (s * (1.0 + pre * (1.0 - s)))

    def spread(i, c):
        for q in range(2):
            for p in range(2):
                to = pl.ds((2 * i + p + 1) * MP + q, 10, stride=2)
                frm = pl.ds(i * LP + 3, 10)
                f1[to, :] = f1s[2 * q + p, frm, :]
                sl1[to, :] = d1s[2 * q + p, frm, :]
        return c

    lax.fori_loop(0, n1, spread, 0)

    def level_two(i, c):
        first = i * 6 + GUARD - 2
        line = [f1[pl.ds(pl.multiple_of((first + d) * MP, 8), 6 * MP), :] for d in (-1, 0, 1)]
        mask = inside(first - GUARD, 6, MP, MR)
        at = pl.ds(pl.multiple_of(first * MP, 8), 6 * MP)
        for ph, pre in enumerate(lifted(line, wu2)):
            s = logistic(pre)
            f2[ph, at, :] = mask * (pre * s + line[1])
            sl2[ph, at, :] = mask * (s * (1.0 + pre * (1.0 - s)))
        return c

    lax.fori_loop(0, (MR + 4) // 6, level_two, 0)

    def paired(planes, weights, q):
        x = jnp.concatenate([planes[m][q + j] for m in range(4) for j in range(3)], axis=1)
        return dot(x, weights[...])

    def head(i, c):
        first = i * 8 + GUARD
        planes = window(f2, first, 8, MP)
        at = pl.ds(pl.multiple_of(first * MP, 8), 8 * MP)
        for q in range(2):
            y = paired(planes, w3, q)
            for p in range(2):
                pre = y[:, p * W : (p + 1) * W]
                s = logistic(pre)
                act2[2 * q + p, at, :] = pre * s
                sl3[2 * q + p, at, :] = s * (1.0 + pre * (1.0 - s))
        return c

    lax.fori_loop(0, MR // 8, head, 0)

    def points(r, c):
        for q in range(2):
            for p in range(2):
                to = pl.ds((2 * r + p) * (4 * LW) + q, 2 * LW, stride=2)
                actp[to, :] = act2[2 * q + p, pl.ds((r + GUARD) * MP + 2, 2 * LW), :]
        return c

    lax.fori_loop(0, MR, points, 0)
    for n in range(npatch):
        ft[n] = dot_nt(opt[...], actp[n * plen : (n + 1) * plen].astype(BF16)).astype(BF16)

    def wait_meta(s, c):
        meta_copy(b, lax.rem(b + s, n_lon)).wait_recv()
        return c

    lax.fori_loop(1, n_lon, wait_meta, 0)
    meta_down = pltpu.make_async_copy(meta_v, meta_s, dma_sem.at[3])
    meta_down.start()
    bank_copy.wait()
    meta_down.wait()
    none = n_lon * CAP
    hist[none] = jnp.zeros((VP, plen), F32)

    def blocks(s, last):
        source = lax.rem(b + n_lon - s, n_lon)

        @pl.when(s > 0)
        def _():
            obs_copy_to(b, source).wait_recv()

        values = rv[source].astype(F32)
        for k in range(CAP):
            patch = meta_s[source, 1, b * CAP + k]
            rows = bank[meta_s[source, 2, b * CAP + k]]
            live = meta_s[source, 3, b * CAP + k].astype(F32)
            predicted = dot(ft[patch], rows)
            adjoint = (w2[...] * live) * (predicted - values[k * VP : (k + 1) * VP])
            grad = dot_nt(adjoint.astype(BF16), rows)
            before = last[0]
            for n in range(1, npatch):
                before = jnp.where(patch == n, last[n], before)
            hist[s * CAP + k] = grad + hist[before]
            last = tuple(jnp.where(patch == n, s * CAP + k, last[n]) for n in range(npatch))
        return last

    last = lax.fori_loop(0, n_lon, blocks, (jnp.int32(none),) * npatch)

    for n in range(npatch):
        grad = hist[last[n]].astype(BF16)
        ga[n * plen : (n + 1) * plen] = lax.dot_general(
            grad, opt[...], (((0,), (0,)), ((), ())), preferred_element_type=F32
        )

    def adjoint_three(r, c):
        at = pl.ds((r + GUARD) * MP + 2, 2 * LW)
        for q in range(2):
            for p in range(2):
                grad = ga[pl.ds((2 * r + p) * (4 * LW) + q, 2 * LW, stride=2), :]
                a3[2 * q + p, at, :] = grad * sl3[2 * q + p, at, :]
        return c

    lax.fori_loop(0, MR, adjoint_three, 0)

    edge_rows = (0, MR - 2)
    edge_cols = (0, 2 * LW - 2)
    for side in range(2):
        for ph in range(4):
            for i in range(2):
                at = (edge_rows[side] + i + GUARD) * MP + 2
                to = (ph * 2 + i) * 2 * LW
                ns_s[side, to : to + 2 * LW] = a3[ph, at : at + 2 * LW, :].astype(BF16)
                at = GUARD * MP + 2 + edge_cols[side] + i
                to = (ph * 2 + i) * MR
                ew_s[side, to : to + MR] = a3[ph, pl.ds(at, MR, stride=MP), :].astype(BF16)
    for v in range(2):
        for h in range(2):
            for ph in range(4):
                for i in range(2):
                    at = (edge_rows[v] + i + GUARD) * MP + 2 + edge_cols[h]
                    ctmp[v * 2 + h, ph * 4 + i * 2 : ph * 4 + i * 2 + 2] = a3[ph, at : at + 2, :]
            co_s[v * 2 + h] = ctmp[v * 2 + h].astype(BF16)

    def halo_copy(k):
        dy, dx = HALO[k]
        v, h = (dy + 1) // 2, (dx + 1) // 2
        if dy == 0:
            src, dst = ew_s.at[h], ew_r.at[1 - h]
        elif dx == 0:
            src, dst = ns_s.at[v], ns_r.at[1 - v]
        else:
            src, dst = co_s.at[v * 2 + h], co_r.at[(1 - v) * 2 + 1 - h]
        return pltpu.make_async_remote_copy(
            src_ref=src,
            dst_ref=dst,
            send_sem=ha_send.at[k],
            recv_sem=ha_recv.at[7 - k],
            device_id=(a + dy, lax.rem(b + n_lon + dx, n_lon)),
            device_id_type=MESH,
        )

    def halo_arrived(k):
        dy, dx = HALO[k]
        v, h = (dy + 1) // 2, (dx + 1) // 2
        if dy == 0:
            ref = ew_r.at[h]
        elif dx == 0:
            ref = ns_r.at[v]
        else:
            ref = co_r.at[v * 2 + h]
        pltpu.make_async_remote_copy(
            src_ref=ref,
            dst_ref=ref,
            send_sem=ha_send.at[k],
            recv_sem=ha_recv.at[k],
            device_id=(a, b),
            device_id_type=MESH,
        ).wait_recv()

    there = {-1: up, 1: down}
    for dy in (-1, 1):

        @pl.when(there[dy])
        def _():
            for k, (ky, _kx) in enumerate(HALO):
                if ky == dy:
                    halo_copy(k).start()

    for k, (ky, _kx) in enumerate(HALO):
        if ky == 0:
            halo_copy(k).start()

    halo_rows = (-2, MR)
    halo_cols = (0, 2 * LW + 2)
    for dy in (-1, 1):

        @pl.when(there[dy])
        def _():
            v = (dy + 1) // 2
            for k, (ky, _kx) in enumerate(HALO):
                if ky == dy:
                    halo_arrived(k)
            for ph in range(4):
                for i in range(2):
                    at = (halo_rows[v] + i + GUARD) * MP + 2
                    frm = (ph * 2 + i) * 2 * LW
                    a3[ph, at : at + 2 * LW, :] = ns_r[v, frm : frm + 2 * LW].astype(F32)
            for h in range(2):
                ctmp[v * 2 + h] = co_r[v * 2 + h].astype(F32)
                for ph in range(4):
                    for i in range(2):
                        at = (halo_rows[v] + i + GUARD) * MP + halo_cols[h]
                        a3[ph, at : at + 2, :] = ctmp[
                            v * 2 + h, ph * 4 + i * 2 : ph * 4 + i * 2 + 2
                        ]

    for k, (ky, kx) in enumerate(HALO):
        if ky == 0:
            h = (kx + 1) // 2
            halo_arrived(k)
            for ph in range(4):
                for i in range(2):
                    frm = (ph * 2 + i) * MR
                    at = GUARD * MP + halo_cols[h] + i
                    a3[ph, pl.ds(at, MR, stride=MP), :] = ew_r[h, frm : frm + MR].astype(F32)

    def back_three(i, c):
        first = i * 6 + GUARD - 2
        planes = window(a3, first, 6, MP)
        at = pl.ds(pl.multiple_of(first * MP, 8), 6 * MP)
        total = jnp.zeros((6 * MP, W), F32)
        for q in range(2):
            y = paired(planes, b3, q)
            for p in range(2):
                back = y[:, p * W : (p + 1) * W]
                a2[2 * q + p, at, :] = back * sl2[2 * q + p, at, :]
                total = total + back
        ds2[at, :] = total
        return c

    lax.fori_loop(0, (MR + 4) // 6, back_three, 0)

    def gathered_down(planes, weights):
        x = jnp.concatenate([planes[m][n] for m in range(4) for n in range(4)], axis=1)
        return dot(x, weights[...])

    def back_two(i, c):
        first = i * 6 + GUARD - 2
        at = pl.ds(pl.multiple_of(first * MP, 8), 6 * MP)
        back = ds2[at, :] + gathered_down(window(a2, first, 6, MP), wd2)
        b1[at, :] = back
        m1[at, :] = back * sl1[at, :]
        return c

    lax.fori_loop(0, (MR + 4) // 6, back_two, 0)

    def gather(i, c):
        total = jnp.zeros((LP, W), F32)
        for q in range(2):
            for p in range(2):
                frm = pl.ds((2 * i + p + 1) * MP + q, LP, stride=2)
                a1[2 * q + p, pl.ds(pl.multiple_of(i * LP, 8), LP), :] = m1[frm, :]
                total = total + b1[frm, :]
        zbuf[pl.ds(pl.multiple_of(i * LP, 8), LP), :] = total
        return c

    lax.fori_loop(0, n1, gather, 0)
    back = zbuf[LP : LP + LR * LP] + gathered_down(window(a1, 1, LR, LP), wd1)
    zbuf[LP : LP + LR * LP] = rounded(back)
    for r in range(LR):
        zs[r] = zbuf[(r + 1) * LP + 1 : (r + 1) * LP + 1 + LW]

    def z_copy(t, slot_at):
        return pltpu.make_async_remote_copy(
            src_ref=zs.at[t],
            dst_ref=zr.at[slot_at],
            send_sem=z_send.at[t],
            recv_sem=z_recv.at[slot_at],
            device_id=(a, t),
            device_id_type=MESH,
        )

    def send_z(s, c):
        z_copy(lax.rem(b + s, n_lon), b).start()
        return c

    lax.fori_loop(1, n_lon, send_z, 0)
    zr[b] = zs[b]

    def sent(s, c):
        t = lax.rem(b + s, n_lon)
        row_copy(a, t, b + 2, t).wait_send()
        meta_copy(t, b).wait_send()
        obs_copy_to(t, b).wait_send()
        return c

    lax.fori_loop(1, n_lon, sent, 0)

    @pl.when((first_two & up) | (last_two & down))
    def _():
        def go(t, c):
            row_copy(a, t, b + 2, n_lon + t).wait_send()
            return c

        lax.fori_loop(0, n_lon, go, 0)

    for dy in (-1, 1):

        @pl.when(there[dy])
        def _():
            for k, (ky, _kx) in enumerate(HALO):
                if ky == dy:
                    halo_copy(k).wait_send()

    for k, (ky, _kx) in enumerate(HALO):
        if ky == 0:
            halo_copy(k).wait_send()

    def finish(s, c):
        t = lax.rem(b + s, n_lon)
        z_copy(t, b).wait_send()
        z_copy(b, t).wait_recv()
        return c

    lax.fori_loop(1, n_lon, finish, 0)
    out_ref[...] = dot_nt(zr[...].reshape(n_col, W).astype(BF16), inp_ref[...])


def per_device(
    n_lat,
    n_lon,
    latents,
    in_proj,
    kernel_one,
    kernel_two,
    kernel_three,
    out_proj,
    bank,
    obs_values,
    obs_scale,
    owner_col,
    patch_id,
    bank_id,
):
    LR = n_lon
    MR = 2 * LR
    npts = 4 * LR * 4 * LW
    plen = bank.shape[1]
    nmid = (MR + 2 * GUARD) * MP
    n1 = LR + 2
    slots = n_lon * CAP
    vmem = pltpu.VMEM
    dma = pltpu.SemaphoreType.DMA
    scratch = [
        vmem(bank.shape, BF16),
        vmem(obs_values.shape, F32),
        vmem((n_lon * LW + 16, W), F32),
        vmem((n_lon, LP, W), BF16),
        vmem((LR + 4, LP, W), BF16),
        vmem((n_lon, 8, W), I32),
        pltpu.SMEM((8, W), I32),
        pltpu.SMEM((n_lon, 8, W), I32),
        vmem((CAP * VP, W), F32),
        vmem((n_lon, CAP * VP, W), BF16),
        vmem((n_lon, CAP * VP, W), BF16),
        vmem((2, 6 * W, 2 * W), BF16),
        vmem((2, 6 * W, 2 * W), BF16),
        vmem((12 * W, 2 * W), BF16),
        vmem((12 * W, 2 * W), BF16),
        vmem((16 * W, W), BF16),
        vmem((16 * W, W), BF16),
        vmem((VP, W), BF16),
        vmem((W, W), F32),
        vmem((VP, W), F32),
        vmem((4, n1 * LP, W), F32),
        vmem((4, n1 * LP, W), F32),
        vmem((nmid, W), F32),
        vmem((nmid, W), F32),
        vmem((4, nmid, W), F32),
        vmem((4, nmid, W), F32),
        vmem((4, nmid, W), F32),
        vmem((4, nmid, W), F32),
        vmem((npts, W), F32),
        vmem((npts // plen, VP, plen), BF16),
        vmem((slots + 1, VP, plen), F32),
        vmem((npts, W), F32),
        vmem((4, nmid, W), F32),
        vmem((4, nmid, W), F32),
        vmem((nmid, W), F32),
        vmem((nmid, W), F32),
        vmem((nmid, W), F32),
        vmem((4, n1 * LP, W), F32),
        vmem((n1 * LP, W), F32),
        vmem((n_lon, LW, W), F32),
        vmem((n_lon, LW, W), F32),
        vmem((4, 16, W), F32),
        vmem((2, 4 * 2 * 2 * LW, W), BF16),
        vmem((2, 4 * 2 * 2 * LW, W), BF16),
        vmem((2, 4 * 2 * MR, W), BF16),
        vmem((2, 4 * 2 * MR, W), BF16),
        vmem((4, 16, W), BF16),
        vmem((4, 16, W), BF16),
        dma((4,)),
        dma((2 * n_lon,)),
        dma((LR + 4,)),
        dma((n_lon,)),
        dma((n_lon,)),
        dma((n_lon,)),
        dma((n_lon,)),
        dma((8,)),
        dma((8,)),
        dma((n_lon,)),
        dma((n_lon,)),
    ]
    here = pl.BlockSpec(memory_space=pltpu.VMEM)
    far = pl.BlockSpec(memory_space=pl.ANY)
    return pl.pallas_call(
        functools.partial(kernel, n_lat, n_lon),
        out_shape=jax.ShapeDtypeStruct((latents.shape[0], latents.shape[1]), F32),
        in_specs=[here] * 6 + [far] * 2 + [here] * 4,
        out_specs=here,
        scratch_shapes=scratch,
        compiler_params=pltpu.CompilerParams(
            collective_id=0, has_side_effects=True, vmem_limit_bytes=56 * 1024 * 1024
        ),
        cost_estimate=pl.CostEstimate(
            flops=5_000_000_000, bytes_accessed=4_000_000, transcendentals=1_000_000
        ),
    )(
        latents,
        in_proj,
        kernel_one,
        kernel_two,
        kernel_three,
        out_proj,
        bank,
        obs_values,
        obs_scale.reshape(1, -1),
        owner_col,
        patch_id.reshape(1, -1),
        bank_id.reshape(1, -1),
    )


def solution(mesh):
    n_lat, n_lon = mesh.shape["lat"], mesh.shape["lon"]
    placed = (
        P(("lat", "lon"), None),
        P(),
        P(),
        P(),
        P(),
        P(),
        P(),
        P(("lat", "lon"), None, None),
        P(),
        P(("lat", "lon"), None),
        P(("lat", "lon")),
        P(("lat", "lon")),
    )
    return jax.shard_map(
        functools.partial(per_device, n_lat, n_lon),
        mesh=mesh,
        in_specs=placed,
        out_specs=P(("lat", "lon"), None),
        check_vma=False,
    )
```

```python
import functools

import jax
import jax.numpy as jnp
from jax import lax
from jax.experimental import pallas as pl
from jax.experimental.pallas import tpu as pltpu
from jax.sharding import PartitionSpec as P

F32 = jnp.float32
BF16 = jnp.bfloat16
I32 = jnp.int32
MESH = pl.DeviceIdType.MESH
CAP = 4
LW = 8
W = 128
VP = 72
MP = 24
LP = 16
C_TWO, C_HEAD, C_B3, C_B2 = 6, 8, 6, 6
PARTS = 4
GUARD = 3
HALO = [(-1, -1), (-1, 0), (-1, 1), (0, -1), (0, 1), (1, -1), (1, 0), (1, 1)]


def dot(x, y):
    return jnp.dot(x, y, preferred_element_type=F32)


def dot_nt(x, y):
    return lax.dot_general(x, y, (((1,), (1,)), ((), ())), preferred_element_type=F32)


def shifted(x, by):
    return x if by == 0 else pltpu.roll(x, (-by) % x.shape[0], 0)


def logistic(x):
    return 0.5 * jnp.tanh(0.5 * x) + 0.5


def rounded(x):
    return x.astype(BF16).astype(F32)


TAPS = [(1, -1), (0, 0), (1, 0), (0, 1)]


def window(src, first, count, pitch):
    planes = []
    for p, dr in TAPS:
        line = []
        for q, dc in TAPS:
            at = pl.multiple_of((first + dr) * pitch, 8)
            line.append(shifted(src[2 * q + p, pl.ds(at, count * pitch), :], dc).astype(BF16))
        planes.append(line)
    return planes


def up_weights(k_ref, out_ref):
    rows = {(0, 0): [0], (0, 1): [1, 2], (0, 2): [], (1, 0): [], (1, 1): [0, 1], (1, 2): [2]}
    cols = {(0, 0): [0], (0, 1): [1, 2], (1, 0): [0, 1], (1, 1): [2]}
    for q in range(2):
        for rr in range(3):
            for cc in range(2):
                for p in range(2):
                    block = jnp.zeros((W, W), F32)
                    for i in rows[p, rr]:
                        for j in cols[q, cc]:
                            block = block + k_ref[i, j].astype(F32)
                    at = (rr * 2 + cc) * W
                    out_ref[q, at : at + W, p * W : (p + 1) * W] = block.astype(BF16)


def pair_weights(k_ref, out_ref, flip):
    for m in range(4):
        for j in range(3):
            at = (m * 3 + j) * W
            for p in range(2):
                i = m - p
                if 0 <= i <= 2:
                    block = k_ref[2 - i, 2 - j].astype(F32).T if flip else k_ref[i, j].astype(F32)
                else:
                    block = jnp.zeros((W, W), F32)
                out_ref[at : at + W, p * W : (p + 1) * W] = block.astype(BF16)


def down_weights(k_ref, out_ref):
    for m in range(4):
        for n in range(4):
            block = jnp.zeros((W, W), F32)
            for i in (m - 1, m):
                for j in (n - 1, n):
                    if 0 <= i <= 2 and 0 <= j <= 2:
                        block = block + k_ref[2 - i, 2 - j].astype(F32)
            at = (m * 4 + n) * W
            out_ref[at : at + W, :] = block.T.astype(BF16)


def kernel(
    n_lat,
    n_lon,
    lat_hbm,
    inp_hbm,
    k1_hbm,
    k2_hbm,
    k3_hbm,
    outp_hbm,
    bank_hbm,
    obs_hbm,
    scale_hbm,
    owner_hbm,
    patch_hbm,
    bankid_hbm,
    out_ref,
    lat_ref,
    inp_ref,
    k1_ref,
    k2_ref,
    k3_ref,
    outp_ref,
    scale_ref,
    owner_ref,
    patch_ref,
    bankid_ref,
    bank,
    obs,
    row_x,
    sbuf,
    srecv,
    meta_v,
    idx_s,
    meta_s,
    tmp,
    sv,
    rv,
    wu1,
    wu2,
    w3,
    b3,
    wd1,
    wd2,
    opt,
    opad,
    w2,
    f1s,
    d1s,
    f1,
    sl1,
    f2,
    sl2,
    act2,
    sl3,
    actp,
    ft,
    pred,
    hist,
    ga,
    a3,
    a2,
    ds2,
    b1,
    m1,
    a1,
    zbuf,
    zs,
    zr,
    ctmp,
    ns_s,
    ns_r,
    ew_s,
    ew_r,
    co_s,
    co_r,
    dma_sem,
    st_send,
    st_recv,
    me_send,
    me_recv,
    ob_send,
    ob_recv,
    ha_send,
    ha_recv,
    z_send,
    z_recv,
):
    a, b = lax.axis_index("lat"), lax.axis_index("lon")
    LR = n_lon
    MR = 2 * LR
    npatch = (4 * LR * 4 * LW) // bank.shape[1]
    plen = bank.shape[1]
    nblk = patch_ref.shape[1]
    nvar = outp_ref.shape[0]
    up, down = a > 0, a < n_lat - 1
    upi, downi = jnp.where(up, 1, 0), jnp.where(down, 1, 0)
    first_two, last_two = b < 2, b >= n_lon - 2

    for row in (0, 1, LR + 2, LR + 3):
        srecv[row] = jnp.zeros((LP, W), BF16)

    barrier = pltpu.get_barrier_semaphore()

    def greet(i, j):
        pl.semaphore_signal(barrier, inc=1, device_id=(i, j), device_id_type=MESH)

    def greet_row(t, c):
        greet(a, lax.rem(b + t, n_lon))
        return c

    lax.fori_loop(1, n_lon, greet_row, 0)

    @pl.when(up)
    def _():
        greet(a - 1, n_lon - 2)
        greet(a - 1, n_lon - 1)
        for d in range(3):
            greet(a - 1, lax.rem(b + n_lon - 1 + d, n_lon))

    @pl.when(down)
    def _():
        greet(a + 1, 0)
        greet(a + 1, 1)
        for d in range(3):
            greet(a + 1, lax.rem(b + n_lon - 1 + d, n_lon))

    def local(src, dst, sem):
        copy = pltpu.make_async_copy(src, dst, dma_sem.at[sem])
        copy.start()
        return copy

    row_parts = [local(lat_hbm, lat_ref, 2), local(inp_hbm, inp_ref, 3)]
    id_parts = [
        local(owner_hbm, owner_ref, 4),
        local(patch_hbm, patch_ref, 5),
        local(bankid_hbm, bankid_ref, 6),
    ]
    obs_rows = obs.shape[0] // PARTS
    bank_rows = bank.shape[0] // PARTS
    cuts = [pl.ds(i * obs_rows, obs_rows) for i in range(PARTS)]
    obs_parts = [local(obs_hbm.at[c], obs.at[c], 12 + i) for i, c in enumerate(cuts)]
    weight_parts = [
        local(k1_hbm, k1_ref, 7),
        local(k2_hbm, k2_ref, 8),
        local(k3_hbm, k3_ref, 9),
        local(outp_hbm, outp_ref, 10),
        local(scale_hbm, scale_ref, 11),
    ]
    cuts = [pl.ds(i * bank_rows, bank_rows) for i in range(PARTS)]
    bank_parts = [local(bank_hbm.at[c], bank.at[c], 12 + PARTS + i) for i, c in enumerate(cuts)]

    for part in row_parts:
        part.wait()
    feat = rounded(dot(lat_ref[...], inp_ref[...]))
    n_col = n_lon * LW
    row_x[0:8] = feat[n_col - 8 :]
    row_x[8 : 8 + n_col] = feat
    row_x[8 + n_col : 16 + n_col] = feat[0:8]
    for t in range(n_lon):
        sbuf[t] = row_x[8 * t + 4 : 8 * t + 20].astype(BF16)

    for part in id_parts:
        part.wait()
    lane = lax.broadcasted_iota(I32, (nblk, W), 1)
    sub = lax.broadcasted_iota(I32, (nblk, W), 0)
    eye = lane == sub

    def column(row_ref):
        row = jnp.broadcast_to(row_ref[...], (nblk, nblk))
        return jnp.sum(jnp.where(eye[:, :nblk], row, 0), axis=1, keepdims=True)

    own_c = jnp.broadcast_to(column(owner_ref), (nblk, W))
    own_r = jnp.sum(jnp.where(eye, own_c, 0), axis=0, keepdims=True)
    earlier = jnp.where((own_c == own_r) & (lane < sub), 1, 0)
    rank = jnp.sum(earlier, axis=1, keepdims=True)
    slot = own_c * CAP + rank
    pick = lane == slot

    def per_slot(value):
        return jnp.sum(jnp.where(pick, value, 0), axis=0, keepdims=True)

    rows8 = lax.broadcasted_iota(I32, (8, W), 0)
    meta = jnp.where(rows8 == 0, per_slot(sub), 0)
    meta = jnp.where(rows8 == 1, per_slot(jnp.broadcast_to(column(patch_ref), (nblk, W))), meta)
    meta = jnp.where(rows8 == 2, per_slot(jnp.broadcast_to(column(bankid_ref), (nblk, W))), meta)
    meta = jnp.where(rows8 == 3, per_slot(jnp.ones_like(sub)), meta)
    meta_v[b] = meta
    idx_copy = pltpu.make_async_copy(meta_v.at[b], idx_s, dma_sem.at[0])
    idx_copy.start()

    expected = (
        n_lon - 1
        + jnp.where(first_two & up, n_lon, 0)
        + jnp.where(last_two & down, n_lon, 0)
        + 3 * upi
        + 3 * downi
    )
    pl.semaphore_wait(barrier, expected)

    def row_copy(i, t, at, sem):
        return pltpu.make_async_remote_copy(
            src_ref=sbuf.at[t],
            dst_ref=srecv.at[at],
            send_sem=st_send.at[sem],
            recv_sem=st_recv.at[at],
            device_id=(i, t),
            device_id_type=MESH,
        )

    def send_row(s, c):
        t = lax.rem(b + s, n_lon)
        row_copy(a, t, b + 2, t).start()
        return c

    @pl.when(first_two & up)
    def _():
        def go(t, c):
            row_copy(a - 1, t, LR + 2 + b, n_lon + t).start()
            return c

        lax.fori_loop(0, n_lon, go, 0)

    @pl.when(last_two & down)
    def _():
        def go(t, c):
            row_copy(a + 1, t, b - (n_lon - 2), n_lon + t).start()
            return c

        lax.fori_loop(0, n_lon, go, 0)

    lax.fori_loop(1, n_lon, send_row, 0)
    srecv[b + 2] = sbuf[b]

    def meta_copy(t, slot_at):
        return pltpu.make_async_remote_copy(
            src_ref=meta_v.at[b],
            dst_ref=meta_v.at[slot_at],
            send_sem=me_send.at[t],
            recv_sem=me_recv.at[slot_at],
            device_id=(a, t),
            device_id_type=MESH,
        )

    def send_meta(s, c):
        meta_copy(lax.rem(b + s, n_lon), b).start()
        return c

    lax.fori_loop(1, n_lon, send_meta, 0)

    def obs_copy_to(t, slot_at):
        return pltpu.make_async_remote_copy(
            src_ref=sv.at[t],
            dst_ref=rv.at[slot_at],
            send_sem=ob_send.at[t],
            recv_sem=ob_recv.at[slot_at],
            device_id=(a, t),
            device_id_type=MESH,
        )

    tmp[...] = jnp.zeros_like(tmp)
    for part in obs_parts:
        part.wait()
    idx_copy.wait()

    def gathered(t):
        for k in range(CAP):
            block = pl.ds(idx_s[0, t * CAP + k], nvar, stride=nblk)
            tmp[pl.ds(k * VP, nvar), :] = obs[block, :]
        return tmp[...].astype(BF16)

    def send_obs(s, c):
        t = lax.rem(b + s, n_lon)
        sv[t] = gathered(t)
        obs_copy_to(t, b).start()
        return c

    lax.fori_loop(1, n_lon, send_obs, 0)
    rv[b] = gathered(b)

    for part in weight_parts:
        part.wait()
    up_weights(k1_ref, wu1)
    up_weights(k2_ref, wu2)
    pair_weights(k3_ref, w3, False)
    pair_weights(k3_ref, b3, True)
    down_weights(k2_ref, wd2)
    down_weights(k1_ref, wd1)
    opad[...] = jnp.zeros_like(opad)
    opad[0:nvar] = outp_ref[...].astype(F32)
    opt[...] = opad[...].astype(BF16)
    vlane = lax.broadcasted_iota(I32, (VP, nvar), 1)
    vsub = lax.broadcasted_iota(I32, (VP, nvar), 0)
    scale = jnp.broadcast_to(scale_ref[...], (VP, nvar))
    scale = jnp.sum(jnp.where(vlane == vsub, scale, 0.0), axis=1, keepdims=True)
    w2[...] = jnp.broadcast_to(scale * scale, (VP, W))
    for ref in (f1, sl1, m1, b1):
        ref[...] = jnp.zeros_like(ref)
    for ref in (a3, a2):
        ref[...] = jnp.zeros_like(ref)

    def wait_row(s, c):
        at = lax.rem(b + s, n_lon) + 2
        row_copy(a, b, at, 0).wait_recv()
        return c

    lax.fori_loop(1, n_lon, wait_row, 0)

    @pl.when(up)
    def _():
        row_copy(a, b, 0, 0).wait_recv()
        row_copy(a, b, 1, 0).wait_recv()

    @pl.when(down)
    def _():
        row_copy(a, b, LR + 2, 0).wait_recv()
        row_copy(a, b, LR + 3, 0).wait_recv()

    def inside(first, count, pitch, size):
        row = lax.broadcasted_iota(I32, (count, pitch, W), 0) + first
        low = jnp.where(up, -8, 0)
        high = jnp.where(down, size + 8, size)
        return jnp.where((row >= low) & (row < high), 1.0, 0.0).reshape(count * pitch, W)

    def lifted(line, weights):
        left = [shifted(x, -1).astype(BF16) for x in line]
        here = [x.astype(BF16) for x in line]
        right = [shifted(x, 1).astype(BF16) for x in line]
        phases = []
        for q, (u, v) in enumerate(((left, here), (here, right))):
            x = jnp.concatenate([u[0], v[0], u[1], v[1], u[2], v[2]], axis=1)
            y = dot(x, weights[q])
            phases += [y[:, :W], y[:, W:]]
        return phases

    n1 = LR + 2
    line = [srecv[pl.ds(i, n1)].astype(F32).reshape(n1 * LP, W) for i in range(3)]
    mask = inside(-1, n1, LP, LR)
    for ph, pre in enumerate(lifted(line, wu1)):
        s = logistic(pre)
        f1s[ph] = mask * rounded(pre * s + line[1])
        d1s[ph] = mask * (s * (1.0 + pre * (1.0 - s)))

    def spread(i, c):
        for q in range(2):
            for p in range(2):
                to = pl.ds((2 * i + p + 1) * MP + q, 10, stride=2)
                frm = pl.ds(i * LP + 3, 10)
                f1[to, :] = f1s[2 * q + p, frm, :]
                sl1[to, :] = d1s[2 * q + p, frm, :]
        return c

    lax.fori_loop(0, n1, spread, 0)

    def level_two(i, c):
        first = i * C_TWO + GUARD - 2
        line = [f1[pl.ds(pl.multiple_of((first + d) * MP, 8), C_TWO * MP), :] for d in (-1, 0, 1)]
        mask = inside(first - GUARD, C_TWO, MP, MR)
        at = pl.ds(pl.multiple_of(first * MP, 8), C_TWO * MP)
        for ph, pre in enumerate(lifted(line, wu2)):
            s = logistic(pre)
            f2[ph, at, :] = mask * (pre * s + line[1])
            sl2[ph, at, :] = mask * (s * (1.0 + pre * (1.0 - s)))
        return c

    lax.fori_loop(0, (MR + 4) // C_TWO, level_two, 0)

    def paired(planes, weights, q):
        x = jnp.concatenate([planes[m][q + j] for m in range(4) for j in range(3)], axis=1)
        return dot(x, weights[...])

    def head(i, c):
        first = i * C_HEAD + GUARD
        planes = window(f2, first, C_HEAD, MP)
        at = pl.ds(pl.multiple_of(first * MP, 8), C_HEAD * MP)
        for q in range(2):
            y = paired(planes, w3, q)
            for p in range(2):
                pre = y[:, p * W : (p + 1) * W]
                s = logistic(pre)
                act2[2 * q + p, at, :] = pre * s
                sl3[2 * q + p, at, :] = s * (1.0 + pre * (1.0 - s))
        return c

    lax.fori_loop(0, MR // C_HEAD, head, 0)

    def points(r, c):
        for q in range(2):
            for p in range(2):
                to = pl.ds((2 * r + p) * (4 * LW) + q, 2 * LW, stride=2)
                actp[to, :] = act2[2 * q + p, pl.ds((r + GUARD) * MP + 2, 2 * LW), :]
        return c

    lax.fori_loop(0, MR, points, 0)
    for n in range(npatch):
        ft[n] = dot_nt(opt[...], actp[n * plen : (n + 1) * plen].astype(BF16)).astype(BF16)

    def wait_meta(s, c):
        meta_copy(b, lax.rem(b + s, n_lon)).wait_recv()
        return c

    lax.fori_loop(1, n_lon, wait_meta, 0)
    meta_down = pltpu.make_async_copy(meta_v, meta_s, dma_sem.at[1])
    meta_down.start()
    for part in bank_parts:
        part.wait()
    meta_down.wait()
    none = n_lon * CAP
    hist[none] = jnp.zeros((VP, plen), F32)

    def predict(s, c):
        source = lax.rem(b + n_lon - s, n_lon)
        for k in range(CAP):
            rows = bank[meta_s[source, 2, b * CAP + k]]
            pred[s * CAP + k] = dot(ft[meta_s[source, 1, b * CAP + k]], rows)
        return c

    lax.fori_loop(0, n_lon, predict, 0)

    def blocks(s, last):
        source = lax.rem(b + n_lon - s, n_lon)

        @pl.when(s > 0)
        def _():
            obs_copy_to(b, source).wait_recv()

        values = rv[source].astype(F32)
        grads = []
        for k in range(CAP):
            rows = bank[meta_s[source, 2, b * CAP + k]]
            live = meta_s[source, 3, b * CAP + k].astype(F32)
            adjoint = (w2[...] * live) * (pred[s * CAP + k] - values[k * VP : (k + 1) * VP])
            grads.append(dot_nt(adjoint.astype(BF16), rows))
        for k in range(CAP):
            patch = meta_s[source, 1, b * CAP + k]
            before = last[0]
            for n in range(1, npatch):
                before = jnp.where(patch == n, last[n], before)
            hist[s * CAP + k] = grads[k] + hist[before]
            last = tuple(jnp.where(patch == n, s * CAP + k, last[n]) for n in range(npatch))
        return last

    last = lax.fori_loop(0, n_lon, blocks, (jnp.int32(none),) * npatch)

    for n in range(npatch):
        grad = hist[last[n]].astype(BF16)
        ga[n * plen : (n + 1) * plen] = lax.dot_general(
            grad, opt[...], (((0,), (0,)), ((), ())), preferred_element_type=F32
        )

    def adjoint_three(r, c):
        at = pl.ds((r + GUARD) * MP + 2, 2 * LW)
        for q in range(2):
            for p in range(2):
                grad = ga[pl.ds((2 * r + p) * (4 * LW) + q, 2 * LW, stride=2), :]
                a3[2 * q + p, at, :] = grad * sl3[2 * q + p, at, :]
        return c

    lax.fori_loop(0, MR, adjoint_three, 0)

    edge_rows = (0, MR - 2)
    edge_cols = (0, 2 * LW - 2)
    for side in range(2):
        for ph in range(4):
            for i in range(2):
                at = (edge_rows[side] + i + GUARD) * MP + 2
                to = (ph * 2 + i) * 2 * LW
                ns_s[side, to : to + 2 * LW] = a3[ph, at : at + 2 * LW, :].astype(BF16)
                at = GUARD * MP + 2 + edge_cols[side] + i
                to = (ph * 2 + i) * MR
                ew_s[side, to : to + MR] = a3[ph, pl.ds(at, MR, stride=MP), :].astype(BF16)
    for v in range(2):
        for h in range(2):
            for ph in range(4):
                for i in range(2):
                    at = (edge_rows[v] + i + GUARD) * MP + 2 + edge_cols[h]
                    ctmp[v * 2 + h, ph * 4 + i * 2 : ph * 4 + i * 2 + 2] = a3[ph, at : at + 2, :]
            co_s[v * 2 + h] = ctmp[v * 2 + h].astype(BF16)

    def halo_copy(k):
        dy, dx = HALO[k]
        v, h = (dy + 1) // 2, (dx + 1) // 2
        if dy == 0:
            src, dst = ew_s.at[h], ew_r.at[1 - h]
        elif dx == 0:
            src, dst = ns_s.at[v], ns_r.at[1 - v]
        else:
            src, dst = co_s.at[v * 2 + h], co_r.at[(1 - v) * 2 + 1 - h]
        return pltpu.make_async_remote_copy(
            src_ref=src,
            dst_ref=dst,
            send_sem=ha_send.at[k],
            recv_sem=ha_recv.at[7 - k],
            device_id=(a + dy, lax.rem(b + n_lon + dx, n_lon)),
            device_id_type=MESH,
        )

    def halo_arrived(k):
        dy, dx = HALO[k]
        v, h = (dy + 1) // 2, (dx + 1) // 2
        if dy == 0:
            ref = ew_r.at[h]
        elif dx == 0:
            ref = ns_r.at[v]
        else:
            ref = co_r.at[v * 2 + h]
        pltpu.make_async_remote_copy(
            src_ref=ref,
            dst_ref=ref,
            send_sem=ha_send.at[k],
            recv_sem=ha_recv.at[k],
            device_id=(a, b),
            device_id_type=MESH,
        ).wait_recv()

    there = {-1: up, 1: down}
    for dy in (-1, 1):

        @pl.when(there[dy])
        def _():
            for k, (ky, _kx) in enumerate(HALO):
                if ky == dy:
                    halo_copy(k).start()

    for k, (ky, _kx) in enumerate(HALO):
        if ky == 0:
            halo_copy(k).start()

    halo_rows = (-2, MR)
    halo_cols = (0, 2 * LW + 2)
    for dy in (-1, 1):

        @pl.when(there[dy])
        def _():
            v = (dy + 1) // 2
            for k, (ky, _kx) in enumerate(HALO):
                if ky == dy:
                    halo_arrived(k)
            for ph in range(4):
                for i in range(2):
                    at = (halo_rows[v] + i + GUARD) * MP + 2
                    frm = (ph * 2 + i) * 2 * LW
                    a3[ph, at : at + 2 * LW, :] = ns_r[v, frm : frm + 2 * LW].astype(F32)
            for h in range(2):
                ctmp[v * 2 + h] = co_r[v * 2 + h].astype(F32)
                for ph in range(4):
                    for i in range(2):
                        at = (halo_rows[v] + i + GUARD) * MP + halo_cols[h]
                        a3[ph, at : at + 2, :] = ctmp[
                            v * 2 + h, ph * 4 + i * 2 : ph * 4 + i * 2 + 2
                        ]

    for k, (ky, kx) in enumerate(HALO):
        if ky == 0:
            h = (kx + 1) // 2
            halo_arrived(k)
            for ph in range(4):
                for i in range(2):
                    frm = (ph * 2 + i) * MR
                    at = GUARD * MP + halo_cols[h] + i
                    a3[ph, pl.ds(at, MR, stride=MP), :] = ew_r[h, frm : frm + MR].astype(F32)

    def back_three(i, c):
        first = i * C_B3 + GUARD - 2
        planes = window(a3, first, C_B3, MP)
        at = pl.ds(pl.multiple_of(first * MP, 8), C_B3 * MP)
        total = jnp.zeros((C_B3 * MP, W), F32)
        for q in range(2):
            y = paired(planes, b3, q)
            for p in range(2):
                back = y[:, p * W : (p + 1) * W]
                a2[2 * q + p, at, :] = back * sl2[2 * q + p, at, :]
                total = total + back
        ds2[at, :] = total
        return c

    lax.fori_loop(0, (MR + 4) // C_B3, back_three, 0)

    def gathered_down(planes, weights):
        x = jnp.concatenate([planes[m][n] for m in range(4) for n in range(4)], axis=1)
        return dot(x, weights[...])

    def back_two(i, c):
        first = i * C_B2 + GUARD - 2
        at = pl.ds(pl.multiple_of(first * MP, 8), C_B2 * MP)
        back = ds2[at, :] + gathered_down(window(a2, first, C_B2, MP), wd2)
        b1[at, :] = back
        m1[at, :] = back * sl1[at, :]
        return c

    lax.fori_loop(0, (MR + 4) // C_B2, back_two, 0)

    def gather(i, c):
        total = jnp.zeros((LP, W), F32)
        for q in range(2):
            for p in range(2):
                frm = pl.ds((2 * i + p + 1) * MP + q, LP, stride=2)
                a1[2 * q + p, pl.ds(pl.multiple_of(i * LP, 8), LP), :] = m1[frm, :]
                total = total + b1[frm, :]
        zbuf[pl.ds(pl.multiple_of(i * LP, 8), LP), :] = total
        return c

    lax.fori_loop(0, n1, gather, 0)
    back = zbuf[LP : LP + LR * LP] + gathered_down(window(a1, 1, LR, LP), wd1)
    zbuf[LP : LP + LR * LP] = rounded(back)
    for r in range(LR):
        zs[r] = zbuf[(r + 1) * LP + 1 : (r + 1) * LP + 1 + LW]

    def z_copy(t, slot_at):
        return pltpu.make_async_remote_copy(
            src_ref=zs.at[t],
            dst_ref=zr.at[slot_at],
            send_sem=z_send.at[t],
            recv_sem=z_recv.at[slot_at],
            device_id=(a, t),
            device_id_type=MESH,
        )

    def send_z(s, c):
        z_copy(lax.rem(b + s, n_lon), b).start()
        return c

    lax.fori_loop(1, n_lon, send_z, 0)
    zr[b] = zs[b]

    def sent(s, c):
        t = lax.rem(b + s, n_lon)
        row_copy(a, t, b + 2, t).wait_send()
        meta_copy(t, b).wait_send()
        obs_copy_to(t, b).wait_send()
        return c

    lax.fori_loop(1, n_lon, sent, 0)

    @pl.when((first_two & up) | (last_two & down))
    def _():
        def go(t, c):
            row_copy(a, t, b + 2, n_lon + t).wait_send()
            return c

        lax.fori_loop(0, n_lon, go, 0)

    for dy in (-1, 1):

        @pl.when(there[dy])
        def _():
            for k, (ky, _kx) in enumerate(HALO):
                if ky == dy:
                    halo_copy(k).wait_send()

    for k, (ky, _kx) in enumerate(HALO):
        if ky == 0:
            halo_copy(k).wait_send()

    def finish(s, c):
        t = lax.rem(b + s, n_lon)
        z_copy(t, b).wait_send()
        z_copy(b, t).wait_recv()
        return c

    lax.fori_loop(1, n_lon, finish, 0)
    out_ref[...] = zr[...].reshape(n_col, W).astype(BF16)


def per_device(
    n_lat,
    n_lon,
    latents,
    in_proj,
    kernel_one,
    kernel_two,
    kernel_three,
    out_proj,
    bank,
    obs_values,
    obs_scale,
    owner_col,
    patch_id,
    bank_id,
):
    LR = n_lon
    MR = 2 * LR
    npts = 4 * LR * 4 * LW
    plen = bank.shape[1]
    nmid = (MR + 2 * GUARD) * MP
    n1 = LR + 2
    slots = n_lon * CAP
    vmem = pltpu.VMEM
    dma = pltpu.SemaphoreType.DMA
    nvar, nblk = obs_values.shape[1], obs_values.shape[0]
    scratch = [
        vmem(latents.shape, BF16),
        vmem(in_proj.shape, BF16),
        vmem(kernel_one.shape, BF16),
        vmem(kernel_two.shape, BF16),
        vmem(kernel_three.shape, BF16),
        vmem((nvar, W), BF16),
        vmem((1, nvar), F32),
        vmem((1, nblk), I32),
        vmem((1, nblk), I32),
        vmem((1, nblk), I32),
        vmem(bank.shape, BF16),
        vmem((obs_values.shape[0] * obs_values.shape[1], W), F32),
        vmem((n_lon * LW + 16, W), F32),
        vmem((n_lon, LP, W), BF16),
        vmem((LR + 4, LP, W), BF16),
        vmem((n_lon, 8, W), I32),
        pltpu.SMEM((8, W), I32),
        pltpu.SMEM((n_lon, 8, W), I32),
        vmem((CAP * VP, W), F32),
        vmem((n_lon, CAP * VP, W), BF16),
        vmem((n_lon, CAP * VP, W), BF16),
        vmem((2, 6 * W, 2 * W), BF16),
        vmem((2, 6 * W, 2 * W), BF16),
        vmem((12 * W, 2 * W), BF16),
        vmem((12 * W, 2 * W), BF16),
        vmem((16 * W, W), BF16),
        vmem((16 * W, W), BF16),
        vmem((VP, W), BF16),
        vmem((VP, W), F32),
        vmem((VP, W), F32),
        vmem((4, n1 * LP, W), F32),
        vmem((4, n1 * LP, W), F32),
        vmem((nmid, W), F32),
        vmem((nmid, W), F32),
        vmem((4, nmid, W), F32),
        vmem((4, nmid, W), F32),
        vmem((4, nmid, W), F32),
        vmem((4, nmid, W), F32),
        vmem((npts, W), F32),
        vmem((npts // plen, VP, plen), BF16),
        vmem((slots, VP, W), F32),
        vmem((slots + 1, VP, plen), F32),
        vmem((npts, W), F32),
        vmem((4, nmid, W), F32),
        vmem((4, nmid, W), F32),
        vmem((nmid, W), F32),
        vmem((nmid, W), F32),
        vmem((nmid, W), F32),
        vmem((4, n1 * LP, W), F32),
        vmem((n1 * LP, W), F32),
        vmem((n_lon, LW, W), F32),
        vmem((n_lon, LW, W), F32),
        vmem((4, 16, W), F32),
        vmem((2, 4 * 2 * 2 * LW, W), BF16),
        vmem((2, 4 * 2 * 2 * LW, W), BF16),
        vmem((2, 4 * 2 * MR, W), BF16),
        vmem((2, 4 * 2 * MR, W), BF16),
        vmem((4, 16, W), BF16),
        vmem((4, 16, W), BF16),
        dma((12 + 2 * PARTS,)),
        dma((2 * n_lon,)),
        dma((LR + 4,)),
        dma((n_lon,)),
        dma((n_lon,)),
        dma((n_lon,)),
        dma((n_lon,)),
        dma((8,)),
        dma((8,)),
        dma((n_lon,)),
        dma((n_lon,)),
    ]
    here = pl.BlockSpec(memory_space=pltpu.VMEM)
    far = pl.BlockSpec(memory_space=pl.ANY)
    back_zero = pl.pallas_call(
        functools.partial(kernel, n_lat, n_lon),
        out_shape=jax.ShapeDtypeStruct((latents.shape[0], W), BF16),
        in_specs=[far] * 12,
        out_specs=here,
        scratch_shapes=scratch,
        compiler_params=pltpu.CompilerParams(
            collective_id=0, has_side_effects=True, vmem_limit_bytes=56 * 1024 * 1024
        ),
        cost_estimate=pl.CostEstimate(
            flops=5_000_000_000, bytes_accessed=4_000_000, transcendentals=1_000_000
        ),
    )(
        latents,
        in_proj,
        kernel_one,
        kernel_two,
        kernel_three,
        out_proj.T,
        bank,
        jnp.transpose(obs_values, (1, 0, 2)).reshape(nvar * nblk, W),
        obs_scale.reshape(1, -1),
        owner_col.reshape(1, -1),
        patch_id.reshape(1, -1),
        bank_id.reshape(1, -1),
    )
    return dot_nt(back_zero, in_proj)


def solution(mesh):
    n_lat, n_lon = mesh.shape["lat"], mesh.shape["lon"]
    placed = (
        P(("lat", "lon"), None),
        P(),
        P(),
        P(),
        P(),
        P(),
        P(),
        P(("lat", "lon"), None, None),
        P(),
        P(("lat", "lon"), None),
        P(("lat", "lon")),
        P(("lat", "lon")),
    )
    return jax.shard_map(
        functools.partial(per_device, n_lat, n_lon),
        mesh=mesh,
        in_specs=placed,
        out_specs=P(("lat", "lon"), None),
        check_vma=False,
    )
```

```python
import functools

import jax
import jax.numpy as jnp
from jax import lax
from jax.experimental import pallas as pl
from jax.experimental.pallas import tpu as pltpu
from jax.sharding import PartitionSpec as P

F32 = jnp.float32
BF16 = jnp.bfloat16
I32 = jnp.int32
MESH = pl.DeviceIdType.MESH
CAP = 4
LW = 8
W = 128
VP = 72
MP = 24
LP = 16
S_TWO, S_HEAD, S_B3, S_B2 = 3, 2, 2, 2
PARTS = 4
GUARD = 3
HALO = [(-1, -1), (-1, 0), (-1, 1), (0, -1), (0, 1), (1, -1), (1, 0), (1, 1)]


def dot(x, y):
    return jnp.dot(x, y, preferred_element_type=F32)


def dot_nt(x, y):
    return lax.dot_general(x, y, (((1,), (1,)), ((), ())), preferred_element_type=F32)


def shifted(x, by):
    return x if by == 0 else pltpu.roll(x, (-by) % x.shape[0], 0)


def logistic(x):
    return 0.5 * jnp.tanh(0.5 * x) + 0.5


def rounded(x):
    return x.astype(BF16).astype(F32)


TAPS = [(1, -1), (0, 0), (1, 0), (0, 1)]


def window(src, first, count, pitch):
    planes = []
    for p, dr in TAPS:
        line = []
        for q, dc in TAPS:
            at = pl.multiple_of((first + dr) * pitch, 8)
            line.append(shifted(src[2 * q + p, pl.ds(at, count * pitch), :], dc).astype(BF16))
        planes.append(line)
    return planes


def up_weights(k_ref, out_ref):
    rows = {(0, 0): [0], (0, 1): [1, 2], (0, 2): [], (1, 0): [], (1, 1): [0, 1], (1, 2): [2]}
    cols = {(0, 0): [0], (0, 1): [1, 2], (1, 0): [0, 1], (1, 1): [2]}
    for q in range(2):
        for rr in range(3):
            for cc in range(2):
                for p in range(2):
                    block = jnp.zeros((W, W), F32)
                    for i in rows[p, rr]:
                        for j in cols[q, cc]:
                            block = block + k_ref[i, j].astype(F32)
                    at = (rr * 2 + cc) * W
                    out_ref[q, at : at + W, p * W : (p + 1) * W] = block.astype(BF16)


def pair_weights(k_ref, out_ref, flip):
    for m in range(4):
        for j in range(3):
            at = (m * 3 + j) * W
            for p in range(2):
                i = m - p
                if 0 <= i <= 2:
                    block = k_ref[2 - i, 2 - j].astype(F32).T if flip else k_ref[i, j].astype(F32)
                else:
                    block = jnp.zeros((W, W), F32)
                out_ref[at : at + W, p * W : (p + 1) * W] = block.astype(BF16)


def down_weights(k_ref, out_ref):
    for m in range(4):
        for n in range(4):
            block = jnp.zeros((W, W), F32)
            for i in (m - 1, m):
                for j in (n - 1, n):
                    if 0 <= i <= 2 and 0 <= j <= 2:
                        block = block + k_ref[2 - i, 2 - j].astype(F32)
            at = (m * 4 + n) * W
            out_ref[at : at + W, :] = block.T.astype(BF16)


def kernel(
    n_lat,
    n_lon,
    lat_hbm,
    inp_hbm,
    k1_hbm,
    k2_hbm,
    k3_hbm,
    outp_hbm,
    bank_hbm,
    obs_hbm,
    scale_hbm,
    owner_hbm,
    patch_hbm,
    bankid_hbm,
    out_ref,
    lat_ref,
    inp_ref,
    k1_ref,
    k2_ref,
    k3_ref,
    outp_ref,
    scale_ref,
    owner_ref,
    patch_ref,
    bankid_ref,
    bank,
    obs,
    row_x,
    sbuf,
    srecv,
    meta_v,
    idx_s,
    meta_s,
    tmp,
    sv,
    rv,
    wu1,
    wu2,
    w3,
    b3,
    wd1,
    wd2,
    opt,
    opad,
    w2,
    f1s,
    d1s,
    f1,
    sl1,
    f2,
    sl2,
    act2,
    sl3,
    actp,
    ft,
    pred,
    hist,
    ga,
    a3,
    a2,
    ds2,
    b1,
    m1,
    a1,
    zbuf,
    zs,
    zr,
    ctmp,
    ns_s,
    ns_r,
    ew_s,
    ew_r,
    co_s,
    co_r,
    dma_sem,
    st_send,
    st_recv,
    me_send,
    me_recv,
    ob_send,
    ob_recv,
    ha_send,
    ha_recv,
    z_send,
    z_recv,
):
    a, b = lax.axis_index("lat"), lax.axis_index("lon")
    LR = n_lon
    MR = 2 * LR
    npatch = (4 * LR * 4 * LW) // bank.shape[1]
    plen = bank.shape[1]
    C_TWO, C_B3, C_B2 = (MR + 4) // S_TWO, (MR + 4) // S_B3, (MR + 4) // S_B2
    C_HEAD = MR // S_HEAD
    nblk = patch_ref.shape[1]
    nvar = outp_ref.shape[0]
    up, down = a > 0, a < n_lat - 1
    upi, downi = jnp.where(up, 1, 0), jnp.where(down, 1, 0)
    first_two, last_two = b < 2, b >= n_lon - 2

    flips = [bit * (1 - 2 * lax.rem(b // bit, 2)) for bit in (1, 2, 4, 8) if bit < n_lon]
    groups = n_lon // 4
    order = range(n_lon - 1, 0, -1)

    def peer(k):
        return b + sum(flip for i, flip in enumerate(flips) if k >> i & 1)

    def after(t):
        return b + t - jnp.where(b + t >= n_lon, n_lon, 0)

    def before_me(t):
        return b - t + jnp.where(b < t, n_lon, 0)

    for row in (0, 1, LR + 2, LR + 3):
        srecv[row] = jnp.zeros((LP, W), BF16)

    barrier = pltpu.get_barrier_semaphore()

    def greet(i, j):
        pl.semaphore_signal(barrier, inc=1, device_id=(i, j), device_id_type=MESH)

    for k in order:
        greet(a, peer(k))

    @pl.when(up)
    def _():
        greet(a - 1, n_lon - 2)
        greet(a - 1, n_lon - 1)
        for d in range(3):
            greet(a - 1, lax.rem(b + n_lon - 1 + d, n_lon))

    @pl.when(down)
    def _():
        greet(a + 1, 0)
        greet(a + 1, 1)
        for d in range(3):
            greet(a + 1, lax.rem(b + n_lon - 1 + d, n_lon))

    def local(src, dst, sem):
        copy = pltpu.make_async_copy(src, dst, dma_sem.at[sem])
        copy.start()
        return copy

    row_parts = [local(lat_hbm, lat_ref, 2), local(inp_hbm, inp_ref, 3)]
    id_parts = [
        local(owner_hbm, owner_ref, 4),
        local(patch_hbm, patch_ref, 5),
        local(bankid_hbm, bankid_ref, 6),
    ]
    obs_rows = obs.shape[0] // PARTS
    bank_rows = bank.shape[0] // PARTS
    cuts = [pl.ds(i * obs_rows, obs_rows) for i in range(PARTS)]
    obs_parts = [local(obs_hbm.at[c], obs.at[c], 12 + i) for i, c in enumerate(cuts)]
    weight_parts = [
        local(k1_hbm, k1_ref, 7),
        local(k2_hbm, k2_ref, 8),
        local(k3_hbm, k3_ref, 9),
        local(outp_hbm, outp_ref, 10),
        local(scale_hbm, scale_ref, 11),
    ]
    cuts = [pl.ds(i * bank_rows, bank_rows) for i in range(PARTS)]
    bank_parts = [local(bank_hbm.at[c], bank.at[c], 12 + PARTS + i) for i, c in enumerate(cuts)]

    for part in row_parts:
        part.wait()
    feat = rounded(dot(lat_ref[...], inp_ref[...]))
    n_col = n_lon * LW
    row_x[0:8] = feat[n_col - 8 :]
    row_x[8 : 8 + n_col] = feat
    row_x[8 + n_col : 16 + n_col] = feat[0:8]
    for t in range(n_lon):
        sbuf[t] = row_x[8 * t + 4 : 8 * t + 20].astype(BF16)

    for part in id_parts:
        part.wait()
    lane = lax.broadcasted_iota(I32, (nblk, W), 1)
    sub = lax.broadcasted_iota(I32, (nblk, W), 0)
    eye = lane == sub

    def column(row_ref):
        row = jnp.broadcast_to(row_ref[...], (nblk, nblk))
        return jnp.sum(jnp.where(eye[:, :nblk], row, 0), axis=1, keepdims=True)

    own_c = jnp.broadcast_to(column(owner_ref), (nblk, W))
    own_r = jnp.sum(jnp.where(eye, own_c, 0), axis=0, keepdims=True)
    earlier = jnp.where((own_c == own_r) & (lane < sub), 1, 0)
    rank = jnp.sum(earlier, axis=1, keepdims=True)
    slot = own_c * CAP + rank
    pick = lane == slot

    def per_slot(value):
        return jnp.sum(jnp.where(pick, value, 0), axis=0, keepdims=True)

    rows8 = lax.broadcasted_iota(I32, (8, W), 0)
    meta = jnp.where(rows8 == 0, per_slot(sub), 0)
    meta = jnp.where(rows8 == 1, per_slot(jnp.broadcast_to(column(patch_ref), (nblk, W))), meta)
    meta = jnp.where(rows8 == 2, per_slot(jnp.broadcast_to(column(bankid_ref), (nblk, W))), meta)
    meta = jnp.where(rows8 == 3, per_slot(jnp.ones_like(sub)), meta)
    meta_v[b] = meta
    idx_copy = pltpu.make_async_copy(meta_v.at[b], idx_s, dma_sem.at[0])
    idx_copy.start()

    expected = (
        n_lon - 1
        + jnp.where(first_two & up, n_lon, 0)
        + jnp.where(last_two & down, n_lon, 0)
        + 3 * upi
        + 3 * downi
    )
    pl.semaphore_wait(barrier, expected)

    def row_copy(i, t, at, sem):
        return pltpu.make_async_remote_copy(
            src_ref=sbuf.at[t],
            dst_ref=srecv.at[at],
            send_sem=st_send.at[sem],
            recv_sem=st_recv.at[at],
            device_id=(i, t),
            device_id_type=MESH,
        )

    for k in order:
        row_copy(a, peer(k), b + 2, peer(k)).start()

    @pl.when(first_two & up)
    def _():
        def go(t, c):
            row_copy(a - 1, t, LR + 2 + b, n_lon + t).start()
            return c

        lax.fori_loop(0, n_lon, go, 0)

    @pl.when(last_two & down)
    def _():
        def go(t, c):
            row_copy(a + 1, t, b - (n_lon - 2), n_lon + t).start()
            return c

        lax.fori_loop(0, n_lon, go, 0)

    srecv[b + 2] = sbuf[b]

    def meta_copy(t, slot_at):
        return pltpu.make_async_remote_copy(
            src_ref=meta_v.at[b],
            dst_ref=meta_v.at[slot_at],
            send_sem=me_send.at[t],
            recv_sem=me_recv.at[slot_at],
            device_id=(a, t),
            device_id_type=MESH,
        )

    for k in order:
        meta_copy(peer(k), b).start()

    def obs_copy_to(t, slot_at):
        return pltpu.make_async_remote_copy(
            src_ref=sv.at[t],
            dst_ref=rv.at[slot_at],
            send_sem=ob_send.at[t],
            recv_sem=ob_recv.at[slot_at],
            device_id=(a, t),
            device_id_type=MESH,
        )

    tmp[...] = jnp.zeros_like(tmp)
    for part in obs_parts:
        part.wait()
    idx_copy.wait()

    def gathered(t):
        for k in range(CAP):
            block = pl.ds(idx_s[0, t * CAP + k], nvar, stride=nblk)
            tmp[pl.ds(k * VP, nvar), :] = obs[block, :]
        return tmp[...].astype(BF16)

    def send_obs(g, c):
        for k in range(4):
            t = after(g * 4 + k)
            if k > 0:
                sv[t] = gathered(t)
                obs_copy_to(t, b).start()
            else:

                @pl.when(g > 0)
                def _():
                    sv[t] = gathered(t)
                    obs_copy_to(t, b).start()

        return c

    lax.fori_loop(0, groups, send_obs, 0)
    rv[b] = gathered(b)

    for part in weight_parts:
        part.wait()
    up_weights(k1_ref, wu1)
    up_weights(k2_ref, wu2)
    pair_weights(k3_ref, w3, False)
    pair_weights(k3_ref, b3, True)
    down_weights(k2_ref, wd2)
    down_weights(k1_ref, wd1)
    opad[...] = jnp.zeros_like(opad)
    opad[0:nvar] = outp_ref[...].astype(F32)
    opt[...] = opad[...].astype(BF16)
    vlane = lax.broadcasted_iota(I32, (VP, nvar), 1)
    vsub = lax.broadcasted_iota(I32, (VP, nvar), 0)
    scale = jnp.broadcast_to(scale_ref[...], (VP, nvar))
    scale = jnp.sum(jnp.where(vlane == vsub, scale, 0.0), axis=1, keepdims=True)
    w2[...] = jnp.broadcast_to(scale * scale, (VP, W))
    for ref in (f1, sl1, m1, b1):
        ref[...] = jnp.zeros_like(ref)
    for ref in (a3, a2):
        ref[...] = jnp.zeros_like(ref)

    for k in order:
        row_copy(a, b, peer(k) + 2, 0).wait_recv()

    @pl.when(up)
    def _():
        row_copy(a, b, 0, 0).wait_recv()
        row_copy(a, b, 1, 0).wait_recv()

    @pl.when(down)
    def _():
        row_copy(a, b, LR + 2, 0).wait_recv()
        row_copy(a, b, LR + 3, 0).wait_recv()

    def inside(first, count, pitch, size):
        row = lax.broadcasted_iota(I32, (count, pitch, W), 0) + first
        low = jnp.where(up, -8, 0)
        high = jnp.where(down, size + 8, size)
        return jnp.where((row >= low) & (row < high), 1.0, 0.0).reshape(count * pitch, W)

    def lifted(line, weights):
        left = [shifted(x, -1).astype(BF16) for x in line]
        here = [x.astype(BF16) for x in line]
        right = [shifted(x, 1).astype(BF16) for x in line]
        phases = []
        for q, (u, v) in enumerate(((left, here), (here, right))):
            x = jnp.concatenate([u[0], v[0], u[1], v[1], u[2], v[2]], axis=1)
            y = dot(x, weights[q])
            phases += [y[:, :W], y[:, W:]]
        return phases

    n1 = LR + 2
    line = [srecv[pl.ds(i, n1)].astype(F32).reshape(n1 * LP, W) for i in range(3)]
    mask = inside(-1, n1, LP, LR)
    for ph, pre in enumerate(lifted(line, wu1)):
        s = logistic(pre)
        f1s[ph] = mask * rounded(pre * s + line[1])
        d1s[ph] = mask * (s * (1.0 + pre * (1.0 - s)))

    def spread(i, c):
        for q in range(2):
            for p in range(2):
                to = pl.ds((2 * i + p + 1) * MP + q, 10, stride=2)
                frm = pl.ds(i * LP + 3, 10)
                f1[to, :] = f1s[2 * q + p, frm, :]
                sl1[to, :] = d1s[2 * q + p, frm, :]
        return c

    lax.fori_loop(0, n1, spread, 0)

    for k in order:
        meta_copy(b, peer(k)).wait_recv()
    meta_down = pltpu.make_async_copy(meta_v, meta_s, dma_sem.at[1])
    meta_down.start()

    def level_two(i, c):
        first = i * C_TWO + GUARD - 2
        line = [f1[pl.ds(pl.multiple_of((first + d) * MP, 8), C_TWO * MP), :] for d in (-1, 0, 1)]
        mask = inside(first - GUARD, C_TWO, MP, MR)
        at = pl.ds(pl.multiple_of(first * MP, 8), C_TWO * MP)
        for ph, pre in enumerate(lifted(line, wu2)):
            s = logistic(pre)
            f2[ph, at, :] = mask * (pre * s + line[1])
            sl2[ph, at, :] = mask * (s * (1.0 + pre * (1.0 - s)))
        return c

    lax.fori_loop(0, (MR + 4) // C_TWO, level_two, 0)

    def paired(planes, weights, q):
        x = jnp.concatenate([planes[m][q + j] for m in range(4) for j in range(3)], axis=1)
        return dot(x, weights[...])

    def head(i, c):
        first = i * C_HEAD + GUARD
        planes = window(f2, first, C_HEAD, MP)
        at = pl.ds(pl.multiple_of(first * MP, 8), C_HEAD * MP)
        for q in range(2):
            y = paired(planes, w3, q)
            for p in range(2):
                pre = y[:, p * W : (p + 1) * W]
                s = logistic(pre)
                act2[2 * q + p, at, :] = pre * s
                sl3[2 * q + p, at, :] = s * (1.0 + pre * (1.0 - s))
        return c

    lax.fori_loop(0, MR // C_HEAD, head, 0)

    def points(r, c):
        for q in range(2):
            for p in range(2):
                to = pl.ds((2 * r + p) * (4 * LW) + q, 2 * LW, stride=2)
                actp[to, :] = act2[2 * q + p, pl.ds((r + GUARD) * MP + 2, 2 * LW), :]
        return c

    lax.fori_loop(0, MR, points, 0)
    for n in range(npatch):
        ft[n] = dot_nt(opt[...], actp[n * plen : (n + 1) * plen].astype(BF16)).astype(BF16)

    for part in bank_parts:
        part.wait()
    meta_down.wait()
    none = n_lon * CAP
    hist[none] = jnp.zeros((VP, plen), F32)

    def predict(g, c):
        for m in range(4):
            source = before_me(g * 4 + m)
            for k in range(CAP):
                rows = bank[meta_s[source, 2, b * CAP + k]]
                slot_at = (g * 4 + m) * CAP + k
                pred[slot_at] = dot(ft[meta_s[source, 1, b * CAP + k]], rows)
        return c

    lax.fori_loop(0, groups, predict, 0)

    def blocks(g, last):
        for m in range(4):
            source = before_me(g * 4 + m)
            if m > 0:
                obs_copy_to(b, source).wait_recv()
            else:

                @pl.when(g > 0)
                def _():
                    obs_copy_to(b, source).wait_recv()

            values = rv[source].astype(F32)
            grads = []
            for k in range(CAP):
                rows = bank[meta_s[source, 2, b * CAP + k]]
                live = meta_s[source, 3, b * CAP + k].astype(F32)
                miss = pred[(g * 4 + m) * CAP + k] - values[k * VP : (k + 1) * VP]
                grads.append(dot_nt(((w2[...] * live) * miss).astype(BF16), rows))
            for k in range(CAP):
                patch = meta_s[source, 1, b * CAP + k]
                slot_at = (g * 4 + m) * CAP + k
                before = last[0]
                for n in range(1, npatch):
                    before = jnp.where(patch == n, last[n], before)
                hist[slot_at] = grads[k] + hist[before]
                last = tuple(jnp.where(patch == n, slot_at, last[n]) for n in range(npatch))
        return last

    last = lax.fori_loop(0, groups, blocks, (jnp.int32(none),) * npatch)

    for n in range(npatch):
        grad = hist[last[n]].astype(BF16)
        ga[n * plen : (n + 1) * plen] = lax.dot_general(
            grad, opt[...], (((0,), (0,)), ((), ())), preferred_element_type=F32
        )

    def adjoint_three(r, c):
        at = pl.ds((r + GUARD) * MP + 2, 2 * LW)
        for q in range(2):
            for p in range(2):
                grad = ga[pl.ds((2 * r + p) * (4 * LW) + q, 2 * LW, stride=2), :]
                a3[2 * q + p, at, :] = grad * sl3[2 * q + p, at, :]
        return c

    lax.fori_loop(0, MR, adjoint_three, 0)

    edge_rows = (0, MR - 2)
    edge_cols = (0, 2 * LW - 2)
    for side in range(2):
        for ph in range(4):
            for i in range(2):
                at = (edge_rows[side] + i + GUARD) * MP + 2
                to = (ph * 2 + i) * 2 * LW
                ns_s[side, to : to + 2 * LW] = a3[ph, at : at + 2 * LW, :].astype(BF16)
                at = GUARD * MP + 2 + edge_cols[side] + i
                to = (ph * 2 + i) * MR
                ew_s[side, to : to + MR] = a3[ph, pl.ds(at, MR, stride=MP), :].astype(BF16)
    for v in range(2):
        for h in range(2):
            for ph in range(4):
                for i in range(2):
                    at = (edge_rows[v] + i + GUARD) * MP + 2 + edge_cols[h]
                    ctmp[v * 2 + h, ph * 4 + i * 2 : ph * 4 + i * 2 + 2] = a3[ph, at : at + 2, :]
            co_s[v * 2 + h] = ctmp[v * 2 + h].astype(BF16)

    def halo_copy(k):
        dy, dx = HALO[k]
        v, h = (dy + 1) // 2, (dx + 1) // 2
        if dy == 0:
            src, dst = ew_s.at[h], ew_r.at[1 - h]
        elif dx == 0:
            src, dst = ns_s.at[v], ns_r.at[1 - v]
        else:
            src, dst = co_s.at[v * 2 + h], co_r.at[(1 - v) * 2 + 1 - h]
        return pltpu.make_async_remote_copy(
            src_ref=src,
            dst_ref=dst,
            send_sem=ha_send.at[k],
            recv_sem=ha_recv.at[7 - k],
            device_id=(a + dy, lax.rem(b + n_lon + dx, n_lon)),
            device_id_type=MESH,
        )

    def halo_arrived(k):
        dy, dx = HALO[k]
        v, h = (dy + 1) // 2, (dx + 1) // 2
        if dy == 0:
            ref = ew_r.at[h]
        elif dx == 0:
            ref = ns_r.at[v]
        else:
            ref = co_r.at[v * 2 + h]
        pltpu.make_async_remote_copy(
            src_ref=ref,
            dst_ref=ref,
            send_sem=ha_send.at[k],
            recv_sem=ha_recv.at[k],
            device_id=(a, b),
            device_id_type=MESH,
        ).wait_recv()

    there = {-1: up, 1: down}
    for dy in (-1, 1):

        @pl.when(there[dy])
        def _():
            for k, (ky, _kx) in enumerate(HALO):
                if ky == dy:
                    halo_copy(k).start()

    for k, (ky, _kx) in enumerate(HALO):
        if ky == 0:
            halo_copy(k).start()

    halo_rows = (-2, MR)
    halo_cols = (0, 2 * LW + 2)
    for dy in (-1, 1):

        @pl.when(there[dy])
        def _():
            v = (dy + 1) // 2
            for k, (ky, _kx) in enumerate(HALO):
                if ky == dy:
                    halo_arrived(k)
            for ph in range(4):
                for i in range(2):
                    at = (halo_rows[v] + i + GUARD) * MP + 2
                    frm = (ph * 2 + i) * 2 * LW
                    a3[ph, at : at + 2 * LW, :] = ns_r[v, frm : frm + 2 * LW].astype(F32)
            for h in range(2):
                ctmp[v * 2 + h] = co_r[v * 2 + h].astype(F32)
                for ph in range(4):
                    for i in range(2):
                        at = (halo_rows[v] + i + GUARD) * MP + halo_cols[h]
                        a3[ph, at : at + 2, :] = ctmp[
                            v * 2 + h, ph * 4 + i * 2 : ph * 4 + i * 2 + 2
                        ]

    for k, (ky, kx) in enumerate(HALO):
        if ky == 0:
            h = (kx + 1) // 2
            halo_arrived(k)
            for ph in range(4):
                for i in range(2):
                    frm = (ph * 2 + i) * MR
                    at = GUARD * MP + halo_cols[h] + i
                    a3[ph, pl.ds(at, MR, stride=MP), :] = ew_r[h, frm : frm + MR].astype(F32)

    def back_three(i, c):
        first = i * C_B3 + GUARD - 2
        planes = window(a3, first, C_B3, MP)
        at = pl.ds(pl.multiple_of(first * MP, 8), C_B3 * MP)
        total = jnp.zeros((C_B3 * MP, W), F32)
        for q in range(2):
            y = paired(planes, b3, q)
            for p in range(2):
                back = y[:, p * W : (p + 1) * W]
                a2[2 * q + p, at, :] = back * sl2[2 * q + p, at, :]
                total = total + back
        ds2[at, :] = total
        return c

    lax.fori_loop(0, (MR + 4) // C_B3, back_three, 0)

    def gathered_down(planes, weights):
        x = jnp.concatenate([planes[m][n] for m in range(4) for n in range(4)], axis=1)
        return dot(x, weights[...])

    def back_two(i, c):
        first = i * C_B2 + GUARD - 2
        at = pl.ds(pl.multiple_of(first * MP, 8), C_B2 * MP)
        back = ds2[at, :] + gathered_down(window(a2, first, C_B2, MP), wd2)
        b1[at, :] = back
        m1[at, :] = back * sl1[at, :]
        return c

    lax.fori_loop(0, (MR + 4) // C_B2, back_two, 0)

    def gather(i, c):
        total = jnp.zeros((LP, W), F32)
        for q in range(2):
            for p in range(2):
                frm = pl.ds((2 * i + p + 1) * MP + q, LP, stride=2)
                a1[2 * q + p, pl.ds(pl.multiple_of(i * LP, 8), LP), :] = m1[frm, :]
                total = total + b1[frm, :]
        zbuf[pl.ds(pl.multiple_of(i * LP, 8), LP), :] = total
        return c

    lax.fori_loop(0, n1, gather, 0)
    back = zbuf[LP : LP + LR * LP] + gathered_down(window(a1, 1, LR, LP), wd1)
    zbuf[LP : LP + LR * LP] = rounded(back)
    for r in range(LR):
        zs[r] = zbuf[(r + 1) * LP + 1 : (r + 1) * LP + 1 + LW]

    def z_copy(t, slot_at):
        return pltpu.make_async_remote_copy(
            src_ref=zs.at[t],
            dst_ref=zr.at[slot_at],
            send_sem=z_send.at[t],
            recv_sem=z_recv.at[slot_at],
            device_id=(a, t),
            device_id_type=MESH,
        )

    for k in order:
        z_copy(peer(k), b).start()
    zr[b] = zs[b]

    for k in order:
        row_copy(a, peer(k), b + 2, peer(k)).wait_send()
        meta_copy(peer(k), b).wait_send()
        obs_copy_to(peer(k), b).wait_send()

    @pl.when((first_two & up) | (last_two & down))
    def _():
        def go(t, c):
            row_copy(a, t, b + 2, n_lon + t).wait_send()
            return c

        lax.fori_loop(0, n_lon, go, 0)

    for dy in (-1, 1):

        @pl.when(there[dy])
        def _():
            for k, (ky, _kx) in enumerate(HALO):
                if ky == dy:
                    halo_copy(k).wait_send()

    for k, (ky, _kx) in enumerate(HALO):
        if ky == 0:
            halo_copy(k).wait_send()

    for k in order:
        z_copy(peer(k), b).wait_send()
        z_copy(b, peer(k)).wait_recv()
    out_ref[...] = zr[...].reshape(n_col, W).astype(BF16)


def per_device(
    n_lat,
    n_lon,
    latents,
    in_proj,
    kernel_one,
    kernel_two,
    kernel_three,
    out_proj,
    bank,
    obs_values,
    obs_scale,
    owner_col,
    patch_id,
    bank_id,
):
    LR = n_lon
    MR = 2 * LR
    npts = 4 * LR * 4 * LW
    plen = bank.shape[1]
    nmid = (MR + 2 * GUARD) * MP
    n1 = LR + 2
    slots = n_lon * CAP
    vmem = pltpu.VMEM
    dma = pltpu.SemaphoreType.DMA
    nvar, nblk = obs_values.shape[1], obs_values.shape[0]
    scratch = [
        vmem(latents.shape, BF16),
        vmem(in_proj.shape, BF16),
        vmem(kernel_one.shape, BF16),
        vmem(kernel_two.shape, BF16),
        vmem(kernel_three.shape, BF16),
        vmem((nvar, W), BF16),
        vmem((1, nvar), F32),
        vmem((1, nblk), I32),
        vmem((1, nblk), I32),
        vmem((1, nblk), I32),
        vmem(bank.shape, BF16),
        vmem((obs_values.shape[0] * obs_values.shape[1], W), F32),
        vmem((n_lon * LW + 16, W), F32),
        vmem((n_lon, LP, W), BF16),
        vmem((LR + 4, LP, W), BF16),
        vmem((n_lon, 8, W), I32),
        pltpu.SMEM((8, W), I32),
        pltpu.SMEM((n_lon, 8, W), I32),
        vmem((CAP * VP, W), F32),
        vmem((n_lon, CAP * VP, W), BF16),
        vmem((n_lon, CAP * VP, W), BF16),
        vmem((2, 6 * W, 2 * W), BF16),
        vmem((2, 6 * W, 2 * W), BF16),
        vmem((12 * W, 2 * W), BF16),
        vmem((12 * W, 2 * W), BF16),
        vmem((16 * W, W), BF16),
        vmem((16 * W, W), BF16),
        vmem((VP, W), BF16),
        vmem((VP, W), F32),
        vmem((VP, W), F32),
        vmem((4, n1 * LP, W), F32),
        vmem((4, n1 * LP, W), F32),
        vmem((nmid, W), F32),
        vmem((nmid, W), F32),
        vmem((4, nmid, W), F32),
        vmem((4, nmid, W), F32),
        vmem((4, nmid, W), F32),
        vmem((4, nmid, W), F32),
        vmem((npts, W), F32),
        vmem((npts // plen, VP, plen), BF16),
        vmem((slots, VP, W), F32),
        vmem((slots + 1, VP, plen), F32),
        vmem((npts, W), F32),
        vmem((4, nmid, W), F32),
        vmem((4, nmid, W), F32),
        vmem((nmid, W), F32),
        vmem((nmid, W), F32),
        vmem((nmid, W), F32),
        vmem((4, n1 * LP, W), F32),
        vmem((n1 * LP, W), F32),
        vmem((n_lon, LW, W), F32),
        vmem((n_lon, LW, W), F32),
        vmem((4, 16, W), F32),
        vmem((2, 4 * 2 * 2 * LW, W), BF16),
        vmem((2, 4 * 2 * 2 * LW, W), BF16),
        vmem((2, 4 * 2 * MR, W), BF16),
        vmem((2, 4 * 2 * MR, W), BF16),
        vmem((4, 16, W), BF16),
        vmem((4, 16, W), BF16),
        dma((12 + 2 * PARTS,)),
        dma((2 * n_lon,)),
        dma((LR + 4,)),
        dma((n_lon,)),
        dma((n_lon,)),
        dma((n_lon,)),
        dma((n_lon,)),
        dma((8,)),
        dma((8,)),
        dma((n_lon,)),
        dma((n_lon,)),
    ]
    here = pl.BlockSpec(memory_space=pltpu.VMEM)
    far = pl.BlockSpec(memory_space=pl.ANY)
    back_zero = pl.pallas_call(
        functools.partial(kernel, n_lat, n_lon),
        out_shape=pltpu.VMEM((latents.shape[0], W), BF16),
        in_specs=[far] * 12,
        out_specs=here,
        scratch_shapes=scratch,
        compiler_params=pltpu.CompilerParams(
            collective_id=0, has_side_effects=True, vmem_limit_bytes=56 * 1024 * 1024
        ),
        cost_estimate=pl.CostEstimate(
            flops=5_000_000_000, bytes_accessed=4_000_000, transcendentals=1_000_000
        ),
    )(
        latents,
        in_proj,
        kernel_one,
        kernel_two,
        kernel_three,
        out_proj.T,
        bank,
        jnp.transpose(obs_values, (1, 0, 2)).reshape(nvar * nblk, W),
        obs_scale.reshape(1, -1),
        owner_col.reshape(1, -1),
        patch_id.reshape(1, -1),
        bank_id.reshape(1, -1),
    )
    return dot_nt(back_zero, in_proj)


def solution(mesh):
    n_lat, n_lon = mesh.shape["lat"], mesh.shape["lon"]
    placed = (
        P(("lat", "lon"), None),
        P(),
        P(),
        P(),
        P(),
        P(),
        P(),
        P(("lat", "lon"), None, None),
        P(),
        P(("lat", "lon"), None),
        P(("lat", "lon")),
        P(("lat", "lon")),
    )
    return jax.shard_map(
        functools.partial(per_device, n_lat, n_lon),
        mesh=mesh,
        in_specs=placed,
        out_specs=P(("lat", "lon"), None),
        check_vma=False,
    )
```

```python
import functools

import jax
import jax.numpy as jnp
from jax import lax
from jax.experimental import pallas as pl
from jax.experimental.pallas import tpu as pltpu
from jax.sharding import PartitionSpec as P

F32 = jnp.float32
BF16 = jnp.bfloat16
I32 = jnp.int32
MESH = pl.DeviceIdType.MESH
CAP = 4
LW = 8
W = 128
VP = 72
MP = 24
LP = 16
S_TWO, S_HEAD, S_B3, S_B2 = 2, 1, 1, 1
PARTS = 4
GUARD = 3
HALO = [(-1, -1), (-1, 0), (-1, 1), (0, -1), (0, 1), (1, -1), (1, 0), (1, 1)]


def dot(x, y):
    return jnp.dot(x, y, preferred_element_type=F32)


def dot_nt(x, y):
    return lax.dot_general(x, y, (((1,), (1,)), ((), ())), preferred_element_type=F32)


def shifted(x, by):
    return x if by == 0 else pltpu.roll(x, (-by) % x.shape[0], 0)


def logistic(x):
    return 0.5 * jnp.tanh(0.5 * x) + 0.5


def rounded(x):
    return x.astype(BF16).astype(F32)


TAPS = [(1, -1), (0, 0), (1, 0), (0, 1)]


def window(src, first, count, pitch):
    planes = []
    for p, dr in TAPS:
        line = []
        for q, dc in TAPS:
            at = pl.multiple_of((first + dr) * pitch, 8)
            line.append(shifted(src[2 * q + p, pl.ds(at, count * pitch), :], dc).astype(BF16))
        planes.append(line)
    return planes


def up_weights(k_ref, out_ref):
    rows = {(0, 0): [0], (0, 1): [1, 2], (0, 2): [], (1, 0): [], (1, 1): [0, 1], (1, 2): [2]}
    cols = {(0, 0): [0], (0, 1): [1, 2], (1, 0): [0, 1], (1, 1): [2]}
    for q in range(2):
        for rr in range(3):
            for cc in range(2):
                for p in range(2):
                    block = jnp.zeros((W, W), F32)
                    for i in rows[p, rr]:
                        for j in cols[q, cc]:
                            block = block + k_ref[i, j].astype(F32)
                    at = (rr * 2 + cc) * W
                    out_ref[q, at : at + W, p * W : (p + 1) * W] = block.astype(BF16)


def pair_weights(k_ref, out_ref, flip):
    for m in range(4):
        for j in range(3):
            at = (m * 3 + j) * W
            for p in range(2):
                i = m - p
                if 0 <= i <= 2:
                    block = k_ref[2 - i, 2 - j].astype(F32).T if flip else k_ref[i, j].astype(F32)
                else:
                    block = jnp.zeros((W, W), F32)
                out_ref[at : at + W, p * W : (p + 1) * W] = block.astype(BF16)


def down_weights(k_ref, out_ref):
    for m in range(4):
        for n in range(4):
            block = jnp.zeros((W, W), F32)
            for i in (m - 1, m):
                for j in (n - 1, n):
                    if 0 <= i <= 2 and 0 <= j <= 2:
                        block = block + k_ref[2 - i, 2 - j].astype(F32)
            at = (m * 4 + n) * W
            out_ref[at : at + W, :] = block.T.astype(BF16)


def kernel(
    n_lat,
    n_lon,
    lat_hbm,
    inp_hbm,
    k1_hbm,
    k2_hbm,
    k3_hbm,
    outp_hbm,
    bank_hbm,
    obs_hbm,
    scale_hbm,
    owner_hbm,
    patch_hbm,
    bankid_hbm,
    out_ref,
    lat_ref,
    inp_ref,
    k1_ref,
    k2_ref,
    k3_ref,
    outp_ref,
    scale_ref,
    owner_ref,
    patch_ref,
    bankid_ref,
    bank,
    obs,
    row_x,
    sbuf,
    srecv,
    meta_v,
    idx_s,
    meta_s,
    tmp,
    sv,
    rv,
    wu1,
    wu2,
    w3,
    b3,
    wd1,
    wd2,
    opt,
    opad,
    w2,
    f1s,
    d1s,
    f1,
    sl1,
    f2,
    sl2,
    act2,
    sl3,
    actp,
    ft,
    pred,
    hist,
    ga,
    a3,
    a2,
    ds2,
    b1,
    m1,
    a1,
    zbuf,
    zs,
    zr,
    ctmp,
    ns_s,
    ns_r,
    ew_s,
    ew_r,
    co_s,
    co_r,
    dma_sem,
    st_send,
    st_recv,
    me_send,
    me_recv,
    ob_send,
    ob_recv,
    ha_send,
    ha_recv,
    z_send,
    z_recv,
):
    a, b = lax.axis_index("lat"), lax.axis_index("lon")
    LR = n_lon
    MR = 2 * LR
    npatch = (4 * LR * 4 * LW) // bank.shape[1]
    plen = bank.shape[1]
    C_TWO, C_B3, C_B2 = (MR + 4) // S_TWO, (MR + 4) // S_B3, (MR + 4) // S_B2
    C_HEAD = MR // S_HEAD
    nblk = patch_ref.shape[1]
    nvar = outp_ref.shape[0]
    up, down = a > 0, a < n_lat - 1
    upi, downi = jnp.where(up, 1, 0), jnp.where(down, 1, 0)
    first_two, last_two = b < 2, b >= n_lon - 2

    flips = [bit * (1 - 2 * lax.rem(b // bit, 2)) for bit in (1, 2, 4, 8) if bit < n_lon]
    groups = n_lon // 4
    order = range(n_lon - 1, 0, -1)

    def peer(k):
        return b + sum(flip for i, flip in enumerate(flips) if k >> i & 1)

    def turn(g, k):
        return 2 * g + 1 + k // 2 + (k % 2) * (n_lon // 2)

    def after(t):
        return b + t - jnp.where(b + t >= n_lon, n_lon, 0)

    def before_me(t):
        return b - t + jnp.where(b < t, n_lon, 0)

    for row in (0, 1, LR + 2, LR + 3):
        srecv[row] = jnp.zeros((LP, W), BF16)

    barrier = pltpu.get_barrier_semaphore()

    def greet(i, j):
        pl.semaphore_signal(barrier, inc=1, device_id=(i, j), device_id_type=MESH)

    for k in order:
        greet(a, peer(k))

    @pl.when(up)
    def _():
        greet(a - 1, n_lon - 2)
        greet(a - 1, n_lon - 1)
        for d in range(3):
            greet(a - 1, lax.rem(b + n_lon - 1 + d, n_lon))

    @pl.when(down)
    def _():
        greet(a + 1, 0)
        greet(a + 1, 1)
        for d in range(3):
            greet(a + 1, lax.rem(b + n_lon - 1 + d, n_lon))

    def local(src, dst, sem):
        copy = pltpu.make_async_copy(src, dst, dma_sem.at[sem])
        copy.start()
        return copy

    row_parts = [local(lat_hbm, lat_ref, 2), local(inp_hbm, inp_ref, 3)]
    id_parts = [
        local(owner_hbm, owner_ref, 4),
        local(patch_hbm, patch_ref, 5),
        local(bankid_hbm, bankid_ref, 6),
    ]
    obs_rows = obs.shape[0] // PARTS
    bank_rows = bank.shape[0] // PARTS
    cuts = [pl.ds(i * obs_rows, obs_rows) for i in range(PARTS)]
    obs_parts = [local(obs_hbm.at[c], obs.at[c], 12 + i) for i, c in enumerate(cuts)]
    weight_parts = [
        local(k1_hbm, k1_ref, 7),
        local(k2_hbm, k2_ref, 8),
        local(k3_hbm, k3_ref, 9),
        local(outp_hbm, outp_ref, 10),
        local(scale_hbm, scale_ref, 11),
    ]
    cuts = [pl.ds(i * bank_rows, bank_rows) for i in range(PARTS)]
    bank_parts = [local(bank_hbm.at[c], bank.at[c], 12 + PARTS + i) for i, c in enumerate(cuts)]

    for part in row_parts:
        part.wait()
    feat = rounded(dot(lat_ref[...], inp_ref[...]))
    n_col = n_lon * LW
    row_x[0:8] = feat[n_col - 8 :]
    row_x[8 : 8 + n_col] = feat
    row_x[8 + n_col : 16 + n_col] = feat[0:8]
    for t in range(n_lon):
        sbuf[t] = row_x[8 * t + 4 : 8 * t + 20].astype(BF16)

    for part in id_parts:
        part.wait()
    lane = lax.broadcasted_iota(I32, (nblk, W), 1)
    sub = lax.broadcasted_iota(I32, (nblk, W), 0)
    eye = lane == sub

    def column(row_ref):
        row = jnp.broadcast_to(row_ref[...], (nblk, nblk))
        return jnp.sum(jnp.where(eye[:, :nblk], row, 0), axis=1, keepdims=True)

    own_c = jnp.broadcast_to(column(owner_ref), (nblk, W))
    own_r = jnp.sum(jnp.where(eye, own_c, 0), axis=0, keepdims=True)
    earlier = jnp.where((own_c == own_r) & (lane < sub), 1, 0)
    rank = jnp.sum(earlier, axis=1, keepdims=True)
    slot = own_c * CAP + rank
    pick = lane == slot

    def per_slot(value):
        return jnp.sum(jnp.where(pick, value, 0), axis=0, keepdims=True)

    rows8 = lax.broadcasted_iota(I32, (8, W), 0)
    meta = jnp.where(rows8 == 0, per_slot(sub), 0)
    meta = jnp.where(rows8 == 1, per_slot(jnp.broadcast_to(column(patch_ref), (nblk, W))), meta)
    meta = jnp.where(rows8 == 2, per_slot(jnp.broadcast_to(column(bankid_ref), (nblk, W))), meta)
    meta = jnp.where(rows8 == 3, per_slot(jnp.ones_like(sub)), meta)
    meta_v[b] = meta
    idx_copy = pltpu.make_async_copy(meta_v.at[b], idx_s, dma_sem.at[0])
    idx_copy.start()

    expected = (
        n_lon - 1
        + jnp.where(first_two & up, n_lon, 0)
        + jnp.where(last_two & down, n_lon, 0)
        + 3 * upi
        + 3 * downi
    )
    pl.semaphore_wait(barrier, expected)

    def row_copy(i, t, at, sem):
        return pltpu.make_async_remote_copy(
            src_ref=sbuf.at[t],
            dst_ref=srecv.at[at],
            send_sem=st_send.at[sem],
            recv_sem=st_recv.at[at],
            device_id=(i, t),
            device_id_type=MESH,
        )

    for k in order:
        row_copy(a, peer(k), b + 2, peer(k)).start()

    @pl.when(first_two & up)
    def _():
        def go(t, c):
            row_copy(a - 1, t, LR + 2 + b, n_lon + t).start()
            return c

        lax.fori_loop(0, n_lon, go, 0)

    @pl.when(last_two & down)
    def _():
        def go(t, c):
            row_copy(a + 1, t, b - (n_lon - 2), n_lon + t).start()
            return c

        lax.fori_loop(0, n_lon, go, 0)

    srecv[b + 2] = sbuf[b]

    def meta_copy(t, slot_at):
        return pltpu.make_async_remote_copy(
            src_ref=meta_v.at[b],
            dst_ref=meta_v.at[slot_at],
            send_sem=me_send.at[t],
            recv_sem=me_recv.at[slot_at],
            device_id=(a, t),
            device_id_type=MESH,
        )

    for k in order:
        meta_copy(peer(k), b).start()

    def obs_copy_to(t, slot_at):
        return pltpu.make_async_remote_copy(
            src_ref=sv.at[t],
            dst_ref=rv.at[slot_at],
            send_sem=ob_send.at[t],
            recv_sem=ob_recv.at[slot_at],
            device_id=(a, t),
            device_id_type=MESH,
        )

    tmp[...] = jnp.zeros_like(tmp)
    for part in obs_parts:
        part.wait()
    idx_copy.wait()

    def gathered(t):
        for k in range(CAP):
            block = pl.ds(idx_s[0, t * CAP + k], nvar, stride=nblk)
            tmp[pl.ds(k * VP, nvar), :] = obs[block, :]
        return tmp[...].astype(BF16)

    def send_obs(g, c):
        for k in range(4):
            t = after(turn(g, k))
            if k < 3:
                sv[t] = gathered(t)
                obs_copy_to(t, b).start()
            else:

                @pl.when(g < groups - 1)
                def _():
                    sv[t] = gathered(t)
                    obs_copy_to(t, b).start()

        return c

    lax.fori_loop(0, groups, send_obs, 0)
    rv[b] = gathered(b)

    for part in weight_parts:
        part.wait()
    up_weights(k1_ref, wu1)
    up_weights(k2_ref, wu2)
    pair_weights(k3_ref, w3, False)
    pair_weights(k3_ref, b3, True)
    down_weights(k2_ref, wd2)
    down_weights(k1_ref, wd1)
    opad[...] = jnp.zeros_like(opad)
    opad[0:nvar] = outp_ref[...].astype(F32)
    opt[...] = opad[...].astype(BF16)
    vlane = lax.broadcasted_iota(I32, (VP, nvar), 1)
    vsub = lax.broadcasted_iota(I32, (VP, nvar), 0)
    scale = jnp.broadcast_to(scale_ref[...], (VP, nvar))
    scale = jnp.sum(jnp.where(vlane == vsub, scale, 0.0), axis=1, keepdims=True)
    w2[...] = jnp.broadcast_to(scale * scale, (VP, W))
    for ref in (f1, sl1, m1, b1):
        ref[...] = jnp.zeros_like(ref)
    for ref in (a3, a2):
        ref[...] = jnp.zeros_like(ref)

    for k in order:
        row_copy(a, b, peer(k) + 2, 0).wait_recv()

    @pl.when(up)
    def _():
        row_copy(a, b, 0, 0).wait_recv()
        row_copy(a, b, 1, 0).wait_recv()

    @pl.when(down)
    def _():
        row_copy(a, b, LR + 2, 0).wait_recv()
        row_copy(a, b, LR + 3, 0).wait_recv()

    def inside(first, count, pitch, size):
        row = lax.broadcasted_iota(I32, (count, pitch, W), 0) + first
        low = jnp.where(up, -8, 0)
        high = jnp.where(down, size + 8, size)
        return jnp.where((row >= low) & (row < high), 1.0, 0.0).reshape(count * pitch, W)

    def lifted(line, weights):
        left = [shifted(x, -1).astype(BF16) for x in line]
        here = [x.astype(BF16) for x in line]
        right = [shifted(x, 1).astype(BF16) for x in line]
        phases = []
        for q, (u, v) in enumerate(((left, here), (here, right))):
            x = jnp.concatenate([u[0], v[0], u[1], v[1], u[2], v[2]], axis=1)
            y = dot(x, weights[q])
            phases += [y[:, :W], y[:, W:]]
        return phases

    n1 = LR + 2
    line = [srecv[pl.ds(i, n1)].astype(F32).reshape(n1 * LP, W) for i in range(3)]
    mask = inside(-1, n1, LP, LR)
    for ph, pre in enumerate(lifted(line, wu1)):
        s = logistic(pre)
        f1s[ph] = mask * rounded(pre * s + line[1])
        d1s[ph] = mask * (s * (1.0 + pre * (1.0 - s)))

    def spread(i, c):
        for q in range(2):
            for p in range(2):
                to = pl.ds((2 * i + p + 1) * MP + q, 10, stride=2)
                frm = pl.ds(i * LP + 3, 10)
                f1[to, :] = f1s[2 * q + p, frm, :]
                sl1[to, :] = d1s[2 * q + p, frm, :]
        return c

    lax.fori_loop(0, n1, spread, 0, unroll=3)

    for k in order:
        meta_copy(b, peer(k)).wait_recv()
    meta_down = pltpu.make_async_copy(meta_v, meta_s, dma_sem.at[1])
    meta_down.start()

    def level_two(i, c):
        first = i * C_TWO + GUARD - 2
        line = [f1[pl.ds(pl.multiple_of((first + d) * MP, 8), C_TWO * MP), :] for d in (-1, 0, 1)]
        mask = inside(first - GUARD, C_TWO, MP, MR)
        at = pl.ds(pl.multiple_of(first * MP, 8), C_TWO * MP)
        for ph, pre in enumerate(lifted(line, wu2)):
            s = logistic(pre)
            f2[ph, at, :] = mask * (pre * s + line[1])
            sl2[ph, at, :] = mask * (s * (1.0 + pre * (1.0 - s)))
        return c

    lax.fori_loop(0, (MR + 4) // C_TWO, level_two, 0)

    def paired(planes, weights, q):
        x = jnp.concatenate([planes[m][q + j] for m in range(4) for j in range(3)], axis=1)
        return dot(x, weights[...])

    def head(i, c):
        first = i * C_HEAD + GUARD
        planes = window(f2, first, C_HEAD, MP)
        at = pl.ds(pl.multiple_of(first * MP, 8), C_HEAD * MP)
        for q in range(2):
            y = paired(planes, w3, q)
            for p in range(2):
                pre = y[:, p * W : (p + 1) * W]
                s = logistic(pre)
                act2[2 * q + p, at, :] = pre * s
                sl3[2 * q + p, at, :] = s * (1.0 + pre * (1.0 - s))
        return c

    lax.fori_loop(0, MR // C_HEAD, head, 0)

    def points(r, c):
        for q in range(2):
            for p in range(2):
                to = pl.ds((2 * r + p) * (4 * LW) + q, 2 * LW, stride=2)
                actp[to, :] = act2[2 * q + p, pl.ds((r + GUARD) * MP + 2, 2 * LW), :]
        return c

    lax.fori_loop(0, MR, points, 0, unroll=4)
    for n in range(npatch):
        ft[n] = dot_nt(opt[...], actp[n * plen : (n + 1) * plen].astype(BF16)).astype(BF16)

    for part in bank_parts:
        part.wait()
    meta_down.wait()
    none = n_lon * CAP
    hist[none] = jnp.zeros((VP, plen), F32)

    def predict(g, c):
        for m in range(4):
            source = before_me(turn(g, m))
            for k in range(CAP):
                rows = bank[meta_s[source, 2, b * CAP + k]]
                slot_at = (g * 4 + m) * CAP + k
                pred[slot_at] = dot(ft[meta_s[source, 1, b * CAP + k]], rows)
        return c

    lax.fori_loop(0, groups, predict, 0)

    def blocks(g, last):
        for m in range(4):
            source = before_me(turn(g, m))
            if m < 3:
                obs_copy_to(b, source).wait_recv()
            else:

                @pl.when(g < groups - 1)
                def _():
                    obs_copy_to(b, source).wait_recv()

            values = rv[source].astype(F32)
            grads = []
            for k in range(CAP):
                rows = bank[meta_s[source, 2, b * CAP + k]]
                live = meta_s[source, 3, b * CAP + k].astype(F32)
                miss = pred[(g * 4 + m) * CAP + k] - values[k * VP : (k + 1) * VP]
                grads.append(dot_nt(((w2[...] * live) * miss).astype(BF16), rows))
            for k in range(CAP):
                patch = meta_s[source, 1, b * CAP + k]
                slot_at = (g * 4 + m) * CAP + k
                before = last[0]
                for n in range(1, npatch):
                    before = jnp.where(patch == n, last[n], before)
                hist[slot_at] = grads[k] + hist[before]
                last = tuple(jnp.where(patch == n, slot_at, last[n]) for n in range(npatch))
        return last

    last = lax.fori_loop(0, groups, blocks, (jnp.int32(none),) * npatch)

    for n in range(npatch):
        grad = hist[last[n]].astype(BF16)
        ga[n * plen : (n + 1) * plen] = lax.dot_general(
            grad, opt[...], (((0,), (0,)), ((), ())), preferred_element_type=F32
        )

    def adjoint_three(r, c):
        at = pl.ds((r + GUARD) * MP + 2, 2 * LW)
        for q in range(2):
            for p in range(2):
                grad = ga[pl.ds((2 * r + p) * (4 * LW) + q, 2 * LW, stride=2), :]
                a3[2 * q + p, at, :] = grad * sl3[2 * q + p, at, :]
        return c

    lax.fori_loop(0, MR, adjoint_three, 0, unroll=4)

    edge_rows = (0, MR - 2)
    edge_cols = (0, 2 * LW - 2)
    for side in range(2):
        for ph in range(4):
            for i in range(2):
                at = (edge_rows[side] + i + GUARD) * MP + 2
                to = (ph * 2 + i) * 2 * LW
                ns_s[side, to : to + 2 * LW] = a3[ph, at : at + 2 * LW, :].astype(BF16)
                at = GUARD * MP + 2 + edge_cols[side] + i
                to = (ph * 2 + i) * MR
                ew_s[side, to : to + MR] = a3[ph, pl.ds(at, MR, stride=MP), :].astype(BF16)
    for v in range(2):
        for h in range(2):
            for ph in range(4):
                for i in range(2):
                    at = (edge_rows[v] + i + GUARD) * MP + 2 + edge_cols[h]
                    ctmp[v * 2 + h, ph * 4 + i * 2 : ph * 4 + i * 2 + 2] = a3[ph, at : at + 2, :]
            co_s[v * 2 + h] = ctmp[v * 2 + h].astype(BF16)

    def halo_copy(k):
        dy, dx = HALO[k]
        v, h = (dy + 1) // 2, (dx + 1) // 2
        if dy == 0:
            src, dst = ew_s.at[h], ew_r.at[1 - h]
        elif dx == 0:
            src, dst = ns_s.at[v], ns_r.at[1 - v]
        else:
            src, dst = co_s.at[v * 2 + h], co_r.at[(1 - v) * 2 + 1 - h]
        return pltpu.make_async_remote_copy(
            src_ref=src,
            dst_ref=dst,
            send_sem=ha_send.at[k],
            recv_sem=ha_recv.at[7 - k],
            device_id=(a + dy, lax.rem(b + n_lon + dx, n_lon)),
            device_id_type=MESH,
        )

    def halo_arrived(k):
        dy, dx = HALO[k]
        v, h = (dy + 1) // 2, (dx + 1) // 2
        if dy == 0:
            ref = ew_r.at[h]
        elif dx == 0:
            ref = ns_r.at[v]
        else:
            ref = co_r.at[v * 2 + h]
        pltpu.make_async_remote_copy(
            src_ref=ref,
            dst_ref=ref,
            send_sem=ha_send.at[k],
            recv_sem=ha_recv.at[k],
            device_id=(a, b),
            device_id_type=MESH,
        ).wait_recv()

    there = {-1: up, 1: down}
    for dy in (-1, 1):

        @pl.when(there[dy])
        def _():
            for k, (ky, _kx) in enumerate(HALO):
                if ky == dy:
                    halo_copy(k).start()

    for k, (ky, _kx) in enumerate(HALO):
        if ky == 0:
            halo_copy(k).start()

    halo_rows = (-2, MR)
    halo_cols = (0, 2 * LW + 2)
    for dy in (-1, 1):

        @pl.when(there[dy])
        def _():
            v = (dy + 1) // 2
            for k, (ky, _kx) in enumerate(HALO):
                if ky == dy:
                    halo_arrived(k)
            for ph in range(4):
                for i in range(2):
                    at = (halo_rows[v] + i + GUARD) * MP + 2
                    frm = (ph * 2 + i) * 2 * LW
                    a3[ph, at : at + 2 * LW, :] = ns_r[v, frm : frm + 2 * LW].astype(F32)
            for h in range(2):
                ctmp[v * 2 + h] = co_r[v * 2 + h].astype(F32)
                for ph in range(4):
                    for i in range(2):
                        at = (halo_rows[v] + i + GUARD) * MP + halo_cols[h]
                        a3[ph, at : at + 2, :] = ctmp[
                            v * 2 + h, ph * 4 + i * 2 : ph * 4 + i * 2 + 2
                        ]

    for k, (ky, kx) in enumerate(HALO):
        if ky == 0:
            h = (kx + 1) // 2
            halo_arrived(k)
            for ph in range(4):
                for i in range(2):
                    frm = (ph * 2 + i) * MR
                    at = GUARD * MP + halo_cols[h] + i
                    a3[ph, pl.ds(at, MR, stride=MP), :] = ew_r[h, frm : frm + MR].astype(F32)

    def back_three(i, c):
        first = i * C_B3 + GUARD - 2
        planes = window(a3, first, C_B3, MP)
        at = pl.ds(pl.multiple_of(first * MP, 8), C_B3 * MP)
        total = jnp.zeros((C_B3 * MP, W), F32)
        for q in range(2):
            y = paired(planes, b3, q)
            for p in range(2):
                back = y[:, p * W : (p + 1) * W]
                a2[2 * q + p, at, :] = back * sl2[2 * q + p, at, :]
                total = total + back
        ds2[at, :] = total
        return c

    lax.fori_loop(0, (MR + 4) // C_B3, back_three, 0)

    def gathered_down(planes, weights):
        x = jnp.concatenate([planes[m][n] for m in range(4) for n in range(4)], axis=1)
        return dot(x, weights[...])

    def back_two(i, c):
        first = i * C_B2 + GUARD - 2
        at = pl.ds(pl.multiple_of(first * MP, 8), C_B2 * MP)
        back = ds2[at, :] + gathered_down(window(a2, first, C_B2, MP), wd2)
        b1[at, :] = back
        m1[at, :] = back * sl1[at, :]
        return c

    lax.fori_loop(0, (MR + 4) // C_B2, back_two, 0)

    def gather(i, c):
        total = jnp.zeros((LP, W), F32)
        for q in range(2):
            for p in range(2):
                frm = pl.ds((2 * i + p + 1) * MP + q, LP, stride=2)
                a1[2 * q + p, pl.ds(pl.multiple_of(i * LP, 8), LP), :] = m1[frm, :]
                total = total + b1[frm, :]
        zbuf[pl.ds(pl.multiple_of(i * LP, 8), LP), :] = total
        return c

    lax.fori_loop(0, n1, gather, 0, unroll=3)
    back = zbuf[LP : LP + LR * LP] + gathered_down(window(a1, 1, LR, LP), wd1)
    zbuf[LP : LP + LR * LP] = rounded(back)
    for r in range(LR):
        zs[r] = zbuf[(r + 1) * LP + 1 : (r + 1) * LP + 1 + LW]

    def z_copy(t, slot_at):
        return pltpu.make_async_remote_copy(
            src_ref=zs.at[t],
            dst_ref=zr.at[slot_at],
            send_sem=z_send.at[t],
            recv_sem=z_recv.at[slot_at],
            device_id=(a, t),
            device_id_type=MESH,
        )

    for k in order:
        z_copy(peer(k), b).start()
    zr[b] = zs[b]

    for k in order:
        row_copy(a, peer(k), b + 2, peer(k)).wait_send()
        meta_copy(peer(k), b).wait_send()
        obs_copy_to(peer(k), b).wait_send()

    @pl.when((first_two & up) | (last_two & down))
    def _():
        def go(t, c):
            row_copy(a, t, b + 2, n_lon + t).wait_send()
            return c

        lax.fori_loop(0, n_lon, go, 0)

    for dy in (-1, 1):

        @pl.when(there[dy])
        def _():
            for k, (ky, _kx) in enumerate(HALO):
                if ky == dy:
                    halo_copy(k).wait_send()

    for k, (ky, _kx) in enumerate(HALO):
        if ky == 0:
            halo_copy(k).wait_send()

    for k in order:
        z_copy(peer(k), b).wait_send()
        z_copy(b, peer(k)).wait_recv()
    out_ref[...] = zr[...].reshape(n_col, W).astype(BF16)


def per_device(
    n_lat,
    n_lon,
    latents,
    in_proj,
    kernel_one,
    kernel_two,
    kernel_three,
    out_proj,
    bank,
    obs_values,
    obs_scale,
    owner_col,
    patch_id,
    bank_id,
):
    LR = n_lon
    MR = 2 * LR
    npts = 4 * LR * 4 * LW
    plen = bank.shape[1]
    nmid = (MR + 2 * GUARD) * MP
    n1 = LR + 2
    slots = n_lon * CAP
    vmem = pltpu.VMEM
    dma = pltpu.SemaphoreType.DMA
    nvar, nblk = obs_values.shape[1], obs_values.shape[0]
    scratch = [
        vmem(latents.shape, BF16),
        vmem(in_proj.shape, BF16),
        vmem(kernel_one.shape, BF16),
        vmem(kernel_two.shape, BF16),
        vmem(kernel_three.shape, BF16),
        vmem((nvar, W), BF16),
        vmem((1, nvar), F32),
        vmem((1, nblk), I32),
        vmem((1, nblk), I32),
        vmem((1, nblk), I32),
        vmem(bank.shape, BF16),
        vmem((obs_values.shape[0] * obs_values.shape[1], W), F32),
        vmem((n_lon * LW + 16, W), F32),
        vmem((n_lon, LP, W), BF16),
        vmem((LR + 4, LP, W), BF16),
        vmem((n_lon, 8, W), I32),
        pltpu.SMEM((8, W), I32),
        pltpu.SMEM((n_lon, 8, W), I32),
        vmem((CAP * VP, W), F32),
        vmem((n_lon, CAP * VP, W), BF16),
        vmem((n_lon, CAP * VP, W), BF16),
        vmem((2, 6 * W, 2 * W), BF16),
        vmem((2, 6 * W, 2 * W), BF16),
        vmem((12 * W, 2 * W), BF16),
        vmem((12 * W, 2 * W), BF16),
        vmem((16 * W, W), BF16),
        vmem((16 * W, W), BF16),
        vmem((VP, W), BF16),
        vmem((VP, W), F32),
        vmem((VP, W), F32),
        vmem((4, n1 * LP, W), F32),
        vmem((4, n1 * LP, W), F32),
        vmem((nmid, W), F32),
        vmem((nmid, W), F32),
        vmem((4, nmid, W), F32),
        vmem((4, nmid, W), F32),
        vmem((4, nmid, W), F32),
        vmem((4, nmid, W), F32),
        vmem((npts, W), F32),
        vmem((npts // plen, VP, plen), BF16),
        vmem((slots, VP, W), F32),
        vmem((slots + 1, VP, plen), F32),
        vmem((npts, W), F32),
        vmem((4, nmid, W), F32),
        vmem((4, nmid, W), F32),
        vmem((nmid, W), F32),
        vmem((nmid, W), F32),
        vmem((nmid, W), F32),
        vmem((4, n1 * LP, W), F32),
        vmem((n1 * LP, W), F32),
        vmem((n_lon, LW, W), F32),
        vmem((n_lon, LW, W), F32),
        vmem((4, 16, W), F32),
        vmem((2, 4 * 2 * 2 * LW, W), BF16),
        vmem((2, 4 * 2 * 2 * LW, W), BF16),
        vmem((2, 4 * 2 * MR, W), BF16),
        vmem((2, 4 * 2 * MR, W), BF16),
        vmem((4, 16, W), BF16),
        vmem((4, 16, W), BF16),
        dma((12 + 2 * PARTS,)),
        dma((2 * n_lon,)),
        dma((LR + 4,)),
        dma((n_lon,)),
        dma((n_lon,)),
        dma((n_lon,)),
        dma((n_lon,)),
        dma((8,)),
        dma((8,)),
        dma((n_lon,)),
        dma((n_lon,)),
    ]
    here = pl.BlockSpec(memory_space=pltpu.VMEM)
    far = pl.BlockSpec(memory_space=pl.ANY)
    back_zero = pl.pallas_call(
        functools.partial(kernel, n_lat, n_lon),
        out_shape=pltpu.VMEM((latents.shape[0], W), BF16),
        in_specs=[far] * 12,
        out_specs=here,
        scratch_shapes=scratch,
        compiler_params=pltpu.CompilerParams(
            collective_id=0, has_side_effects=True, vmem_limit_bytes=56 * 1024 * 1024
        ),
        cost_estimate=pl.CostEstimate(
            flops=5_000_000_000, bytes_accessed=4_000_000, transcendentals=1_000_000
        ),
    )(
        latents,
        in_proj,
        kernel_one,
        kernel_two,
        kernel_three,
        out_proj.T,
        bank,
        jnp.transpose(obs_values, (1, 0, 2)).reshape(nvar * nblk, W),
        obs_scale.reshape(1, -1),
        owner_col.reshape(1, -1),
        patch_id.reshape(1, -1),
        bank_id.reshape(1, -1),
    )
    return dot_nt(back_zero, in_proj)


def solution(mesh):
    n_lat, n_lon = mesh.shape["lat"], mesh.shape["lon"]
    placed = (
        P(("lat", "lon"), None),
        P(),
        P(),
        P(),
        P(),
        P(),
        P(),
        P(("lat", "lon"), None, None),
        P(),
        P(("lat", "lon"), None),
        P(("lat", "lon")),
        P(("lat", "lon")),
    )
    return jax.shard_map(
        functools.partial(per_device, n_lat, n_lon),
        mesh=mesh,
        in_specs=placed,
        out_specs=P(("lat", "lon"), None),
        check_vma=False,
    )
```

```python
import functools

import jax
import jax.numpy as jnp
from jax import lax
from jax.experimental import pallas as pl
from jax.experimental.pallas import tpu as pltpu
from jax.sharding import PartitionSpec as P

F32 = jnp.float32
BF16 = jnp.bfloat16
I32 = jnp.int32
MESH = pl.DeviceIdType.MESH
CAP = 4
LW = 8
W = 128
VP = 72
MP = 24
LP = 16
S_TWO, S_HEAD, S_B3 = 2, 1, 1
PARTS = 4
GUARD = 3
HALO = [(-1, -1), (-1, 0), (-1, 1), (0, -1), (0, 1), (1, -1), (1, 0), (1, 1)]


def dot(x, y):
    return jnp.dot(x, y, preferred_element_type=F32)


def dot_nt(x, y):
    return lax.dot_general(x, y, (((1,), (1,)), ((), ())), preferred_element_type=F32)


def shifted(x, by):
    return x if by == 0 else pltpu.roll(x, (-by) % x.shape[0], 0)


def logistic(x):
    return 0.5 * jnp.tanh(0.5 * x) + 0.5


def rounded(x):
    return x.astype(BF16).astype(F32)


TAPS = [(1, -1), (0, 0), (1, 0), (0, 1)]


def window(src, first, count, pitch):
    planes = []
    for p, dr in TAPS:
        line = []
        for q, dc in TAPS:
            at = pl.multiple_of((first + dr) * pitch, 8)
            line.append(shifted(src[2 * q + p, pl.ds(at, count * pitch), :], dc).astype(BF16))
        planes.append(line)
    return planes


def up_weights(k_ref, out_ref):
    rows = {(0, 0): [0], (0, 1): [1, 2], (0, 2): [], (1, 0): [], (1, 1): [0, 1], (1, 2): [2]}
    cols = {(0, 0): [0], (0, 1): [1, 2], (1, 0): [0, 1], (1, 1): [2]}
    for q in range(2):
        for rr in range(3):
            for cc in range(2):
                for p in range(2):
                    block = jnp.zeros((W, W), F32)
                    for i in rows[p, rr]:
                        for j in cols[q, cc]:
                            block = block + k_ref[i, j].astype(F32)
                    at = (rr * 2 + cc) * W
                    out_ref[q, at : at + W, p * W : (p + 1) * W] = block.astype(BF16)


def pair_weights(k_ref, out_ref, flip):
    for m in range(4):
        for j in range(3):
            at = (m * 3 + j) * W
            for p in range(2):
                i = m - p
                if 0 <= i <= 2:
                    block = k_ref[2 - i, 2 - j].astype(F32).T if flip else k_ref[i, j].astype(F32)
                else:
                    block = jnp.zeros((W, W), F32)
                out_ref[at : at + W, p * W : (p + 1) * W] = block.astype(BF16)


def down_weights(k_ref, out_ref):
    for m in range(4):
        for n in range(4):
            block = jnp.zeros((W, W), F32)
            for i in (m - 1, m):
                for j in (n - 1, n):
                    if 0 <= i <= 2 and 0 <= j <= 2:
                        block = block + k_ref[2 - i, 2 - j].astype(F32)
            p, near = 1 - m % 2, m in (1, 2)
            to = 0 if near else W
            out_ref[p, n * W : (n + 1) * W, to : to + W] = block.T.astype(BF16)


def kernel(
    n_lat,
    n_lon,
    lat_hbm,
    inp_hbm,
    k1_hbm,
    k2_hbm,
    k3_hbm,
    outp_hbm,
    bank_hbm,
    obs_hbm,
    scale_hbm,
    owner_hbm,
    patch_hbm,
    bankid_hbm,
    out_ref,
    lat_ref,
    inp_ref,
    k1_ref,
    k2_ref,
    k3_ref,
    outp_ref,
    scale_ref,
    owner_ref,
    patch_ref,
    bankid_ref,
    bank,
    obs,
    row_x,
    sbuf,
    srecv,
    meta_v,
    idx_s,
    meta_s,
    tmp,
    sv,
    rv,
    wu1,
    wu2,
    w3,
    b3,
    wd1,
    wd2,
    opt,
    opad,
    w2,
    f1s,
    d1s,
    f1,
    sl1,
    f2,
    sl2,
    act2,
    sl3,
    actp,
    ft,
    pred,
    hist,
    ga,
    a3,
    a2,
    ds2,
    b1,
    m1,
    a1,
    zbuf,
    zs,
    zr,
    ctmp,
    ns_s,
    ns_r,
    ew_s,
    ew_r,
    co_s,
    co_r,
    dma_sem,
    st_send,
    st_recv,
    me_send,
    me_recv,
    ob_send,
    ob_recv,
    ha_send,
    ha_recv,
    z_send,
    z_recv,
):
    a, b = lax.axis_index("lat"), lax.axis_index("lon")
    LR = n_lon
    MR = 2 * LR
    npatch = (4 * LR * 4 * LW) // bank.shape[1]
    plen = bank.shape[1]
    C_TWO, C_B3 = (MR + 4) // S_TWO, (MR + 4) // S_B3
    C_HEAD = MR // S_HEAD
    nblk = patch_ref.shape[1]
    nvar = outp_ref.shape[0]
    up, down = a > 0, a < n_lat - 1
    upi, downi = jnp.where(up, 1, 0), jnp.where(down, 1, 0)
    first_two, last_two = b < 2, b >= n_lon - 2

    flips = [bit * (1 - 2 * lax.rem(b // bit, 2)) for bit in (1, 2, 4, 8) if bit < n_lon]
    groups = n_lon // 4
    order = range(n_lon - 1, 0, -1)

    def peer(k):
        return b + sum(flip for i, flip in enumerate(flips) if k >> i & 1)

    def turn(g, k):
        return 2 * g + 1 + k // 2 + (k % 2) * (n_lon // 2)

    def after(t):
        return b + t - jnp.where(b + t >= n_lon, n_lon, 0)

    def before_me(t):
        return b - t + jnp.where(b < t, n_lon, 0)

    for row in (0, 1, LR + 2, LR + 3):
        srecv[row] = jnp.zeros((LP, W), BF16)

    barrier = pltpu.get_barrier_semaphore()

    def greet(i, j):
        pl.semaphore_signal(barrier, inc=1, device_id=(i, j), device_id_type=MESH)

    for k in order:
        greet(a, peer(k))

    @pl.when(up)
    def _():
        greet(a - 1, n_lon - 2)
        greet(a - 1, n_lon - 1)
        for d in range(3):
            greet(a - 1, lax.rem(b + n_lon - 1 + d, n_lon))

    @pl.when(down)
    def _():
        greet(a + 1, 0)
        greet(a + 1, 1)
        for d in range(3):
            greet(a + 1, lax.rem(b + n_lon - 1 + d, n_lon))

    def local(src, dst, sem):
        copy = pltpu.make_async_copy(src, dst, dma_sem.at[sem])
        copy.start()
        return copy

    row_parts = [local(lat_hbm, lat_ref, 2), local(inp_hbm, inp_ref, 3)]
    id_parts = [
        local(owner_hbm, owner_ref, 4),
        local(patch_hbm, patch_ref, 5),
        local(bankid_hbm, bankid_ref, 6),
    ]
    obs_rows = obs.shape[0] // PARTS
    bank_rows = bank.shape[0] // PARTS
    cuts = [pl.ds(i * obs_rows, obs_rows) for i in range(PARTS)]
    obs_parts = [local(obs_hbm.at[c], obs.at[c], 12 + i) for i, c in enumerate(cuts)]
    weight_parts = [
        local(k1_hbm, k1_ref, 7),
        local(k2_hbm, k2_ref, 8),
        local(k3_hbm, k3_ref, 9),
        local(outp_hbm, outp_ref, 10),
        local(scale_hbm, scale_ref, 11),
    ]
    cuts = [pl.ds(i * bank_rows, bank_rows) for i in range(PARTS)]
    bank_parts = [local(bank_hbm.at[c], bank.at[c], 12 + PARTS + i) for i, c in enumerate(cuts)]

    for part in row_parts:
        part.wait()
    feat = rounded(dot(lat_ref[...], inp_ref[...]))
    n_col = n_lon * LW
    row_x[0:8] = feat[n_col - 8 :]
    row_x[8 : 8 + n_col] = feat
    row_x[8 + n_col : 16 + n_col] = feat[0:8]
    for t in range(n_lon):
        sbuf[t] = row_x[8 * t + 4 : 8 * t + 20].astype(BF16)

    for part in id_parts:
        part.wait()
    lane = lax.broadcasted_iota(I32, (nblk, W), 1)
    sub = lax.broadcasted_iota(I32, (nblk, W), 0)
    eye = lane == sub

    def column(row_ref):
        row = jnp.broadcast_to(row_ref[...], (nblk, nblk))
        return jnp.sum(jnp.where(eye[:, :nblk], row, 0), axis=1, keepdims=True)

    own_c = jnp.broadcast_to(column(owner_ref), (nblk, W))
    own_r = jnp.sum(jnp.where(eye, own_c, 0), axis=0, keepdims=True)
    earlier = jnp.where((own_c == own_r) & (lane < sub), 1, 0)
    rank = jnp.sum(earlier, axis=1, keepdims=True)
    slot = own_c * CAP + rank
    pick = lane == slot

    def per_slot(value):
        return jnp.sum(jnp.where(pick, value, 0), axis=0, keepdims=True)

    rows8 = lax.broadcasted_iota(I32, (8, W), 0)
    meta = jnp.where(rows8 == 0, per_slot(sub), 0)
    meta = jnp.where(rows8 == 1, per_slot(jnp.broadcast_to(column(patch_ref), (nblk, W))), meta)
    meta = jnp.where(rows8 == 2, per_slot(jnp.broadcast_to(column(bankid_ref), (nblk, W))), meta)
    meta = jnp.where(rows8 == 3, per_slot(jnp.ones_like(sub)), meta)
    meta_v[b] = meta
    idx_copy = pltpu.make_async_copy(meta_v.at[b], idx_s, dma_sem.at[0])
    idx_copy.start()

    expected = (
        n_lon - 1
        + jnp.where(first_two & up, n_lon, 0)
        + jnp.where(last_two & down, n_lon, 0)
        + 3 * upi
        + 3 * downi
    )
    pl.semaphore_wait(barrier, expected)

    def row_copy(i, t, at, sem):
        return pltpu.make_async_remote_copy(
            src_ref=sbuf.at[t],
            dst_ref=srecv.at[at],
            send_sem=st_send.at[sem],
            recv_sem=st_recv.at[at],
            device_id=(i, t),
            device_id_type=MESH,
        )

    for k in order:
        row_copy(a, peer(k), b + 2, peer(k)).start()

    @pl.when(first_two & up)
    def _():
        def go(t, c):
            row_copy(a - 1, t, LR + 2 + b, n_lon + t).start()
            return c

        lax.fori_loop(0, n_lon, go, 0)

    @pl.when(last_two & down)
    def _():
        def go(t, c):
            row_copy(a + 1, t, b - (n_lon - 2), n_lon + t).start()
            return c

        lax.fori_loop(0, n_lon, go, 0)

    srecv[b + 2] = sbuf[b]

    def meta_copy(t, slot_at):
        return pltpu.make_async_remote_copy(
            src_ref=meta_v.at[b],
            dst_ref=meta_v.at[slot_at],
            send_sem=me_send.at[t],
            recv_sem=me_recv.at[slot_at],
            device_id=(a, t),
            device_id_type=MESH,
        )

    for k in order:
        meta_copy(peer(k), b).start()

    def obs_copy_to(t, slot_at):
        return pltpu.make_async_remote_copy(
            src_ref=sv.at[t],
            dst_ref=rv.at[slot_at],
            send_sem=ob_send.at[t],
            recv_sem=ob_recv.at[slot_at],
            device_id=(a, t),
            device_id_type=MESH,
        )

    tmp[...] = jnp.zeros_like(tmp)
    for part in obs_parts:
        part.wait()
    idx_copy.wait()

    def gathered(t):
        for k in range(CAP):
            block = pl.ds(idx_s[0, t * CAP + k], nvar, stride=nblk)
            tmp[pl.ds(k * VP, nvar), :] = obs[block, :]
        return tmp[...].astype(BF16)

    def send_obs(g, c):
        for k in range(4):
            t = after(turn(g, k))
            if k < 3:
                sv[t] = gathered(t)
                obs_copy_to(t, b).start()
            else:

                @pl.when(g < groups - 1)
                def _():
                    sv[t] = gathered(t)
                    obs_copy_to(t, b).start()

        return c

    lax.fori_loop(0, groups, send_obs, 0)
    rv[b] = gathered(b)

    for part in weight_parts:
        part.wait()
    up_weights(k1_ref, wu1)
    up_weights(k2_ref, wu2)
    pair_weights(k3_ref, w3, False)
    pair_weights(k3_ref, b3, True)
    down_weights(k2_ref, wd2)
    down_weights(k1_ref, wd1)
    opad[...] = jnp.zeros_like(opad)
    opad[0:nvar] = outp_ref[...].astype(F32)
    opt[...] = opad[...].astype(BF16)
    vlane = lax.broadcasted_iota(I32, (VP, nvar), 1)
    vsub = lax.broadcasted_iota(I32, (VP, nvar), 0)
    scale = jnp.broadcast_to(scale_ref[...], (VP, nvar))
    scale = jnp.sum(jnp.where(vlane == vsub, scale, 0.0), axis=1, keepdims=True)
    w2[...] = jnp.broadcast_to(scale * scale, (VP, W))
    for ref in (f1, sl1, m1, b1):
        ref[...] = jnp.zeros_like(ref)
    for ref in (a3, a2):
        ref[...] = jnp.zeros_like(ref)

    for k in order:
        row_copy(a, b, peer(k) + 2, 0).wait_recv()

    @pl.when(up)
    def _():
        row_copy(a, b, 0, 0).wait_recv()
        row_copy(a, b, 1, 0).wait_recv()

    @pl.when(down)
    def _():
        row_copy(a, b, LR + 2, 0).wait_recv()
        row_copy(a, b, LR + 3, 0).wait_recv()

    def inside(first, count, pitch, size):
        row = lax.broadcasted_iota(I32, (count, pitch, W), 0) + first
        low = jnp.where(up, -8, 0)
        high = jnp.where(down, size + 8, size)
        return jnp.where((row >= low) & (row < high), 1.0, 0.0).reshape(count * pitch, W)

    def lifted(line, weights):
        left = [shifted(x, -1).astype(BF16) for x in line]
        here = [x.astype(BF16) for x in line]
        right = [shifted(x, 1).astype(BF16) for x in line]
        phases = []
        for q, (u, v) in enumerate(((left, here), (here, right))):
            x = jnp.concatenate([u[0], v[0], u[1], v[1], u[2], v[2]], axis=1)
            y = dot(x, weights[q])
            phases += [y[:, :W], y[:, W:]]
        return phases

    n1 = LR + 2
    line = [srecv[pl.ds(i, n1)].astype(F32).reshape(n1 * LP, W) for i in range(3)]
    mask = inside(-1, n1, LP, LR)
    for ph, pre in enumerate(lifted(line, wu1)):
        s = logistic(pre)
        f1s[ph] = mask * rounded(pre * s + line[1])
        d1s[ph] = mask * (s * (1.0 + pre * (1.0 - s)))

    def spread(i, c):
        for q in range(2):
            for p in range(2):
                to = pl.ds((2 * i + p + 1) * MP + q, 10, stride=2)
                frm = pl.ds(i * LP + 3, 10)
                f1[to, :] = f1s[2 * q + p, frm, :]
                sl1[to, :] = d1s[2 * q + p, frm, :]
        return c

    lax.fori_loop(0, n1, spread, 0, unroll=3)

    for k in order:
        meta_copy(b, peer(k)).wait_recv()
    meta_down = pltpu.make_async_copy(meta_v, meta_s, dma_sem.at[1])
    meta_down.start()

    def level_two(i, c):
        first = i * C_TWO + GUARD - 2
        line = [f1[pl.ds(pl.multiple_of((first + d) * MP, 8), C_TWO * MP), :] for d in (-1, 0, 1)]
        mask = inside(first - GUARD, C_TWO, MP, MR)
        at = pl.ds(pl.multiple_of(first * MP, 8), C_TWO * MP)
        for ph, pre in enumerate(lifted(line, wu2)):
            s = logistic(pre)
            f2[ph, at, :] = mask * (pre * s + line[1])
            sl2[ph, at, :] = mask * (s * (1.0 + pre * (1.0 - s)))
        return c

    lax.fori_loop(0, (MR + 4) // C_TWO, level_two, 0)

    def paired(planes, weights, q):
        x = jnp.concatenate([planes[m][q + j] for m in range(4) for j in range(3)], axis=1)
        return dot(x, weights[...])

    def head(i, c):
        first = i * C_HEAD + GUARD
        planes = window(f2, first, C_HEAD, MP)
        at = pl.ds(pl.multiple_of(first * MP, 8), C_HEAD * MP)
        for q in range(2):
            y = paired(planes, w3, q)
            for p in range(2):
                pre = y[:, p * W : (p + 1) * W]
                s = logistic(pre)
                act2[2 * q + p, at, :] = pre * s
                sl3[2 * q + p, at, :] = s * (1.0 + pre * (1.0 - s))
        return c

    lax.fori_loop(0, MR // C_HEAD, head, 0)

    def points(r, c):
        for q in range(2):
            for p in range(2):
                to = pl.ds((2 * r + p) * (4 * LW) + q, 2 * LW, stride=2)
                actp[to, :] = act2[2 * q + p, pl.ds((r + GUARD) * MP + 2, 2 * LW), :]
        return c

    lax.fori_loop(0, MR, points, 0, unroll=4)
    for n in range(npatch):
        ft[n] = dot_nt(opt[...], actp[n * plen : (n + 1) * plen].astype(BF16)).astype(BF16)

    for part in bank_parts:
        part.wait()
    meta_down.wait()
    none = n_lon * CAP
    hist[none] = jnp.zeros((VP, plen), F32)

    def predict(g, c):
        for m in range(4):
            source = before_me(turn(g, m))
            for k in range(CAP):
                rows = bank[meta_s[source, 2, b * CAP + k]]
                slot_at = (g * 4 + m) * CAP + k
                pred[slot_at] = dot(ft[meta_s[source, 1, b * CAP + k]], rows)
        return c

    lax.fori_loop(0, groups, predict, 0)

    def blocks(g, last):
        for m in range(4):
            source = before_me(turn(g, m))
            if m < 3:
                obs_copy_to(b, source).wait_recv()
            else:

                @pl.when(g < groups - 1)
                def _():
                    obs_copy_to(b, source).wait_recv()

            values = rv[source].astype(F32)
            grads = []
            for k in range(CAP):
                rows = bank[meta_s[source, 2, b * CAP + k]]
                live = meta_s[source, 3, b * CAP + k].astype(F32)
                miss = pred[(g * 4 + m) * CAP + k] - values[k * VP : (k + 1) * VP]
                grads.append(dot_nt(((w2[...] * live) * miss).astype(BF16), rows))
            for k in range(CAP):
                patch = meta_s[source, 1, b * CAP + k]
                slot_at = (g * 4 + m) * CAP + k
                before = last[0]
                for n in range(1, npatch):
                    before = jnp.where(patch == n, last[n], before)
                hist[slot_at] = grads[k] + hist[before]
                last = tuple(jnp.where(patch == n, slot_at, last[n]) for n in range(npatch))
        return last

    last = lax.fori_loop(0, groups, blocks, (jnp.int32(none),) * npatch)

    for n in range(npatch):
        grad = hist[last[n]].astype(BF16)
        ga[n * plen : (n + 1) * plen] = lax.dot_general(
            grad, opt[...], (((0,), (0,)), ((), ())), preferred_element_type=F32
        )

    def adjoint_three(r, c):
        at = pl.ds((r + GUARD) * MP + 2, 2 * LW)
        for q in range(2):
            for p in range(2):
                grad = ga[pl.ds((2 * r + p) * (4 * LW) + q, 2 * LW, stride=2), :]
                a3[2 * q + p, at, :] = grad * sl3[2 * q + p, at, :]
        return c

    lax.fori_loop(0, MR, adjoint_three, 0, unroll=4)

    edge_rows = (0, MR - 2)
    edge_cols = (0, 2 * LW - 2)
    for side in range(2):
        for ph in range(4):
            for i in range(2):
                at = (edge_rows[side] + i + GUARD) * MP + 2
                to = (ph * 2 + i) * 2 * LW
                ns_s[side, to : to + 2 * LW] = a3[ph, at : at + 2 * LW, :].astype(BF16)
                at = GUARD * MP + 2 + edge_cols[side] + i
                to = (ph * 2 + i) * MR
                ew_s[side, to : to + MR] = a3[ph, pl.ds(at, MR, stride=MP), :].astype(BF16)
    for v in range(2):
        for h in range(2):
            for ph in range(4):
                for i in range(2):
                    at = (edge_rows[v] + i + GUARD) * MP + 2 + edge_cols[h]
                    ctmp[v * 2 + h, ph * 4 + i * 2 : ph * 4 + i * 2 + 2] = a3[ph, at : at + 2, :]
            co_s[v * 2 + h] = ctmp[v * 2 + h].astype(BF16)

    def halo_copy(k):
        dy, dx = HALO[k]
        v, h = (dy + 1) // 2, (dx + 1) // 2
        if dy == 0:
            src, dst = ew_s.at[h], ew_r.at[1 - h]
        elif dx == 0:
            src, dst = ns_s.at[v], ns_r.at[1 - v]
        else:
            src, dst = co_s.at[v * 2 + h], co_r.at[(1 - v) * 2 + 1 - h]
        return pltpu.make_async_remote_copy(
            src_ref=src,
            dst_ref=dst,
            send_sem=ha_send.at[k],
            recv_sem=ha_recv.at[7 - k],
            device_id=(a + dy, lax.rem(b + n_lon + dx, n_lon)),
            device_id_type=MESH,
        )

    def halo_arrived(k):
        dy, dx = HALO[k]
        v, h = (dy + 1) // 2, (dx + 1) // 2
        if dy == 0:
            ref = ew_r.at[h]
        elif dx == 0:
            ref = ns_r.at[v]
        else:
            ref = co_r.at[v * 2 + h]
        pltpu.make_async_remote_copy(
            src_ref=ref,
            dst_ref=ref,
            send_sem=ha_send.at[k],
            recv_sem=ha_recv.at[k],
            device_id=(a, b),
            device_id_type=MESH,
        ).wait_recv()

    there = {-1: up, 1: down}
    for dy in (-1, 1):

        @pl.when(there[dy])
        def _():
            for k, (ky, _kx) in enumerate(HALO):
                if ky == dy:
                    halo_copy(k).start()

    for k, (ky, _kx) in enumerate(HALO):
        if ky == 0:
            halo_copy(k).start()

    halo_rows = (-2, MR)
    halo_cols = (0, 2 * LW + 2)
    for dy in (-1, 1):

        @pl.when(there[dy])
        def _():
            v = (dy + 1) // 2
            for k, (ky, _kx) in enumerate(HALO):
                if ky == dy:
                    halo_arrived(k)
            for ph in range(4):
                for i in range(2):
                    at = (halo_rows[v] + i + GUARD) * MP + 2
                    frm = (ph * 2 + i) * 2 * LW
                    a3[ph, at : at + 2 * LW, :] = ns_r[v, frm : frm + 2 * LW].astype(F32)
            for h in range(2):
                ctmp[v * 2 + h] = co_r[v * 2 + h].astype(F32)
                for ph in range(4):
                    for i in range(2):
                        at = (halo_rows[v] + i + GUARD) * MP + halo_cols[h]
                        a3[ph, at : at + 2, :] = ctmp[
                            v * 2 + h, ph * 4 + i * 2 : ph * 4 + i * 2 + 2
                        ]

    for k, (ky, kx) in enumerate(HALO):
        if ky == 0:
            h = (kx + 1) // 2
            halo_arrived(k)
            for ph in range(4):
                for i in range(2):
                    frm = (ph * 2 + i) * MR
                    at = GUARD * MP + halo_cols[h] + i
                    a3[ph, pl.ds(at, MR, stride=MP), :] = ew_r[h, frm : frm + MR].astype(F32)

    def back_three(i, c):
        first = i * C_B3 + GUARD - 2
        planes = window(a3, first, C_B3, MP)
        at = pl.ds(pl.multiple_of(first * MP, 8), C_B3 * MP)
        total = jnp.zeros((C_B3 * MP, W), F32)
        for q in range(2):
            y = paired(planes, b3, q)
            for p in range(2):
                back = y[:, p * W : (p + 1) * W]
                a2[2 * q + p, at, :] = back * sl2[2 * q + p, at, :]
                total = total + back
        ds2[at, :] = total
        return c

    lax.fori_loop(0, (MR + 4) // C_B3, back_three, 0)

    def gathered_down(planes, weights):
        x = jnp.concatenate([planes[m][n] for m in range(4) for n in range(4)], axis=1)
        return dot(x, weights[...])

    def gathered_down(src, first, count, pitch, weights):
        at = slice(first * pitch, (first + count) * pitch)
        total = 0.0
        for p in range(2):
            x = jnp.concatenate(
                [shifted(src[2 * q + p, at, :], dc).astype(BF16) for q, dc in TAPS], axis=1
            )
            y = dot(x, weights[p])
            other = jnp.zeros((pitch, W), F32)
            if p == 1:
                other = jnp.concatenate([other, y[:-pitch, W:]], axis=0)
            else:
                other = jnp.concatenate([y[pitch:, W:], other], axis=0)
            total = total + (y[:, :W] + other)
        return total

    at = slice((GUARD - 2) * MP, (GUARD + MR + 2) * MP)
    back = ds2[at, :] + gathered_down(a2, GUARD - 2, MR + 4, MP, wd2)
    b1[at, :] = back
    m1[at, :] = back * sl1[at, :]

    def gather(i, c):
        total = jnp.zeros((LP, W), F32)
        for q in range(2):
            for p in range(2):
                frm = pl.ds((2 * i + p + 1) * MP + q, LP, stride=2)
                a1[2 * q + p, pl.ds(pl.multiple_of(i * LP, 8), LP), :] = m1[frm, :]
                total = total + b1[frm, :]
        zbuf[pl.ds(pl.multiple_of(i * LP, 8), LP), :] = total
        return c

    lax.fori_loop(0, n1, gather, 0, unroll=3)
    back = gathered_down(a1, 0, n1, LP, wd1)[LP : LP + LR * LP] + zbuf[LP : LP + LR * LP]
    zbuf[LP : LP + LR * LP] = rounded(back)
    for r in range(LR):
        zs[r] = zbuf[(r + 1) * LP + 1 : (r + 1) * LP + 1 + LW]

    def z_copy(t, slot_at):
        return pltpu.make_async_remote_copy(
            src_ref=zs.at[t],
            dst_ref=zr.at[slot_at],
            send_sem=z_send.at[t],
            recv_sem=z_recv.at[slot_at],
            device_id=(a, t),
            device_id_type=MESH,
        )

    for k in order:
        z_copy(peer(k), b).start()
    zr[b] = zs[b]

    for k in order:
        row_copy(a, peer(k), b + 2, peer(k)).wait_send()
        meta_copy(peer(k), b).wait_send()
        obs_copy_to(peer(k), b).wait_send()

    @pl.when((first_two & up) | (last_two & down))
    def _():
        def go(t, c):
            row_copy(a, t, b + 2, n_lon + t).wait_send()
            return c

        lax.fori_loop(0, n_lon, go, 0)

    for dy in (-1, 1):

        @pl.when(there[dy])
        def _():
            for k, (ky, _kx) in enumerate(HALO):
                if ky == dy:
                    halo_copy(k).wait_send()

    for k, (ky, _kx) in enumerate(HALO):
        if ky == 0:
            halo_copy(k).wait_send()

    for k in order:
        z_copy(peer(k), b).wait_send()
        z_copy(b, peer(k)).wait_recv()
    out_ref[...] = zr[...].reshape(n_col, W).astype(BF16)


def per_device(
    n_lat,
    n_lon,
    latents,
    in_proj,
    kernel_one,
    kernel_two,
    kernel_three,
    out_proj,
    bank,
    obs_values,
    obs_scale,
    owner_col,
    patch_id,
    bank_id,
):
    LR = n_lon
    MR = 2 * LR
    npts = 4 * LR * 4 * LW
    plen = bank.shape[1]
    nmid = (MR + 2 * GUARD) * MP
    n1 = LR + 2
    slots = n_lon * CAP
    vmem = pltpu.VMEM
    dma = pltpu.SemaphoreType.DMA
    nvar, nblk = obs_values.shape[1], obs_values.shape[0]
    scratch = [
        vmem(latents.shape, BF16),
        vmem(in_proj.shape, BF16),
        vmem(kernel_one.shape, BF16),
        vmem(kernel_two.shape, BF16),
        vmem(kernel_three.shape, BF16),
        vmem((nvar, W), BF16),
        vmem((1, nvar), F32),
        vmem((1, nblk), I32),
        vmem((1, nblk), I32),
        vmem((1, nblk), I32),
        vmem(bank.shape, BF16),
        vmem((obs_values.shape[0] * obs_values.shape[1], W), F32),
        vmem((n_lon * LW + 16, W), F32),
        vmem((n_lon, LP, W), BF16),
        vmem((LR + 4, LP, W), BF16),
        vmem((n_lon, 8, W), I32),
        pltpu.SMEM((8, W), I32),
        pltpu.SMEM((n_lon, 8, W), I32),
        vmem((CAP * VP, W), F32),
        vmem((n_lon, CAP * VP, W), BF16),
        vmem((n_lon, CAP * VP, W), BF16),
        vmem((2, 6 * W, 2 * W), BF16),
        vmem((2, 6 * W, 2 * W), BF16),
        vmem((12 * W, 2 * W), BF16),
        vmem((12 * W, 2 * W), BF16),
        vmem((2, 4 * W, 2 * W), BF16),
        vmem((2, 4 * W, 2 * W), BF16),
        vmem((VP, W), BF16),
        vmem((VP, W), F32),
        vmem((VP, W), F32),
        vmem((4, n1 * LP, W), F32),
        vmem((4, n1 * LP, W), F32),
        vmem((nmid, W), F32),
        vmem((nmid, W), F32),
        vmem((4, nmid, W), F32),
        vmem((4, nmid, W), F32),
        vmem((4, nmid, W), F32),
        vmem((4, nmid, W), F32),
        vmem((npts, W), F32),
        vmem((npts // plen, VP, plen), BF16),
        vmem((slots, VP, W), F32),
        vmem((slots + 1, VP, plen), F32),
        vmem((npts, W), F32),
        vmem((4, nmid, W), F32),
        vmem((4, nmid, W), F32),
        vmem((nmid, W), F32),
        vmem((nmid, W), F32),
        vmem((nmid, W), F32),
        vmem((4, n1 * LP, W), F32),
        vmem((n1 * LP, W), F32),
        vmem((n_lon, LW, W), F32),
        vmem((n_lon, LW, W), F32),
        vmem((4, 16, W), F32),
        vmem((2, 4 * 2 * 2 * LW, W), BF16),
        vmem((2, 4 * 2 * 2 * LW, W), BF16),
        vmem((2, 4 * 2 * MR, W), BF16),
        vmem((2, 4 * 2 * MR, W), BF16),
        vmem((4, 16, W), BF16),
        vmem((4, 16, W), BF16),
        dma((12 + 2 * PARTS,)),
        dma((2 * n_lon,)),
        dma((LR + 4,)),
        dma((n_lon,)),
        dma((n_lon,)),
        dma((n_lon,)),
        dma((n_lon,)),
        dma((8,)),
        dma((8,)),
        dma((n_lon,)),
        dma((n_lon,)),
    ]
    here = pl.BlockSpec(memory_space=pltpu.VMEM)
    far = pl.BlockSpec(memory_space=pl.ANY)
    back_zero = pl.pallas_call(
        functools.partial(kernel, n_lat, n_lon),
        out_shape=pltpu.VMEM((latents.shape[0], W), BF16),
        in_specs=[far] * 12,
        out_specs=here,
        scratch_shapes=scratch,
        compiler_params=pltpu.CompilerParams(
            collective_id=0, has_side_effects=True, vmem_limit_bytes=56 * 1024 * 1024
        ),
        cost_estimate=pl.CostEstimate(
            flops=5_000_000_000, bytes_accessed=4_000_000, transcendentals=1_000_000
        ),
    )(
        latents,
        in_proj,
        kernel_one,
        kernel_two,
        kernel_three,
        out_proj.T,
        bank,
        jnp.transpose(obs_values, (1, 0, 2)).reshape(nvar * nblk, W),
        obs_scale.reshape(1, -1),
        owner_col.reshape(1, -1),
        patch_id.reshape(1, -1),
        bank_id.reshape(1, -1),
    )
    return dot_nt(back_zero, in_proj)


def solution(mesh):
    n_lat, n_lon = mesh.shape["lat"], mesh.shape["lon"]
    placed = (
        P(("lat", "lon"), None),
        P(),
        P(),
        P(),
        P(),
        P(),
        P(),
        P(("lat", "lon"), None, None),
        P(),
        P(("lat", "lon"), None),
        P(("lat", "lon")),
        P(("lat", "lon")),
    )
    return jax.shard_map(
        functools.partial(per_device, n_lat, n_lon),
        mesh=mesh,
        in_specs=placed,
        out_specs=P(("lat", "lon"), None),
        check_vma=False,
    )
```

```python
import functools

import jax
import jax.numpy as jnp
from jax import lax
from jax.experimental import pallas as pl
from jax.experimental.pallas import tpu as pltpu
from jax.sharding import PartitionSpec as P

F32 = jnp.float32
BF16 = jnp.bfloat16
I32 = jnp.int32
MESH = pl.DeviceIdType.MESH
CAP = 4
LW = 8
W = 128
VP = 72
MP = 24
LP = 16
S_TWO, S_HEAD, S_B3 = 2, 1, 1
PARTS = 4
GUARD = 3
HALO = [(-1, -1), (-1, 0), (-1, 1), (0, -1), (0, 1), (1, -1), (1, 0), (1, 1)]


def dot(x, y):
    return jnp.dot(x, y, preferred_element_type=F32)


def dot_nt(x, y):
    return lax.dot_general(x, y, (((1,), (1,)), ((), ())), preferred_element_type=F32)


def shifted(x, by):
    return x if by == 0 else pltpu.roll(x, (-by) % x.shape[0], 0)


def logistic(x):
    return 0.5 * jnp.tanh(0.5 * x) + 0.5


def rounded(x):
    return x.astype(BF16).astype(F32)


TAPS = [(1, -1), (0, 0), (1, 0), (0, 1)]


def window(src, first, count, pitch):
    planes = []
    for p, dr in TAPS:
        line = []
        for q, dc in TAPS:
            at = pl.multiple_of((first + dr) * pitch, 8)
            line.append(shifted(src[2 * q + p, pl.ds(at, count * pitch), :], dc).astype(BF16))
        planes.append(line)
    return planes


def up_weights(k_ref, out_ref):
    rows = {(0, 0): [0], (0, 1): [1, 2], (0, 2): [], (1, 0): [], (1, 1): [0, 1], (1, 2): [2]}
    cols = {(0, 0): [0], (0, 1): [1, 2], (1, 0): [0, 1], (1, 1): [2]}
    for q in range(2):
        for rr in range(3):
            for cc in range(2):
                for p in range(2):
                    block = jnp.zeros((W, W), F32)
                    for i in rows[p, rr]:
                        for j in cols[q, cc]:
                            block = block + k_ref[i, j].astype(F32)
                    at = (rr * 2 + cc) * W
                    out_ref[q, at : at + W, p * W : (p + 1) * W] = block.astype(BF16)


def pair_weights(k_ref, out_ref, flip):
    for m in range(4):
        for j in range(3):
            at = (m * 3 + j) * W
            for p in range(2):
                i = m - p
                if 0 <= i <= 2:
                    block = k_ref[2 - i, 2 - j].astype(F32).T if flip else k_ref[i, j].astype(F32)
                else:
                    block = jnp.zeros((W, W), F32)
                out_ref[at : at + W, p * W : (p + 1) * W] = block.astype(BF16)


def down_weights(k_ref, out_ref):
    for m in range(4):
        for n in range(4):
            block = jnp.zeros((W, W), F32)
            for i in (m - 1, m):
                for j in (n - 1, n):
                    if 0 <= i <= 2 and 0 <= j <= 2:
                        block = block + k_ref[2 - i, 2 - j].astype(F32)
            p, near = 1 - m % 2, m in (1, 2)
            to = 0 if near else W
            out_ref[p, n * W : (n + 1) * W, to : to + W] = block.T.astype(BF16)


def kernel(
    n_lat,
    n_lon,
    lat_hbm,
    inp_hbm,
    k1_hbm,
    k2_hbm,
    k3_hbm,
    outp_hbm,
    bank_hbm,
    obs_hbm,
    scale_hbm,
    owner_hbm,
    patch_hbm,
    bankid_hbm,
    out_ref,
    lat_ref,
    inp_ref,
    k1_ref,
    k2_ref,
    k3_ref,
    outp_ref,
    scale_ref,
    owner_ref,
    patch_ref,
    bankid_ref,
    bank,
    obs,
    row_x,
    sbuf,
    srecv,
    meta_v,
    idx_s,
    meta_s,
    tmp,
    sv,
    rv,
    wu1,
    wu2,
    w3,
    b3,
    wd1,
    wd2,
    opt,
    opad,
    w2,
    f1s,
    d1s,
    f1,
    sl1,
    f2,
    sl2,
    act2,
    sl3,
    actp,
    ft,
    pred,
    hist,
    ga,
    a3,
    a2,
    ds2,
    b1,
    m1,
    a1,
    zbuf,
    zs,
    zr,
    ctmp,
    ns_s,
    ns_r,
    ew_s,
    ew_r,
    co_s,
    co_r,
    dma_sem,
    st_send,
    st_recv,
    me_send,
    me_recv,
    ob_send,
    ob_recv,
    ha_send,
    ha_recv,
    z_send,
    z_recv,
):
    a, b = lax.axis_index("lat"), lax.axis_index("lon")
    LR = n_lon
    MR = 2 * LR
    npatch = (4 * LR * 4 * LW) // bank.shape[1]
    plen = bank.shape[1]
    C_TWO, C_B3 = (MR + 4) // S_TWO, (MR + 4) // S_B3
    C_HEAD = MR // S_HEAD
    nblk = patch_ref.shape[1]
    nvar = outp_ref.shape[0]
    up, down = a > 0, a < n_lat - 1
    upi, downi = jnp.where(up, 1, 0), jnp.where(down, 1, 0)
    first_two, last_two = b < 2, b >= n_lon - 2

    flips = [bit * (1 - 2 * lax.rem(b // bit, 2)) for bit in (1, 2, 4, 8) if bit < n_lon]
    groups = n_lon // 4
    order = range(n_lon - 1, 0, -1)

    def peer(k):
        return b + sum(flip for i, flip in enumerate(flips) if k >> i & 1)

    def turn(g, k):
        return 2 * g + 1 + k // 2 + (k % 2) * (n_lon // 2)

    def after(t):
        return b + t - jnp.where(b + t >= n_lon, n_lon, 0)

    def before_me(t):
        return b - t + jnp.where(b < t, n_lon, 0)

    for row in (0, 1, LR + 2, LR + 3):
        srecv[row] = jnp.zeros((LP, W), BF16)

    barrier = pltpu.get_barrier_semaphore()

    def greet(i, j):
        pl.semaphore_signal(barrier, inc=1, device_id=(i, j), device_id_type=MESH)

    for k in order:
        greet(a, peer(k))

    @pl.when(up)
    def _():
        greet(a - 1, n_lon - 2)
        greet(a - 1, n_lon - 1)
        for d in range(3):
            greet(a - 1, lax.rem(b + n_lon - 1 + d, n_lon))

    @pl.when(down)
    def _():
        greet(a + 1, 0)
        greet(a + 1, 1)
        for d in range(3):
            greet(a + 1, lax.rem(b + n_lon - 1 + d, n_lon))

    def local(src, dst, sem):
        copy = pltpu.make_async_copy(src, dst, dma_sem.at[sem])
        copy.start()
        return copy

    row_parts = [local(lat_hbm, lat_ref, 2), local(inp_hbm, inp_ref, 3)]
    id_parts = [
        local(owner_hbm, owner_ref, 4),
        local(patch_hbm, patch_ref, 5),
        local(bankid_hbm, bankid_ref, 6),
    ]
    obs_rows = obs.shape[0] // PARTS
    bank_rows = bank.shape[0] // PARTS
    cuts = [pl.ds(i * obs_rows, obs_rows) for i in range(PARTS)]
    obs_parts = [local(obs_hbm.at[c], obs.at[c], 12 + i) for i, c in enumerate(cuts)]
    weight_parts = [
        local(k1_hbm, k1_ref, 7),
        local(k2_hbm, k2_ref, 8),
        local(k3_hbm, k3_ref, 9),
        local(outp_hbm, outp_ref, 10),
        local(scale_hbm, scale_ref, 11),
    ]
    cuts = [pl.ds(i * bank_rows, bank_rows) for i in range(PARTS)]
    bank_parts = [local(bank_hbm.at[c], bank.at[c], 12 + PARTS + i) for i, c in enumerate(cuts)]

    for part in row_parts:
        part.wait()
    feat = rounded(dot(lat_ref[...], inp_ref[...]))
    n_col = n_lon * LW
    row_x[0:8] = feat[n_col - 8 :]
    row_x[8 : 8 + n_col] = feat
    row_x[8 + n_col : 16 + n_col] = feat[0:8]
    for t in range(n_lon):
        sbuf[t] = row_x[8 * t + 4 : 8 * t + 20].astype(BF16)

    for part in id_parts:
        part.wait()
    lane = lax.broadcasted_iota(I32, (nblk, W), 1)
    sub = lax.broadcasted_iota(I32, (nblk, W), 0)
    eye = lane == sub

    def column(row_ref):
        row = jnp.broadcast_to(row_ref[...], (nblk, nblk))
        return jnp.sum(jnp.where(eye[:, :nblk], row, 0), axis=1, keepdims=True)

    own_c = jnp.broadcast_to(column(owner_ref), (nblk, W))
    own_r = jnp.sum(jnp.where(eye, own_c, 0), axis=0, keepdims=True)
    earlier = jnp.where((own_c == own_r) & (lane < sub), 1, 0)
    rank = jnp.sum(earlier, axis=1, keepdims=True)
    slot = own_c * CAP + rank
    pick = lane == slot

    def per_slot(value):
        return jnp.sum(jnp.where(pick, value, 0), axis=0, keepdims=True)

    rows8 = lax.broadcasted_iota(I32, (8, W), 0)
    meta = jnp.where(rows8 == 0, per_slot(sub), 0)
    meta = jnp.where(rows8 == 1, per_slot(jnp.broadcast_to(column(patch_ref), (nblk, W))), meta)
    meta = jnp.where(rows8 == 2, per_slot(jnp.broadcast_to(column(bankid_ref), (nblk, W))), meta)
    meta = jnp.where(rows8 == 3, per_slot(jnp.ones_like(sub)), meta)
    meta_v[b] = meta
    idx_copy = pltpu.make_async_copy(meta_v.at[b], idx_s, dma_sem.at[0])
    idx_copy.start()

    tmp[...] = jnp.zeros_like(tmp)
    for part in obs_parts:
        part.wait()
    idx_copy.wait()

    def gathered(t):
        for k in range(CAP):
            block = pl.ds(idx_s[0, t * CAP + k], nvar, stride=nblk)
            tmp[pl.ds(k * VP, nvar), :] = obs[block, :]
        return tmp[...].astype(BF16)

    for k in range(4):
        if turn(0, k) < n_lon:
            sv[after(turn(0, k))] = gathered(after(turn(0, k)))

    expected = (
        n_lon - 1
        + jnp.where(first_two & up, n_lon, 0)
        + jnp.where(last_two & down, n_lon, 0)
        + 3 * upi
        + 3 * downi
    )
    pl.semaphore_wait(barrier, expected)

    def row_copy(i, t, at, sem):
        return pltpu.make_async_remote_copy(
            src_ref=sbuf.at[t],
            dst_ref=srecv.at[at],
            send_sem=st_send.at[sem],
            recv_sem=st_recv.at[at],
            device_id=(i, t),
            device_id_type=MESH,
        )

    for k in order:
        row_copy(a, peer(k), b + 2, peer(k)).start()

    @pl.when(first_two & up)
    def _():
        def go(t, c):
            row_copy(a - 1, t, LR + 2 + b, n_lon + t).start()
            return c

        lax.fori_loop(0, n_lon, go, 0)

    @pl.when(last_two & down)
    def _():
        def go(t, c):
            row_copy(a + 1, t, b - (n_lon - 2), n_lon + t).start()
            return c

        lax.fori_loop(0, n_lon, go, 0)

    srecv[b + 2] = sbuf[b]

    def meta_copy(t, slot_at):
        return pltpu.make_async_remote_copy(
            src_ref=meta_v.at[b],
            dst_ref=meta_v.at[slot_at],
            send_sem=me_send.at[t],
            recv_sem=me_recv.at[slot_at],
            device_id=(a, t),
            device_id_type=MESH,
        )

    for k in order:
        meta_copy(peer(k), b).start()

    def obs_copy_to(t, slot_at):
        return pltpu.make_async_remote_copy(
            src_ref=sv.at[t],
            dst_ref=rv.at[slot_at],
            send_sem=ob_send.at[t],
            recv_sem=ob_recv.at[slot_at],
            device_id=(a, t),
            device_id_type=MESH,
        )

    first = [turn(0, k) for k in range(4) if turn(0, k) < n_lon]
    for t in first:
        obs_copy_to(after(t), b).start()

    def send_obs(g, c):
        for k in range(4):
            t = after(turn(g, k))
            if k < 3:
                sv[t] = gathered(t)
                obs_copy_to(t, b).start()
            else:

                @pl.when(g < groups - 1)
                def _():
                    sv[t] = gathered(t)
                    obs_copy_to(t, b).start()

        return c

    lax.fori_loop(1, groups, send_obs, 0)
    rv[b] = gathered(b)

    for part in weight_parts:
        part.wait()
    up_weights(k1_ref, wu1)
    up_weights(k2_ref, wu2)
    pair_weights(k3_ref, w3, False)
    pair_weights(k3_ref, b3, True)
    down_weights(k2_ref, wd2)
    down_weights(k1_ref, wd1)
    opad[...] = jnp.zeros_like(opad)
    opad[0:nvar] = outp_ref[...].astype(F32)
    opt[...] = opad[...].astype(BF16)
    vlane = lax.broadcasted_iota(I32, (VP, nvar), 1)
    vsub = lax.broadcasted_iota(I32, (VP, nvar), 0)
    scale = jnp.broadcast_to(scale_ref[...], (VP, nvar))
    scale = jnp.sum(jnp.where(vlane == vsub, scale, 0.0), axis=1, keepdims=True)
    w2[...] = jnp.broadcast_to(scale * scale, (VP, W))
    for ref in (f1, sl1, m1, b1):
        ref[...] = jnp.zeros_like(ref)
    for ref in (a3, a2):
        ref[...] = jnp.zeros_like(ref)

    for k in order:
        row_copy(a, b, peer(k) + 2, 0).wait_recv()

    @pl.when(up)
    def _():
        row_copy(a, b, 0, 0).wait_recv()
        row_copy(a, b, 1, 0).wait_recv()

    @pl.when(down)
    def _():
        row_copy(a, b, LR + 2, 0).wait_recv()
        row_copy(a, b, LR + 3, 0).wait_recv()

    def inside(first, count, pitch, size):
        row = lax.broadcasted_iota(I32, (count, pitch, W), 0) + first
        low = jnp.where(up, -8, 0)
        high = jnp.where(down, size + 8, size)
        return jnp.where((row >= low) & (row < high), 1.0, 0.0).reshape(count * pitch, W)

    def lifted(line, weights):
        left = [shifted(x, -1).astype(BF16) for x in line]
        here = [x.astype(BF16) for x in line]
        right = [shifted(x, 1).astype(BF16) for x in line]
        phases = []
        for q, (u, v) in enumerate(((left, here), (here, right))):
            x = jnp.concatenate([u[0], v[0], u[1], v[1], u[2], v[2]], axis=1)
            y = dot(x, weights[q])
            phases += [y[:, :W], y[:, W:]]
        return phases

    n1 = LR + 2
    line = [srecv[pl.ds(i, n1)].astype(F32).reshape(n1 * LP, W) for i in range(3)]
    mask = inside(-1, n1, LP, LR)
    for ph, pre in enumerate(lifted(line, wu1)):
        s = logistic(pre)
        f1s[ph] = mask * rounded(pre * s + line[1])
        d1s[ph] = mask * (s * (1.0 + pre * (1.0 - s)))

    def spread(i, c):
        for q in range(2):
            for p in range(2):
                to = pl.ds((2 * i + p + 1) * MP + q, 10, stride=2)
                frm = pl.ds(i * LP + 3, 10)
                f1[to, :] = f1s[2 * q + p, frm, :]
                sl1[to, :] = d1s[2 * q + p, frm, :]
        return c

    lax.fori_loop(0, n1, spread, 0, unroll=3)

    for k in order:
        meta_copy(b, peer(k)).wait_recv()
    meta_down = pltpu.make_async_copy(meta_v, meta_s, dma_sem.at[1])
    meta_down.start()

    def level_two(i, c):
        first = i * C_TWO + GUARD - 2
        line = [f1[pl.ds(pl.multiple_of((first + d) * MP, 8), C_TWO * MP), :] for d in (-1, 0, 1)]
        mask = inside(first - GUARD, C_TWO, MP, MR)
        at = pl.ds(pl.multiple_of(first * MP, 8), C_TWO * MP)
        for ph, pre in enumerate(lifted(line, wu2)):
            s = logistic(pre)
            f2[ph, at, :] = mask * (pre * s + line[1])
            sl2[ph, at, :] = mask * (s * (1.0 + pre * (1.0 - s)))
        return c

    lax.fori_loop(0, (MR + 4) // C_TWO, level_two, 0)

    def paired(planes, weights, q):
        x = jnp.concatenate([planes[m][q + j] for m in range(4) for j in range(3)], axis=1)
        return dot(x, weights[...])

    def head(i, c):
        first = i * C_HEAD + GUARD
        planes = window(f2, first, C_HEAD, MP)
        at = pl.ds(pl.multiple_of(first * MP, 8), C_HEAD * MP)
        for q in range(2):
            y = paired(planes, w3, q)
            for p in range(2):
                pre = y[:, p * W : (p + 1) * W]
                s = logistic(pre)
                act2[2 * q + p, at, :] = pre * s
                sl3[2 * q + p, at, :] = s * (1.0 + pre * (1.0 - s))
        return c

    lax.fori_loop(0, MR // C_HEAD, head, 0)

    def points(r, c):
        for q in range(2):
            for p in range(2):
                to = pl.ds((2 * r + p) * (4 * LW) + q, 2 * LW, stride=2)
                actp[to, :] = act2[2 * q + p, pl.ds((r + GUARD) * MP + 2, 2 * LW), :]
        return c

    lax.fori_loop(0, MR, points, 0, unroll=4)
    for n in range(npatch):
        ft[n] = dot_nt(opt[...], actp[n * plen : (n + 1) * plen].astype(BF16)).astype(BF16)

    for part in bank_parts:
        part.wait()
    meta_down.wait()
    none = n_lon * CAP
    hist[none] = jnp.zeros((VP, plen), F32)

    def predict(g, c):
        for m in range(4):
            source = before_me(turn(g, m))
            for k in range(CAP):
                rows = bank[meta_s[source, 2, b * CAP + k]]
                slot_at = (g * 4 + m) * CAP + k
                pred[slot_at] = dot(ft[meta_s[source, 1, b * CAP + k]], rows)
        return c

    lax.fori_loop(0, groups, predict, 0)

    def blocks(g, last):
        for m in range(4):
            source = before_me(turn(g, m))
            if m < 3:
                obs_copy_to(b, source).wait_recv()
            else:

                @pl.when(g < groups - 1)
                def _():
                    obs_copy_to(b, source).wait_recv()

            values = rv[source].astype(F32)
            grads = []
            for k in range(CAP):
                rows = bank[meta_s[source, 2, b * CAP + k]]
                live = meta_s[source, 3, b * CAP + k].astype(F32)
                miss = pred[(g * 4 + m) * CAP + k] - values[k * VP : (k + 1) * VP]
                grads.append(dot_nt(((w2[...] * live) * miss).astype(BF16), rows))
            for k in range(CAP):
                patch = meta_s[source, 1, b * CAP + k]
                slot_at = (g * 4 + m) * CAP + k
                before = last[0]
                for n in range(1, npatch):
                    before = jnp.where(patch == n, last[n], before)
                hist[slot_at] = grads[k] + hist[before]
                last = tuple(jnp.where(patch == n, slot_at, last[n]) for n in range(npatch))
        return last

    last = lax.fori_loop(0, groups, blocks, (jnp.int32(none),) * npatch)

    for n in range(npatch):
        grad = hist[last[n]].astype(BF16)
        ga[n * plen : (n + 1) * plen] = lax.dot_general(
            grad, opt[...], (((0,), (0,)), ((), ())), preferred_element_type=F32
        )

    def adjoint_three(r, c):
        at = pl.ds((r + GUARD) * MP + 2, 2 * LW)
        for q in range(2):
            for p in range(2):
                grad = ga[pl.ds((2 * r + p) * (4 * LW) + q, 2 * LW, stride=2), :]
                a3[2 * q + p, at, :] = grad * sl3[2 * q + p, at, :]
        return c

    lax.fori_loop(0, MR, adjoint_three, 0, unroll=4)

    edge_rows = (0, MR - 2)
    edge_cols = (0, 2 * LW - 2)
    for side in range(2):
        for ph in range(4):
            for i in range(2):
                at = (edge_rows[side] + i + GUARD) * MP + 2
                to = (ph * 2 + i) * 2 * LW
                ns_s[side, to : to + 2 * LW] = a3[ph, at : at + 2 * LW, :].astype(BF16)
                at = GUARD * MP + 2 + edge_cols[side] + i
                to = (ph * 2 + i) * MR
                ew_s[side, to : to + MR] = a3[ph, pl.ds(at, MR, stride=MP), :].astype(BF16)
    for v in range(2):
        for h in range(2):
            for ph in range(4):
                for i in range(2):
                    at = (edge_rows[v] + i + GUARD) * MP + 2 + edge_cols[h]
                    ctmp[v * 2 + h, ph * 4 + i * 2 : ph * 4 + i * 2 + 2] = a3[ph, at : at + 2, :]
            co_s[v * 2 + h] = ctmp[v * 2 + h].astype(BF16)

    def halo_copy(k):
        dy, dx = HALO[k]
        v, h = (dy + 1) // 2, (dx + 1) // 2
        if dy == 0:
            src, dst = ew_s.at[h], ew_r.at[1 - h]
        elif dx == 0:
            src, dst = ns_s.at[v], ns_r.at[1 - v]
        else:
            src, dst = co_s.at[v * 2 + h], co_r.at[(1 - v) * 2 + 1 - h]
        return pltpu.make_async_remote_copy(
            src_ref=src,
            dst_ref=dst,
            send_sem=ha_send.at[k],
            recv_sem=ha_recv.at[7 - k],
            device_id=(a + dy, lax.rem(b + n_lon + dx, n_lon)),
            device_id_type=MESH,
        )

    def halo_arrived(k):
        dy, dx = HALO[k]
        v, h = (dy + 1) // 2, (dx + 1) // 2
        if dy == 0:
            ref = ew_r.at[h]
        elif dx == 0:
            ref = ns_r.at[v]
        else:
            ref = co_r.at[v * 2 + h]
        pltpu.make_async_remote_copy(
            src_ref=ref,
            dst_ref=ref,
            send_sem=ha_send.at[k],
            recv_sem=ha_recv.at[k],
            device_id=(a, b),
            device_id_type=MESH,
        ).wait_recv()

    there = {-1: up, 1: down}
    for dy in (-1, 1):

        @pl.when(there[dy])
        def _():
            for k, (ky, _kx) in enumerate(HALO):
                if ky == dy:
                    halo_copy(k).start()

    for k, (ky, _kx) in enumerate(HALO):
        if ky == 0:
            halo_copy(k).start()

    halo_rows = (-2, MR)
    halo_cols = (0, 2 * LW + 2)
    for dy in (-1, 1):

        @pl.when(there[dy])
        def _():
            v = (dy + 1) // 2
            for k, (ky, _kx) in enumerate(HALO):
                if ky == dy:
                    halo_arrived(k)
            for ph in range(4):
                for i in range(2):
                    at = (halo_rows[v] + i + GUARD) * MP + 2
                    frm = (ph * 2 + i) * 2 * LW
                    a3[ph, at : at + 2 * LW, :] = ns_r[v, frm : frm + 2 * LW].astype(F32)
            for h in range(2):
                ctmp[v * 2 + h] = co_r[v * 2 + h].astype(F32)
                for ph in range(4):
                    for i in range(2):
                        at = (halo_rows[v] + i + GUARD) * MP + halo_cols[h]
                        a3[ph, at : at + 2, :] = ctmp[
                            v * 2 + h, ph * 4 + i * 2 : ph * 4 + i * 2 + 2
                        ]

    for k, (ky, kx) in enumerate(HALO):
        if ky == 0:
            h = (kx + 1) // 2
            halo_arrived(k)
            for ph in range(4):
                for i in range(2):
                    frm = (ph * 2 + i) * MR
                    at = GUARD * MP + halo_cols[h] + i
                    a3[ph, pl.ds(at, MR, stride=MP), :] = ew_r[h, frm : frm + MR].astype(F32)

    def back_three(i, c):
        first = i * C_B3 + GUARD - 2
        planes = window(a3, first, C_B3, MP)
        at = pl.ds(pl.multiple_of(first * MP, 8), C_B3 * MP)
        total = jnp.zeros((C_B3 * MP, W), F32)
        for q in range(2):
            y = paired(planes, b3, q)
            for p in range(2):
                back = y[:, p * W : (p + 1) * W]
                a2[2 * q + p, at, :] = back * sl2[2 * q + p, at, :]
                total = total + back
        ds2[at, :] = total
        return c

    lax.fori_loop(0, (MR + 4) // C_B3, back_three, 0)

    def gathered_down(planes, weights):
        x = jnp.concatenate([planes[m][n] for m in range(4) for n in range(4)], axis=1)
        return dot(x, weights[...])

    def gathered_down(src, first, count, pitch, weights):
        at = slice(first * pitch, (first + count) * pitch)
        total = 0.0
        for p in range(2):
            x = jnp.concatenate(
                [shifted(src[2 * q + p, at, :], dc).astype(BF16) for q, dc in TAPS], axis=1
            )
            y = dot(x, weights[p])
            other = jnp.zeros((pitch, W), F32)
            if p == 1:
                other = jnp.concatenate([other, y[:-pitch, W:]], axis=0)
            else:
                other = jnp.concatenate([y[pitch:, W:], other], axis=0)
            total = total + (y[:, :W] + other)
        return total

    at = slice((GUARD - 2) * MP, (GUARD + MR + 2) * MP)
    back = ds2[at, :] + gathered_down(a2, GUARD - 2, MR + 4, MP, wd2)
    b1[at, :] = back
    m1[at, :] = back * sl1[at, :]

    def gather(i, c):
        total = jnp.zeros((LP, W), F32)
        for q in range(2):
            for p in range(2):
                frm = pl.ds((2 * i + p + 1) * MP + q, LP, stride=2)
                a1[2 * q + p, pl.ds(pl.multiple_of(i * LP, 8), LP), :] = m1[frm, :]
                total = total + b1[frm, :]
        zbuf[pl.ds(pl.multiple_of(i * LP, 8), LP), :] = total
        return c

    lax.fori_loop(0, n1, gather, 0, unroll=3)
    back = gathered_down(a1, 0, n1, LP, wd1)[LP : LP + LR * LP] + zbuf[LP : LP + LR * LP]
    zbuf[LP : LP + LR * LP] = rounded(back)
    for r in range(LR):
        zs[r] = zbuf[(r + 1) * LP + 1 : (r + 1) * LP + 1 + LW]

    def z_copy(t, slot_at):
        return pltpu.make_async_remote_copy(
            src_ref=zs.at[t],
            dst_ref=zr.at[slot_at],
            send_sem=z_send.at[t],
            recv_sem=z_recv.at[slot_at],
            device_id=(a, t),
            device_id_type=MESH,
        )

    for k in order:
        z_copy(peer(k), b).start()
    zr[b] = zs[b]

    for k in order:
        row_copy(a, peer(k), b + 2, peer(k)).wait_send()
        meta_copy(peer(k), b).wait_send()
        obs_copy_to(peer(k), b).wait_send()

    @pl.when((first_two & up) | (last_two & down))
    def _():
        def go(t, c):
            row_copy(a, t, b + 2, n_lon + t).wait_send()
            return c

        lax.fori_loop(0, n_lon, go, 0)

    for dy in (-1, 1):

        @pl.when(there[dy])
        def _():
            for k, (ky, _kx) in enumerate(HALO):
                if ky == dy:
                    halo_copy(k).wait_send()

    for k, (ky, _kx) in enumerate(HALO):
        if ky == 0:
            halo_copy(k).wait_send()

    for k in order:
        z_copy(peer(k), b).wait_send()
        z_copy(b, peer(k)).wait_recv()
    out_ref[...] = zr[...].reshape(n_col, W).astype(BF16)


def per_device(
    n_lat,
    n_lon,
    latents,
    in_proj,
    kernel_one,
    kernel_two,
    kernel_three,
    out_proj,
    bank,
    obs_values,
    obs_scale,
    owner_col,
    patch_id,
    bank_id,
):
    LR = n_lon
    MR = 2 * LR
    npts = 4 * LR * 4 * LW
    plen = bank.shape[1]
    nmid = (MR + 2 * GUARD) * MP
    n1 = LR + 2
    slots = n_lon * CAP
    vmem = pltpu.VMEM
    dma = pltpu.SemaphoreType.DMA
    nvar, nblk = obs_values.shape[1], obs_values.shape[0]
    scratch = [
        vmem(latents.shape, BF16),
        vmem(in_proj.shape, BF16),
        vmem(kernel_one.shape, BF16),
        vmem(kernel_two.shape, BF16),
        vmem(kernel_three.shape, BF16),
        vmem((nvar, W), BF16),
        vmem((1, nvar), F32),
        vmem((1, nblk), I32),
        vmem((1, nblk), I32),
        vmem((1, nblk), I32),
        vmem(bank.shape, BF16),
        vmem((obs_values.shape[0] * obs_values.shape[1], W), F32),
        vmem((n_lon * LW + 16, W), F32),
        vmem((n_lon, LP, W), BF16),
        vmem((LR + 4, LP, W), BF16),
        vmem((n_lon, 8, W), I32),
        pltpu.SMEM((8, W), I32),
        pltpu.SMEM((n_lon, 8, W), I32),
        vmem((CAP * VP, W), F32),
        vmem((n_lon, CAP * VP, W), BF16),
        vmem((n_lon, CAP * VP, W), BF16),
        vmem((2, 6 * W, 2 * W), BF16),
        vmem((2, 6 * W, 2 * W), BF16),
        vmem((12 * W, 2 * W), BF16),
        vmem((12 * W, 2 * W), BF16),
        vmem((2, 4 * W, 2 * W), BF16),
        vmem((2, 4 * W, 2 * W), BF16),
        vmem((VP, W), BF16),
        vmem((VP, W), F32),
        vmem((VP, W), F32),
        vmem((4, n1 * LP, W), F32),
        vmem((4, n1 * LP, W), F32),
        vmem((nmid, W), F32),
        vmem((nmid, W), F32),
        vmem((4, nmid, W), F32),
        vmem((4, nmid, W), F32),
        vmem((4, nmid, W), F32),
        vmem((4, nmid, W), F32),
        vmem((npts, W), F32),
        vmem((npts // plen, VP, plen), BF16),
        vmem((slots, VP, W), F32),
        vmem((slots + 1, VP, plen), F32),
        vmem((npts, W), F32),
        vmem((4, nmid, W), F32),
        vmem((4, nmid, W), F32),
        vmem((nmid, W), F32),
        vmem((nmid, W), F32),
        vmem((nmid, W), F32),
        vmem((4, n1 * LP, W), F32),
        vmem((n1 * LP, W), F32),
        vmem((n_lon, LW, W), F32),
        vmem((n_lon, LW, W), F32),
        vmem((4, 16, W), F32),
        vmem((2, 4 * 2 * 2 * LW, W), BF16),
        vmem((2, 4 * 2 * 2 * LW, W), BF16),
        vmem((2, 4 * 2 * MR, W), BF16),
        vmem((2, 4 * 2 * MR, W), BF16),
        vmem((4, 16, W), BF16),
        vmem((4, 16, W), BF16),
        dma((12 + 2 * PARTS,)),
        dma((2 * n_lon,)),
        dma((LR + 4,)),
        dma((n_lon,)),
        dma((n_lon,)),
        dma((n_lon,)),
        dma((n_lon,)),
        dma((8,)),
        dma((8,)),
        dma((n_lon,)),
        dma((n_lon,)),
    ]
    here = pl.BlockSpec(memory_space=pltpu.VMEM)
    far = pl.BlockSpec(memory_space=pl.ANY)
    back_zero = pl.pallas_call(
        functools.partial(kernel, n_lat, n_lon),
        out_shape=pltpu.VMEM((latents.shape[0], W), BF16),
        in_specs=[far] * 12,
        out_specs=here,
        scratch_shapes=scratch,
        compiler_params=pltpu.CompilerParams(
            collective_id=0, has_side_effects=True, vmem_limit_bytes=56 * 1024 * 1024
        ),
        cost_estimate=pl.CostEstimate(
            flops=5_000_000_000, bytes_accessed=4_000_000, transcendentals=1_000_000
        ),
    )(
        latents,
        in_proj,
        kernel_one,
        kernel_two,
        kernel_three,
        out_proj.T,
        bank,
        jnp.transpose(obs_values, (1, 0, 2)).reshape(nvar * nblk, W),
        obs_scale.reshape(1, -1),
        owner_col.reshape(1, -1),
        patch_id.reshape(1, -1),
        bank_id.reshape(1, -1),
    )
    return dot_nt(back_zero, in_proj)


def solution(mesh):
    n_lat, n_lon = mesh.shape["lat"], mesh.shape["lon"]
    placed = (
        P(("lat", "lon"), None),
        P(),
        P(),
        P(),
        P(),
        P(),
        P(),
        P(("lat", "lon"), None, None),
        P(),
        P(("lat", "lon"), None),
        P(("lat", "lon")),
        P(("lat", "lon")),
    )
    return jax.shard_map(
        functools.partial(per_device, n_lat, n_lon),
        mesh=mesh,
        in_specs=placed,
        out_specs=P(("lat", "lon"), None),
        check_vma=False,
    )
```
